32 devices in a mesh: dp: 4 (over y, x), seq: 8 (over z, core).
Axes of the slice: x: 2, y: 2, z: 4, core: 2. Of those that a mesh axis runs over, the one named last changes fastest.
Arguments:
- tokens: bfloat16 [16, 1024, 1536], P('dp', 'seq'), may hold values from -6 to 6
- conv_state: bfloat16 [16, 3, 3072], P('dp'), may hold values from -6 to 6
- entry_state: float32 [16, 16, 3072], P('dp'), may hold values from -4 to 4
- norm_gain: float32 [1536], replicated, may hold values from 0.5 to 1.5
- in_proj: bfloat16 [1536, 6144], replicated, may hold values from -0.15625 to 0.15625
- conv_weight: float32 [4, 3072], replicated, may hold values from -3 to 3
- conv_bias: float32 [3072], replicated, may hold values from -2 to 2
- x_proj: bfloat16 [3072, 128], replicated, may hold values from -0.109375 to 0.109375
- dt_proj: bfloat16 [96, 3072], replicated, may hold values from -0.625 to 0.625
- dt_bias: float32 [3072], replicated, may hold values from -7 to -2.3
- a_log: float32 [16, 3072], replicated, may hold values from -5.8 to 1.1
- d_skip: float32 [3072], replicated, may hold values from 0.5 to 1.5
- out_proj: bfloat16 [3072, 1536], replicated, may hold values from -0.109375 to 0.109375
- cotangent: bfloat16 [16, 1024, 1536], P('dp', 'seq'), may hold values from -6 to 6
Outputs:
- output: float32 [16, 1024, 1536], P('dp', 'seq')
- d_tokens: float32 [16, 1024, 1536], P('dp', 'seq')
- d_conv_state: float32 [16, 3, 3072], P('dp')
- d_entry_state: float32 [16, 16, 3072], P('dp')
- d_norm_gain: float32 [1536], P('seq')
- d_in_proj: float32 [1536, 6144], P(None, 'seq')
- d_conv_weight: float32 [4, 3072], P(None, 'seq')
- d_conv_bias: float32 [3072], P('seq')
- d_x_proj: float32 [3072, 128], P('seq')
- d_dt_proj: float32 [96, 3072], P(None, 'seq')
- d_dt_bias: float32 [3072], P('seq')
- d_a_log: float32 [16, 3072], P(None, 'seq')
- d_d_skip: float32 [3072], P('seq')
- d_out_proj: float32 [3072, 1536], P('seq')
The draws below stay inside these ranges and needn't reach their ends.
All inputs are finite; a program needn't handle non-finite values.
Results may differ from the reference program's by a relative error of at most 0.0095.
Values may be sent and summed in bfloat16 or wider, within the bound.
A program may use at most 320 MiB of HBM per device.

```python
import jax
import jax.numpy as jnp
from jax import lax

D = 1536
E = 3072
N = 16
R = 96
K = 4
SEGS = 4
LENGTH = 1024
SEGMENTS = 16
N_DP = 4


def block_scale(key, dims, cuts, low, largest):
    gain, own = 1.0, jax.random.fold_in(key, 6)
    for position, blocks in cuts:
        heights = jnp.exp(jax.random.uniform(jax.random.fold_in(own, position), (blocks,), jnp.float32, low / len(cuts), largest / len(cuts)))
        gain = gain * jnp.repeat(heights, dims[position] // blocks).reshape([-1 if axis == position else 1 for axis in range(len(dims))])
    return gain


def scatter_about(stream_key, dims, spread, most, cuts=(), held_as=jnp.bfloat16):
    level = block_scale(stream_key, dims, cuts, -0.22, 0.18) if cuts else 1.0
    values = jax.random.normal(stream_key, dims, jnp.float32) * spread * level
    return jnp.minimum(jnp.maximum(values, -most), most).astype(held_as)


def setup_inputs(seed: int = 0) -> dict:
    key_list = jax.random.split(jax.random.key(seed), 15)
    return {
        "tokens": scatter_about(key_list[0], (SEGMENTS, LENGTH, D), 1.0, 6.0, ((0, 4), (1, 8))),
        "conv_state": scatter_about(key_list[1], (SEGMENTS, K - 1, E), 1.0, 6.0, ((0, 4),)),
        "entry_state": scatter_about(key_list[2], (SEGMENTS, N, E), 0.5, 4.0, ((0, 4),), jnp.float32),
        "norm_gain": jnp.clip(1.0 + 0.1 * jax.random.normal(key_list[3], (D,), jnp.float32), 0.5, 1.5),
        "in_proj": scatter_about(key_list[4], (D, 2 * E), D ** -0.5, 0.15625),
        "conv_weight": scatter_about(key_list[5], (K, E), K ** -0.5, 3.0, (), jnp.float32),
        "conv_bias": scatter_about(key_list[6], (E,), 0.3, 2.0, (), jnp.float32),
        "x_proj": scatter_about(key_list[7], (E, R + 2 * N), E ** -0.5, 0.109375),
        "dt_proj": scatter_about(key_list[8], (R, E), R ** -0.5, 0.625),
        "dt_bias": jnp.clip(jax.random.uniform(key_list[9], (E,), jnp.float32, -7.0, -2.3), -7.0, -2.3),
        "a_log": jnp.clip(jax.random.uniform(key_list[10], (N, E), jnp.float32, -5.8, 1.1), -5.8, 1.1),
        "d_skip": jnp.clip(jax.random.uniform(key_list[11], (E,), jnp.float32, 0.5, 1.5), 0.5, 1.5),
        "out_proj": scatter_about(key_list[12], (E, D), E ** -0.5, 0.109375),
        "cotangent": scatter_about(key_list[13], (SEGMENTS, LENGTH, D), 1.0, 6.0, ((0, 4), (1, 8))),
    }


@jax.custom_vjp
def low(v):
    return lax.optimization_barrier(v.astype(jnp.bfloat16)).astype(jnp.float32)

@jax.custom_vjp
def low_back(v):
    return v

def low_keep(v):
    return (low(v), None)

def low_pass(kept, grad):
    return (grad,)

def back_keep(v):
    return (v, None)

def back_low(kept, grad):
    return (low(grad),)
low.defvjp(low_keep, low_pass)
low_back.defvjp(back_keep, back_low)
EPS = 1e-05
HIGH = lax.Precision.HIGHEST

def silu(value):
    return value * jax.nn.sigmoid(value)

def matmul(left, right):
    return jnp.einsum('sti,ij->stj', left, right, precision=HIGH)

def scan_block(carry, block):
    current, a_mat = carry

    def advance(state_now, item):
        delta, drive, b_in, c_in = item
        state_now = jnp.exp(delta[:, None, :] * a_mat) * state_now + drive[:, None, :] * b_in[:, :, None]
        return (state_now, lax.optimization_barrier(jnp.sum(state_now * c_in[:, :, None], axis=1)))
    current, produced = lax.scan(advance, current, block)
    return ((current, a_mat), produced)

def to_blocks(value):
    moved = jnp.moveaxis(value, 1, 0)
    return moved.reshape((LENGTH // 16, 16) + moved.shape[1:])

def forward(tokens, conv_state, entry_state, norm_gain, in_proj, conv_weight, conv_bias, x_proj, dt_proj, dt_bias, a_log, d_skip, out_proj):
    inverse = lax.rsqrt(lax.optimization_barrier(jnp.mean(tokens * tokens, axis=-1, keepdims=True)) + EPS)
    normed = low(tokens * inverse * norm_gain)
    projected = low_back(matmul(normed, in_proj))
    conv_in = low(projected[..., :E])
    gate_in = projected[..., E:]
    padded = jnp.concatenate([conv_state, conv_in], axis=1)
    conv_out = conv_bias + jnp.zeros_like(conv_in)
    for tap in range(K):
        conv_out = conv_out + conv_weight[tap] * padded[:, tap:tap + LENGTH]
    activated = low(silu(conv_out))
    coeffs = low_back(matmul(activated, x_proj))
    dt_low = low(coeffs[..., :R])
    b_in = coeffs[..., R:R + N]
    c_in = coeffs[..., R + N:]
    delta = jax.nn.softplus(low_back(matmul(dt_low, dt_proj)) + dt_bias)
    a_mat = -jnp.exp(a_log)
    drive = delta * activated
    blocked = (to_blocks(delta), to_blocks(drive), to_blocks(b_in), to_blocks(c_in))
    _, produced = lax.scan(jax.checkpoint(scan_block), (entry_state, a_mat), blocked)
    produced = jnp.moveaxis(produced.reshape((LENGTH, SEGS, E)), 0, 1)
    scanned = produced + d_skip * activated
    gated = low(scanned * silu(gate_in))
    return tokens + matmul(gated, out_proj)

def reference(tokens, conv_state, entry_state, norm_gain, in_proj, conv_weight, conv_bias, x_proj, dt_proj, dt_bias, a_log, d_skip, out_proj, cotangent):
    weights = (norm_gain.astype(jnp.float32), in_proj.astype(jnp.float32), conv_weight.astype(jnp.float32), conv_bias.astype(jnp.float32), x_proj.astype(jnp.float32), dt_proj.astype(jnp.float32), dt_bias.astype(jnp.float32), a_log.astype(jnp.float32), d_skip.astype(jnp.float32), out_proj.astype(jnp.float32))

    def grouped(value):
        return value.reshape((N_DP, SEGS) + value.shape[1:])

    def per_group(running, item):
        group_tokens, group_conv, group_entry, group_cot = item
        group_out, pull = jax.vjp(forward, group_tokens.astype(jnp.float32), group_conv.astype(jnp.float32), group_entry.astype(jnp.float32), *weights)
        gradients = pull(group_cot.astype(jnp.float32))
        updated = tuple((before + gradient for before, gradient in zip(running, gradients[3:])))
        return (updated, (group_out, gradients[0], gradients[1], gradients[2]))
    start = tuple((jnp.zeros_like(weight) for weight in weights))
    totals, stacked = lax.scan(per_group, start, (grouped(tokens), grouped(conv_state), grouped(entry_state), grouped(cotangent)))

    def flat(value):
        return value.reshape((SEGMENTS,) + value.shape[2:])
    return (flat(stacked[0]), flat(stacked[1]), flat(stacked[2]), flat(stacked[3]), totals[0], totals[1], totals[2], totals[3], totals[4], totals[5], totals[6], totals[7], totals[8], totals[9])
```

```python
import functools
import math

import jax
import jax.numpy as jnp
from jax import lax
from jax.experimental import pallas as pl
from jax.experimental.pallas import tpu as pltpu
from jax.sharding import PartitionSpec as P

EPS = 1e-05
LANES = 128
CHUNK = 16
LOG2E = math.log2(math.e)
LN2 = math.log(2.0)
BF16 = jnp.bfloat16
F32 = jnp.float32
VMEM_BYTES = 56 * 2**20


def silu_parts(value):
    sigmoid = jax.nn.sigmoid(value)
    return value * sigmoid, sigmoid * (1.0 + value * (1.0 - sigmoid))


def matmul(left, right):
    return lax.dot_general(left, right, (((1,), (0,)), ((), ())), preferred_element_type=F32)


def matmul_nt(left, right):
    return lax.dot_general(left, right, (((1,), (1,)), ((), ())), preferred_element_type=F32)


def matmul_tn(left, right):
    return lax.dot_general(left, right, (((0,), (0,)), ((), ())), preferred_element_type=F32)


def partner_route(axis, step):
    count = lax.axis_size(axis)
    if count & (count - 1) == 0:
        return [(i, i ^ step) for i in range(count)]
    return [(i, (i + step) % count) for i in range(count)]


def partners(axis, step):
    count, mine = lax.axis_size(axis), lax.axis_index(axis)
    if count & (count - 1) == 0:
        return mine ^ step, mine ^ step
    return (mine + step) % count, (mine + count - step) % count


def swap_columns(block, axis):
    count = lax.axis_size(axis)
    rows, width = block.shape[0], block.shape[1] // count
    gathered = jnp.zeros((count * rows, width), block.dtype)
    for step in range(count):
        target, source = partners(axis, step)
        piece = lax.dynamic_slice_in_dim(block, target * width, width, 1)
        if step:
            piece = lax.ppermute(piece, axis, partner_route(axis, step))
        gathered = lax.dynamic_update_slice_in_dim(gathered, piece, source * rows, 0)
    return gathered


def sum_scatter_rows(block, axis):
    count = lax.axis_size(axis)
    rows = block.shape[0] // count
    low = block.astype(BF16)
    total = None
    for step in range(count):
        target, _ = partners(axis, step)
        if step == 0:
            total = lax.dynamic_slice_in_dim(block, target * rows, rows, 0)
        else:
            piece = lax.dynamic_slice_in_dim(low, target * rows, rows, 0)
            total = total + lax.ppermute(piece, axis, partner_route(axis, step)).astype(F32)
    return total


def gather_rows(block, axis):
    count = lax.axis_size(axis)
    rows = block.shape[0]
    gathered = jnp.zeros((count * rows,) + block.shape[1:], block.dtype)
    for step in range(count):
        _, source = partners(axis, step)
        piece = lax.ppermute(block, axis, partner_route(axis, step)) if step else block
        gathered = lax.dynamic_update_slice_in_dim(gathered, piece, source * rows, 0)
    return gathered


def shifted(block, axis, distance):
    devices = range(lax.axis_size(axis))
    route = [(i - distance, i) for i in devices if i - distance in devices]
    return lax.ppermute(block, axis, route)


def from_first(block, axis):
    count, mine = lax.axis_size(axis), lax.axis_index(axis)
    reach = 1
    while reach < count:
        route = [(i, i + reach) for i in range(min(reach, count - reach))]
        arrived = lax.ppermute(block, axis, route)
        block = jnp.where(mine < reach, block, arrived)
        reach *= 2
    return block


def carried(state, total, first, a_mat, axis, sign):
    count, mine = lax.axis_size(axis), lax.axis_index(axis)
    edge = mine == (0 if sign > 0 else count - 1)
    held, span = shifted(state, axis, sign), shifted(total, axis, sign)
    held = jnp.where(edge, first, held)
    reach = 1
    while reach < count:
        far = shifted(held, axis, sign * reach)
        far_span = shifted(span, axis, sign * reach)
        held = held + jnp.exp(span * a_mat) * far
        span = span + far_span
        reach *= 2
    return held


def spread_row(ref, rows, at, tile, states):
    row = ref.at[0, rows][at : at + 1, tile * LANES : (tile + 1) * LANES]
    return jnp.broadcast_to(row, (states, LANES))


def column(tile):
    return slice(tile * LANES, (tile + 1) * LANES)


def ends_kernel(d_ref, act_ref, y_ref, b_ref, c_ref, a_ref, end_ref, mu_ref, drive):
    states = a_ref.shape[0]
    length, width = d_ref.shape[1:]
    tiles = width // LANES
    rate = [a_ref[:, column(j)] * LOG2E for j in range(tiles)]
    drive[0] = d_ref[0] * act_ref[0].astype(F32)

    def chunk(i, carry):
        h, p, mu = (list(part) for part in carry)
        rows = pl.ds(pl.multiple_of(i * CHUNK, CHUNK), CHUNK)
        for r in range(CHUNK):
            b, c = b_ref[0, i * CHUNK + r], c_ref[0, i * CHUNK + r]
            for j in range(tiles):
                decay = jnp.exp2(spread_row(d_ref, rows, r, j, states) * rate[j])
                h[j] = h[j] * decay + spread_row(drive, rows, r, j, states) * b
                p[j] = p[j] * decay
                mu[j] = mu[j] + p[j] * (spread_row(y_ref, rows, r, j, states) * c)
        return tuple(h), tuple(p), tuple(mu)

    zeros = tuple(jnp.zeros((states, LANES), F32) for _ in range(tiles))
    ones = tuple(jnp.ones((states, LANES), F32) for _ in range(tiles))
    h, _, mu = lax.fori_loop(0, length // CHUNK, chunk, (zeros, ones, zeros))
    for j in range(tiles):
        end_ref[0, :, column(j)] = h[j]
        mu_ref[0, :, column(j)] = mu[j]


def widest(inner, most):
    width = most
    while inner % width:
        width -= LANES
    return width


def block_ends(delta, act, d_scanned, b_wide, c_wide, a_mat):
    segs, length, inner = delta.shape
    states = a_mat.shape[0]
    width = widest(inner, 512)
    tokens = pl.BlockSpec((1, length, width), lambda s, e: (s, 0, e))
    wide = pl.BlockSpec((1, length, states, LANES), lambda s, e: (s, 0, 0, 0))
    state = pl.BlockSpec((1, states, width), lambda s, e: (s, 0, e))
    shape = jax.ShapeDtypeStruct((segs, states, inner), F32)
    return pl.pallas_call(
        ends_kernel,
        grid=(segs, inner // width),
        in_specs=[tokens, tokens, tokens, wide, wide, pl.BlockSpec((states, width), lambda s, e: (0, e))],
        out_specs=[state, state],
        out_shape=[shape, shape],
        scratch_shapes=[pltpu.VMEM((1, length, width), F32)],
        compiler_params=pltpu.CompilerParams(vmem_limit_bytes=VMEM_BYTES),
        cost_estimate=pl.CostEstimate(
            flops=9 * delta.size * states, bytes_accessed=12 * delta.size, transcendentals=delta.size * states
        ),
        name="block_ends",
    )(delta, act, d_scanned, b_wide, c_wide, a_mat)


def scan_kernel(
    d_ref, act_ref, dy_ref, b_ref, c_ref, c_diag, b_diag, ones_ref, a_ref, start_ref, end_ref,
    y_ref, dv_ref, dd_ref, db_ref, dc_ref, da_ref,
    history, drive, low_a, low_b, through_a, through_b,
):
    states = a_ref.shape[0]
    length, width = d_ref.shape[1:]
    tiles, chunks = width // LANES, length // CHUNK
    span = min(width, 256)
    parts = width // span
    rate = [a_ref[:, column(j)] * LOG2E for j in range(tiles)]
    history[0:states, :] = start_ref[0]
    drive[0] = d_ref[0] * act_ref[0].astype(F32)

    def rows_of(i):
        return pl.ds(pl.multiple_of(i * CHUNK, CHUNK), CHUNK)

    def kept(i, r):
        return pl.ds(pl.multiple_of((i * CHUNK + r) * states, states), states)

    def sum_y(i, low, part):
        at = slice(part * span, (part + 1) * span)
        y_ref[0, rows_of(i), at] = jnp.dot(c_diag[0, i], low[:, at], preferred_element_type=F32)

    def forward(i, h, low, before, low_before):
        rows = rows_of(i)
        waiting = list(range(parts))
        for r in range(CHUNK):
            b = b_ref[0, i * CHUNK + r]
            for j in range(tiles):
                decay = jnp.exp2(spread_row(d_ref, rows, r, j, states) * rate[j])
                h[j] = h[j] * decay + spread_row(drive, rows, r, j, states) * b
                history[kept(i, r + 1), column(j)] = h[j]
                low[r * states : (r + 1) * states, column(j)] = h[j].astype(BF16)
            if waiting and r % (CHUNK // parts) == 1:
                sum_y(before, low_before, waiting.pop(0))
        return h

    def forward_pair(pair, carry):
        h = forward(2 * pair, list(carry), low_a, jnp.maximum(2 * pair - 1, 0), low_b)
        return tuple(forward(2 * pair + 1, h, low_b, 2 * pair, low_a))

    lax.fori_loop(0, chunks // 2, forward_pair, tuple(start_ref[0, :, column(j)] for j in range(tiles)))
    for part in range(parts):
        sum_y(chunks - 1, low_b, part)

    @pl.when(pl.program_id(1) == 0)
    def _():
        db_ref[...] = jnp.zeros_like(db_ref)
        dc_ref[...] = jnp.zeros_like(dc_ref)

    def sum_back(i, low, through, part, which):
        at = slice(part * span, (part + 1) * span)
        if which == 0:
            dv_ref[0, rows_of(i), at] = jnp.dot(b_diag[0, i], low[:, at], preferred_element_type=F32)
        else:
            dd_ref[0, rows_of(i), at] = jnp.dot(ones_ref[...], through[:, at], preferred_element_type=F32)

    def backward(i, lam, da, low, through, before, low_before, through_before):
        rows = rows_of(i)
        waiting = [(part, which) for part in range(parts) for which in (0, 1)]
        for r in reversed(range(CHUNK)):
            c = c_ref[0, i * CHUNK + r]
            db = dc = None
            for j in range(tiles):
                step = spread_row(d_ref, rows, r, j, states)
                up = spread_row(dy_ref, rows, r, j, states)
                adjoint = lam[j] + up * c
                db_j = adjoint * spread_row(drive, rows, r, j, states)
                dc_j = up * history[kept(i, r + 1), column(j)]
                db, dc = (db_j, dc_j) if db is None else (db + db_j, dc + dc_j)
                low[r * states : (r + 1) * states, column(j)] = adjoint.astype(BF16)
                lam[j] = adjoint * jnp.exp2(step * rate[j])
                flow = lam[j] * history[kept(i, r), column(j)]
                through[r * states : (r + 1) * states, column(j)] = (flow * rate[j]).astype(BF16)
                da[j] = da[j] + flow * step
            db_ref[0, i * CHUNK + r] += db
            dc_ref[0, i * CHUNK + r] += dc
            if waiting and (CHUNK - 1 - r) % max(1, CHUNK // (2 * parts)) == 1:
                sum_back(before, low_before, through_before, *waiting.pop(0))
        for item in waiting:
            sum_back(before, low_before, through_before, *item)
        return lam, da

    def backward_pair(pair, carry):
        lam, da = (list(part) for part in carry)
        i = chunks - 1 - 2 * pair
        lam, da = backward(i, lam, da, low_a, through_a, jnp.minimum(i + 1, chunks - 1), low_b, through_b)
        lam, da = backward(i - 1, lam, da, low_b, through_b, i, low_a, through_a)
        return tuple(lam), tuple(da)

    zeros = tuple(jnp.zeros((states, LANES), F32) for _ in range(tiles))
    _, da = lax.fori_loop(
        0, chunks // 2, backward_pair, (tuple(end_ref[0, :, column(j)] for j in range(tiles)), zeros)
    )
    for part in range(parts):
        sum_back(0, low_b, through_b, part, 0)
        sum_back(0, low_b, through_b, part, 1)
    for j in range(tiles):
        da_ref[0, :, column(j)] = da[j]


def scan_both(delta, act, d_scanned, b_wide, c_wide, c_diag, b_diag, ones_diag, a_mat, start, end):
    segs, length, inner = delta.shape
    states = a_mat.shape[0]
    width = widest(inner, 1024)
    tokens = pl.BlockSpec((1, length, width), lambda s, e: (s, 0, e))
    wide = pl.BlockSpec((1, length, states, LANES), lambda s, e: (s, 0, 0, 0))
    diag = pl.BlockSpec((1,) + c_diag.shape[1:], lambda s, e: (s, 0, 0, 0))
    state = pl.BlockSpec((1, states, width), lambda s, e: (s, 0, e))
    by_token = jax.ShapeDtypeStruct((segs, length, inner), F32)
    by_lane = jax.ShapeDtypeStruct((segs, length, states, LANES), F32)
    low = pltpu.VMEM((CHUNK * states, width), BF16)
    return pl.pallas_call(
        scan_kernel,
        grid=(segs, inner // width),
        in_specs=[
            tokens, tokens, tokens, wide, wide, diag, diag,
            pl.BlockSpec(ones_diag.shape, lambda s, e: (0, 0)),
            pl.BlockSpec((states, width), lambda s, e: (0, e)),
            state, state,
        ],
        out_specs=[tokens, tokens, tokens, wide, wide, state],
        out_shape=[by_token, by_token, by_token, by_lane, by_lane, jax.ShapeDtypeStruct((segs, states, inner), F32)],
        scratch_shapes=[
            pltpu.VMEM(((length + 1) * states, width), F32),
            pltpu.VMEM((1, length, width), F32),
            low, low, low, low,
        ],
        compiler_params=pltpu.CompilerParams(vmem_limit_bytes=VMEM_BYTES),
        cost_estimate=pl.CostEstimate(
            flops=20 * delta.size * states, bytes_accessed=30 * delta.size, transcendentals=2 * delta.size * states
        ),
        name="scan_both",
    )(delta, act, d_scanned, b_wide, c_wide, c_diag, b_diag, ones_diag, a_mat, start, end)


def diagonal_blocks(value):
    segs, length, states = value.shape
    spread = value.reshape(segs, length // CHUNK, CHUNK, 1, states)
    spread = spread * jnp.eye(CHUNK, dtype=value.dtype)[:, :, None]
    return spread.reshape(segs, length // CHUNK, CHUNK, CHUNK * states).astype(BF16)


def body(
    tokens, conv_state, entry_state, norm_gain, in_proj, conv_weight, conv_bias, x_proj,
    dt_proj, dt_bias, a_log, d_skip, out_proj, cotangent,
):
    segs, length, width = tokens.shape
    inner = in_proj.shape[1] // 2
    rank, states, taps = dt_proj.shape[0], a_log.shape[0], conv_weight.shape[0]
    halo = taps - 1
    count = segs * length
    n_seq = lax.axis_size("seq")
    mine = lax.axis_index("seq")
    is_first = mine == 0

    def flat(value):
        return value.reshape((count,) + value.shape[2:])

    def split(value):
        return value.reshape((segs, length) + value.shape[1:])

    token_float = flat(tokens).astype(F32)
    inverse = lax.rsqrt(jnp.mean(token_float * token_float, axis=-1, keepdims=True) + EPS)
    normed = (token_float * inverse * norm_gain).astype(BF16)
    cot = flat(cotangent)
    normed_all = lax.all_gather(normed, "seq", axis=0, tiled=True)
    cot_all = lax.all_gather(cot, "seq", axis=0, tiled=True)
    conv_in = matmul(normed, in_proj[:, :inner]).astype(BF16)
    gate_in = matmul(normed, in_proj[:, inner:])
    d_gated = matmul_nt(cot, out_proj)
    conv_in = split(conv_in)
    before = jnp.where(is_first, conv_state, shifted(conv_in[:, length - halo :], "seq", 1))
    padded = jnp.concatenate([before, conv_in], axis=1).astype(F32)
    conv_out = conv_bias + sum(conv_weight[tap] * padded[:, tap : tap + length] for tap in range(taps))
    activated = (conv_out * jax.nn.sigmoid(conv_out)).astype(BF16)
    coeffs = matmul(flat(activated), x_proj)
    dt_low = coeffs[:, :rank].astype(BF16)
    b_in = split(coeffs[:, rank : rank + states])
    c_in = split(coeffs[:, rank + states :])
    pre_delta = matmul(dt_low, dt_proj) + dt_bias
    delta = split(jax.nn.softplus(pre_delta))
    a_mat = -jnp.exp(a_log)
    gate_act, gate_slope = silu_parts(gate_in)
    d_scanned = d_gated * gate_act

    b_wide = jnp.broadcast_to(b_in[..., None], b_in.shape + (LANES,))
    c_wide = jnp.broadcast_to(c_in[..., None], c_in.shape + (LANES,))
    ends, entry_mu = block_ends(delta, activated, split(d_scanned), b_wide, c_wide, a_mat)
    total = jnp.sum(delta, axis=1, keepdims=True)
    start = carried(ends, total, entry_state, a_mat, "seq", 1)
    end = carried(entry_mu, total, 0.0, a_mat, "seq", -1)
    d_entry = from_first(entry_mu + jnp.exp(total * a_mat) * end, "seq")
    ones_diag = diagonal_blocks(jnp.ones((1, CHUNK, states), F32))[0, 0]
    produced, d_drive, d_delta_scan, d_b, d_c, d_amat = scan_both(
        delta, activated, split(d_scanned), b_wide, c_wide,
        diagonal_blocks(c_in), diagonal_blocks(b_in), ones_diag, a_mat, start, end,
    )
    d_b = jnp.sum(flat(d_b), axis=-1)
    d_c = jnp.sum(flat(d_c), axis=-1)
    delta, act_float = flat(delta), flat(activated).astype(F32)
    produced, d_drive, d_delta_scan = flat(produced), flat(d_drive), flat(d_delta_scan)

    scanned = produced + d_skip * act_float
    gated = (scanned * gate_act).astype(BF16)
    d_gate = (d_gated * scanned * gate_slope).astype(BF16)
    out_columns = swap_columns(gated, "seq")
    gate_columns = swap_columns(d_gate, "seq")
    output = token_float + matmul(gated, out_proj)
    d_d_skip = jnp.sum(d_scanned * act_float, axis=0)

    d_act = d_skip * d_scanned + d_drive * delta
    d_delta = LN2 * d_delta_scan + d_drive * act_float
    d_pre = d_delta * jax.nn.sigmoid(pre_delta)
    d_dt_bias = jnp.sum(d_pre, axis=0)
    d_pre_low = d_pre.astype(BF16)
    d_dt_proj = matmul_tn(dt_low, d_pre_low)
    d_dt_low = matmul_nt(d_pre_low, dt_proj)
    d_coeffs = jnp.concatenate([d_dt_low, d_b, d_c], axis=-1).astype(BF16)
    d_x_proj = matmul_tn(d_coeffs, flat(activated))
    d_a_log = jnp.sum(d_amat, axis=0) * a_mat
    d_act = split(d_act + matmul_nt(d_coeffs, x_proj))
    conv_sigmoid = jax.nn.sigmoid(conv_out)
    d_conv_out = d_act * (conv_sigmoid * (1.0 + conv_out * (1.0 - conv_sigmoid)))
    d_conv_bias = jnp.sum(d_conv_out, axis=(0, 1))
    d_conv_weight = jnp.stack(
        [jnp.sum(d_conv_out * padded[:, tap : tap + length], axis=(0, 1)) for tap in range(taps)]
    )
    head = jnp.pad(d_conv_out[:, :halo], ((0, 0), (0, halo), (0, 0)))
    halo_grad = sum(
        conv_weight[tap] * jnp.pad(d_conv_out[:, : halo - tap], ((0, 0), (tap, 0), (0, 0))) for tap in range(halo)
    )
    del head
    returned = shifted(halo_grad, "seq", -1)
    tail = jnp.pad(d_conv_out, ((0, 0), (0, halo), (0, 0)))
    d_conv_in = sum(conv_weight[tap] * tail[:, halo - tap : halo - tap + length] for tap in range(taps))
    d_conv_in = d_conv_in + jnp.pad(returned, ((0, 0), (length - halo, 0), (0, 0)))
    d_conv_in = flat(d_conv_in).astype(BF16)
    d_conv_state = from_first(halo_grad, "seq")

    small = jnp.concatenate([d_x_proj, d_dt_proj, d_a_log, d_dt_bias[None], d_d_skip[None]], axis=0)
    edges = jnp.concatenate([d_conv_weight, d_conv_bias[None]], axis=0)

    def pad_rows(value):
        return jnp.pad(value, ((0, -value.shape[0] % (16 * lax.axis_size("dp"))), (0, 0))).astype(BF16)

    def summed_small(value):
        padded_rows = pad_rows(value)
        parts = swap_columns(padded_rows, "seq").reshape(n_seq, padded_rows.shape[0], -1)
        whole = sum_scatter_rows(jnp.sum(parts.astype(F32), axis=0), "dp")
        return gather_rows(whole.astype(BF16), "dp").astype(F32)

    small = summed_small(small)
    conv_columns = swap_columns(d_conv_in, "seq")
    edges = summed_small(edges)
    out_part = sum_scatter_rows(matmul_tn(out_columns, cot_all), "dp")
    d_out_proj = gather_rows(out_part.astype(BF16), "dp").astype(F32)

    gate_part = sum_scatter_rows(matmul_tn(normed_all, gate_columns), "dp").astype(BF16)
    conv_part = sum_scatter_rows(matmul_tn(normed_all, conv_columns), "dp").astype(BF16)
    half = n_seq // 2
    even = mine % 2 == 0
    straight = [(i, i // 2 + (0 if i % 2 == 0 else half)) for i in range(n_seq)]
    crossed = [(i, i // 2 + (half if i % 2 == 0 else 0)) for i in range(n_seq)]
    first = lax.ppermute(jnp.where(even, conv_part, gate_part), "seq", straight)
    second = lax.ppermute(jnp.where(even, gate_part, conv_part), "seq", crossed)
    low_half = mine < half
    d_in_part = jnp.concatenate(
        [jnp.where(low_half, first, second), jnp.where(low_half, second, first)], axis=1
    )
    d_in_proj = gather_rows(d_in_part, "dp").astype(F32)

    d_normed = matmul_nt(d_conv_in, in_proj[:, :inner]) + matmul_nt(d_gate, in_proj[:, inner:])
    d_norm_gain = jnp.sum(d_normed * token_float * inverse, axis=0)
    scaled = d_normed * norm_gain
    cubed = inverse * inverse * inverse
    d_tokens = (
        cot.astype(F32)
        + inverse * scaled
        - token_float * cubed * jnp.mean(scaled * token_float, axis=-1, keepdims=True)
    )
    gain_parts = swap_columns(d_norm_gain[None], "seq")
    d_norm_gain = jnp.sum(gather_rows(jnp.sum(gain_parts, axis=0, keepdims=True), "dp"), axis=0)

    return (
        split(output),
        split(d_tokens),
        d_conv_state,
        d_entry,
        d_norm_gain,
        d_in_proj,
        edges[:taps],
        edges[taps],
        small[: rank + 2 * states].T,
        small[rank + 2 * states : 2 * rank + 2 * states],
        small[2 * rank + 3 * states],
        small[2 * rank + 2 * states : 2 * rank + 3 * states],
        small[2 * rank + 3 * states + 1],
        d_out_proj,
    )


def solution(mesh):
    by_token, by_segment, whole = P("dp", "seq", None), P("dp", None, None), P()
    return jax.shard_map(
        body,
        mesh=mesh,
        in_specs=(by_token, by_segment, by_segment) + (whole,) * 10 + (by_token,),
        out_specs=(
            by_token, by_token, by_segment, by_segment, P("seq"), P(None, "seq"), P(None, "seq"), P("seq"),
            P("seq", None), P(None, "seq"), P("seq"), P(None, "seq"), P("seq"), P("seq", None),
        ),
        check_vma=False,
    )
```

```python
import functools
import math

import jax
import jax.numpy as jnp
from jax import lax
from jax.experimental import pallas as pl
from jax.experimental.pallas import tpu as pltpu
from jax.sharding import PartitionSpec as P

EPS = 1e-05
LANES = 128
CHUNK = 16
LOG2E = math.log2(math.e)
LN2 = math.log(2.0)
BF16 = jnp.bfloat16
F32 = jnp.float32
VMEM_BYTES = 56 * 2**20


def silu_parts(value):
    sigmoid = jax.nn.sigmoid(value)
    return value * sigmoid, sigmoid * (1.0 + value * (1.0 - sigmoid))


def matmul(left, right):
    return lax.dot_general(left, right, (((1,), (0,)), ((), ())), preferred_element_type=F32)


def matmul_nt(left, right):
    return lax.dot_general(left, right, (((1,), (1,)), ((), ())), preferred_element_type=F32)


def matmul_tn(left, right):
    return lax.dot_general(left, right, (((0,), (0,)), ((), ())), preferred_element_type=F32)


def partner_route(axis, step):
    count = lax.axis_size(axis)
    if count & (count - 1) == 0:
        return [(i, i ^ step) for i in range(count)]
    return [(i, (i + step) % count) for i in range(count)]


def partners(axis, step):
    count, mine = lax.axis_size(axis), lax.axis_index(axis)
    if count & (count - 1) == 0:
        return mine ^ step, mine ^ step
    return (mine + step) % count, (mine + count - step) % count


def swap_columns(block, axis):
    count = lax.axis_size(axis)
    rows, width = block.shape[0], block.shape[1] // count
    gathered = jnp.zeros((count * rows, width), block.dtype)
    for step in range(count):
        target, source = partners(axis, step)
        piece = lax.dynamic_slice_in_dim(block, target * width, width, 1)
        if step:
            piece = lax.ppermute(piece, axis, partner_route(axis, step))
        gathered = lax.dynamic_update_slice_in_dim(gathered, piece, source * rows, 0)
    return gathered


def sum_scatter(blocks, axis):
    count, mine = lax.axis_size(axis), lax.axis_index(axis)
    if count & (count - 1):
        return lax.psum_scatter(blocks, axis, scatter_dimension=0)
    levels = count.bit_length() - 1
    held = blocks.reshape((2,) * levels + blocks.shape[1:])
    for level in range(levels):
        bit = (mine >> level) & 1
        at = levels - 1 - level
        sent = lax.dynamic_index_in_dim(held, 1 - bit, at, keepdims=False).astype(BF16)
        arrived = lax.ppermute(sent, axis, [(i, i ^ (1 << level)) for i in range(count)])
        held = lax.dynamic_index_in_dim(held, bit, at, keepdims=False).astype(F32) + arrived.astype(F32)
    return held


def gather_rows(block, axis):
    count = lax.axis_size(axis)
    rows = block.shape[0]
    gathered = jnp.zeros((count * rows,) + block.shape[1:], block.dtype)
    for step in range(count):
        _, source = partners(axis, step)
        piece = lax.ppermute(block, axis, partner_route(axis, step)) if step else block
        gathered = lax.dynamic_update_slice_in_dim(gathered, piece, source * rows, 0)
    return gathered


def shifted(block, axis, distance):
    devices = range(lax.axis_size(axis))
    route = [(i - distance, i) for i in devices if i - distance in devices]
    return lax.ppermute(block, axis, route)


def from_first(block, axis):
    count, mine = lax.axis_size(axis), lax.axis_index(axis)
    reach = 1
    while reach < count:
        route = [(i, i + reach) for i in range(min(reach, count - reach))]
        arrived = lax.ppermute(block, axis, route)
        block = jnp.where(mine < reach, block, arrived)
        reach *= 2
    return block


MESH = pl.DeviceIdType.MESH


def carry_kernel(
    pieces, end_ref, mu_ref, total_ref, entry_ref, a_ref, start_ref, lam_ref,
    ahead, back, from_left, from_right, sent_right, sent_left, got_left, got_right,
):
    count, mine = lax.axis_size("seq"), lax.axis_index("seq")
    width = end_ref.shape[2] // pieces
    has_left, has_right = mine > 0, mine < count - 1
    left, right = jnp.maximum(mine - 1, 0), jnp.minimum(mine + 1, count - 1)

    barrier = pltpu.get_barrier_semaphore()

    @pl.when(has_left)
    def _():
        pl.semaphore_signal(barrier, inc=1, device_id={"seq": left}, device_id_type=MESH)

    @pl.when(has_right)
    def _():
        pl.semaphore_signal(barrier, inc=1, device_id={"seq": right}, device_id_type=MESH)

    pl.semaphore_wait(barrier, has_left.astype(jnp.int32) + has_right.astype(jnp.int32))

    def at(piece):
        return pl.ds(pl.multiple_of(piece * width, LANES), width)

    def to_right(piece):
        return pltpu.make_async_remote_copy(
            src_ref=ahead.at[:, :, at(piece)], dst_ref=from_left.at[:, :, at(piece)],
            send_sem=sent_right.at[piece], recv_sem=got_left.at[piece],
            device_id={"seq": right}, device_id_type=MESH,
        )

    def to_left(piece):
        return pltpu.make_async_remote_copy(
            src_ref=back.at[:, :, at(piece)], dst_ref=from_right.at[:, :, at(piece)],
            send_sem=sent_left.at[piece], recv_sem=got_right.at[piece],
            device_id={"seq": left}, device_id_type=MESH,
        )

    def decay(piece):
        return jnp.exp(total_ref[:, :, at(piece)] * a_ref[:, at(piece)][None])

    def step(tick, nothing):
        piece = tick - mine

        @pl.when(jnp.logical_and(piece >= 0, piece < pieces))
        def _():
            @pl.when(has_left)
            def _():
                to_right(piece).wait_recv()
                start_ref[:, :, at(piece)] = from_left[:, :, at(piece)]

            @pl.when(jnp.logical_not(has_left))
            def _():
                start_ref[:, :, at(piece)] = entry_ref[:, :, at(piece)]

            @pl.when(has_right)
            def _():
                ahead[:, :, at(piece)] = end_ref[:, :, at(piece)] + decay(piece) * start_ref[:, :, at(piece)]
                to_right(piece).start()

        other = tick - (count - 1 - mine)

        @pl.when(jnp.logical_and(other >= 0, other < pieces))
        def _():
            @pl.when(has_right)
            def _():
                to_left(other).wait_recv()
                lam_ref[:, :, at(other)] = from_right[:, :, at(other)]

            @pl.when(jnp.logical_not(has_right))
            def _():
                lam_ref[:, :, at(other)] = jnp.zeros(lam_ref.shape[:2] + (width,), F32)

            @pl.when(has_left)
            def _():
                back[:, :, at(other)] = mu_ref[:, :, at(other)] + decay(other) * lam_ref[:, :, at(other)]
                to_left(other).start()

        return nothing

    lax.fori_loop(0, pieces + count - 1, step, 0)

    def finish(piece, nothing):
        @pl.when(has_right)
        def _():
            to_right(piece).wait_send()

        @pl.when(has_left)
        def _():
            to_left(piece).wait_send()

        return nothing

    lax.fori_loop(0, pieces, finish, 0)


def carry(ends, entry_mu, total, entry_state, a_mat):
    pieces = 6
    while ends.shape[2] % (pieces * LANES):
        pieces -= 1
    shape = jax.ShapeDtypeStruct(ends.shape, F32)
    held = pltpu.VMEM(ends.shape, F32)
    vmem = pl.BlockSpec(memory_space=pltpu.VMEM)
    return pl.pallas_call(
        functools.partial(carry_kernel, pieces),
        in_specs=[vmem] * 5,
        out_specs=[vmem] * 2,
        out_shape=[shape, shape],
        scratch_shapes=[held] * 4 + [pltpu.SemaphoreType.DMA((pieces,))] * 4,
        compiler_params=pltpu.CompilerParams(
            collective_id=1, has_side_effects=True, vmem_limit_bytes=32 * 2**20
        ),
        name="carry",
    )(ends, entry_mu, total, entry_state, a_mat)


def spread_row(ref, rows, at, tile, states):
    row = ref.at[0, rows][at : at + 1, tile * LANES : (tile + 1) * LANES]
    return jnp.broadcast_to(row, (states, LANES))


def column(tile):
    return slice(tile * LANES, (tile + 1) * LANES)


def ends_kernel(d_ref, act_ref, gate_ref, dg_ref, b_ref, c_ref, a_ref, end_ref, mu_ref, drive, up):
    states = a_ref.shape[0]
    length, width = d_ref.shape[1:]
    tiles = width // LANES
    rate = [a_ref[:, column(j)] * LOG2E for j in range(tiles)]
    drive[0] = d_ref[0] * act_ref[0].astype(F32)
    gate = gate_ref[0]
    up[0] = dg_ref[0] * (gate * jax.nn.sigmoid(gate))

    def chunk(i, carry):
        h, p, mu = (list(part) for part in carry)
        rows = pl.ds(pl.multiple_of(i * CHUNK, CHUNK), CHUNK)
        for r in range(CHUNK):
            b, c = b_ref[0, i * CHUNK + r], c_ref[0, i * CHUNK + r]
            for j in range(tiles):
                decay = jnp.exp2(spread_row(d_ref, rows, r, j, states) * rate[j])
                h[j] = h[j] * decay + spread_row(drive, rows, r, j, states) * b
                p[j] = p[j] * decay
                mu[j] = mu[j] + p[j] * (spread_row(up, rows, r, j, states) * c)
        return tuple(h), tuple(p), tuple(mu)

    zeros = tuple(jnp.zeros((states, LANES), F32) for _ in range(tiles))
    ones = tuple(jnp.ones((states, LANES), F32) for _ in range(tiles))
    h, _, mu = lax.fori_loop(0, length // CHUNK, chunk, (zeros, ones, zeros))
    for j in range(tiles):
        end_ref[0, :, column(j)] = h[j]
        mu_ref[0, :, column(j)] = mu[j]


def widest(inner, most):
    width = most
    while inner % width:
        width -= LANES
    return width


def block_ends(delta, act, gate_in, d_gated, b_wide, c_wide, a_mat):
    segs, length, inner = delta.shape
    states = a_mat.shape[0]
    width = widest(inner, 512)
    tokens = pl.BlockSpec((1, length, width), lambda s, e: (s, 0, e))
    wide = pl.BlockSpec((1, length, states, LANES), lambda s, e: (s, 0, 0, 0))
    state = pl.BlockSpec((1, states, width), lambda s, e: (s, 0, e))
    shape = jax.ShapeDtypeStruct((segs, states, inner), F32)
    return pl.pallas_call(
        ends_kernel,
        grid=(segs, inner // width),
        in_specs=[tokens] * 4 + [wide, wide, pl.BlockSpec((states, width), lambda s, e: (0, e))],
        out_specs=[state, state],
        out_shape=[shape, shape],
        scratch_shapes=[pltpu.VMEM((1, length, width), F32)] * 2,
        compiler_params=pltpu.CompilerParams(vmem_limit_bytes=VMEM_BYTES),
        cost_estimate=pl.CostEstimate(
            flops=9 * delta.size * states, bytes_accessed=12 * delta.size, transcendentals=delta.size * states
        ),
        name="block_ends",
    )(delta, act, gate_in, d_gated, b_wide, c_wide, a_mat)


def scan_kernel(
    hosted, n_blocks_static, d_ref, act_ref, gate_ref, dg_ref, b_ref, c_ref, c_diag, b_diag, ones_ref, a_ref, skip_ref, start_ref, end_ref,
    gated_ref, dgate_ref, dpre_ref, dact_ref, db_ref, dc_ref, da_ref, sums_ref, gated_all, gate_all,
    history, drive, up, low_a, low_b, through_a, through_b, db_acc, dc_acc, sum_acc,
    gated_out, gate_out, gated_sent, gated_got, gate_sent, gate_got, own_sem,
):
    states = a_ref.shape[0]
    length, width = d_ref.shape[1:]
    tiles, chunks = width // LANES, length // CHUNK
    span = math.gcd(width, 256)
    parts = width // span
    rate = [a_ref[:, column(j)] * LOG2E for j in range(tiles)]
    seg, block, n_blocks = pl.program_id(0), pl.program_id(1), pl.num_programs(1)
    n_dp, n_seq = lax.axis_size("dp"), lax.axis_size("seq")
    my_dp, my_seq = lax.axis_index("dp"), lax.axis_index("seq")
    tick = seg * n_blocks + block
    slot = lax.rem(tick, 2)
    channels = n_blocks_static * width // n_seq
    owners = width // channels if hosted else 0

    @pl.when(tick == 0)
    def _():
        barrier = pltpu.get_barrier_semaphore()
        for p in range(1, n_dp):
            pl.semaphore_signal(barrier, inc=1, device_id={"dp": lax.rem(my_dp + p, n_dp)}, device_id_type=MESH)
        for p in range(1, n_seq if hosted else 1):
            pl.semaphore_signal(barrier, inc=1, device_id={"seq": lax.rem(my_seq + p, n_seq)}, device_id_type=MESH)
        pl.semaphore_wait(barrier, n_dp - 1 + (n_seq - 1 if hosted else 0))

    def gated_copies(s, e, slot):
        at = (my_dp, s, slice(None), pl.ds(pl.multiple_of(e * width, LANES), width))
        own = pltpu.make_async_copy(gated_out.at[slot], gated_all.at[at], own_sem.at[slot, 0])
        far = [
            pltpu.make_async_remote_copy(
                src_ref=gated_out.at[slot], dst_ref=gated_all.at[at],
                send_sem=gated_sent.at[slot, p], recv_sem=gated_got.at[my_dp],
                device_id={"dp": lax.rem(my_dp + p, n_dp)}, device_id_type=MESH,
            )
            for p in range(1, n_dp)
        ]
        return own, far

    def gate_copies(s, e, slot):
        for q in range(owners):
            owner = e * owners + q
            source = gate_out.at[slot, :, q * channels : (q + 1) * channels]
            own = pltpu.make_async_copy(source, gate_all.at[my_seq, s], own_sem.at[slot, 1 + q])
            far = pltpu.make_async_remote_copy(
                src_ref=source, dst_ref=gate_all.at[my_seq, s],
                send_sem=gate_sent.at[slot, q], recv_sem=gate_got.at[my_seq],
                device_id={"seq": owner}, device_id_type=MESH,
            )
            yield owner, own, far

    def send(s, e, slot):
        own, far = gated_copies(s, e, slot)
        own.start()
        for copy in far:
            copy.start()
        for owner, own, far in gate_copies(s, e, slot):
            pl.when(owner == my_seq)(own.start)
            pl.when(owner != my_seq)(far.start)

    def drain(s, e, slot):
        own, far = gated_copies(s, e, slot)
        own.wait()
        for copy in far:
            copy.wait_send()
        for owner, own, far in gate_copies(s, e, slot):
            pl.when(owner == my_seq)(own.wait)
            pl.when(owner != my_seq)(far.wait_send)

    @pl.when(tick >= 2)
    def _():
        drain((tick - 2) // n_blocks, lax.rem(tick - 2, n_blocks), slot)

    history[0:states, :] = start_ref[0]
    drive[0] = d_ref[0] * act_ref[0].astype(F32)
    gate_block = gate_ref[0]
    up[0] = dg_ref[0] * (gate_block * jax.nn.sigmoid(gate_block))
    sum_acc[...] = jnp.zeros_like(sum_acc)

    def rows_of(i):
        return pl.ds(pl.multiple_of(i * CHUNK, CHUNK), CHUNK)

    def kept(i, r):
        return pl.ds(pl.multiple_of((i * CHUNK + r) * states, states), states)

    def sum_y(i, low, part):
        at, rows = slice(part * span, (part + 1) * span), rows_of(i)
        produced = jnp.dot(c_diag[0, i], low[:, at], preferred_element_type=F32)
        scanned = produced + skip_ref[:, at] * act_ref[0, rows, at].astype(F32)
        gate = gate_ref[0, rows, at]
        sigmoid = jax.nn.sigmoid(gate)
        gated = (scanned * (gate * sigmoid)).astype(BF16)
        slope = sigmoid * (1.0 + gate * (1.0 - sigmoid))
        d_gate = (dg_ref[0, rows, at] * scanned * slope).astype(BF16)
        gated_ref[0, rows, at] = gated
        dgate_ref[0, rows, at] = d_gate
        gated_out[slot, rows, at] = gated
        if hosted:
            gate_out[slot, rows, at] = d_gate

    def forward(i, h, low, before, low_before):
        rows = rows_of(i)
        waiting = list(range(parts))
        for r in range(CHUNK):
            b = b_ref[0, i * CHUNK + r]
            for j in range(tiles):
                decay = jnp.exp2(spread_row(d_ref, rows, r, j, states) * rate[j])
                h[j] = h[j] * decay + spread_row(drive, rows, r, j, states) * b
                history[kept(i, r + 1), column(j)] = h[j]
                low[r * states : (r + 1) * states, column(j)] = h[j].astype(BF16)
            if waiting and r % max(1, CHUNK // parts) == 1:
                sum_y(before, low_before, waiting.pop(0))
        for part in waiting:
            sum_y(before, low_before, part)
        return h

    def forward_pair(pair, carry):
        h = forward(2 * pair, list(carry), low_a, jnp.maximum(2 * pair - 1, 0), low_b)
        return tuple(forward(2 * pair + 1, h, low_b, 2 * pair, low_a))

    lax.fori_loop(0, chunks // 2, forward_pair, tuple(start_ref[0, :, column(j)] for j in range(tiles)))
    for part in range(parts):
        sum_y(chunks - 1, low_b, part)
    send(seg, block, slot)

    @pl.when(pl.program_id(1) == 0)
    def _():
        db_acc[...] = jnp.zeros_like(db_acc)
        dc_acc[...] = jnp.zeros_like(dc_acc)

    def sum_back(i, low, through, part, count=None):
        at, rows = slice(part * span, (part + 1) * span), rows_of(i)
        d_drive = jnp.dot(b_diag[0, i], low[:, at], preferred_element_type=F32)
        d_rate = jnp.dot(ones_ref[...], through[:, at], preferred_element_type=F32)
        delta, act, d_scanned = d_ref[0, rows, at], act_ref[0, rows, at].astype(F32), up[0, rows, at]
        near = delta * (1.0 - delta * (0.5 - delta * (1.0 / 6.0 - delta * (1.0 / 24.0))))
        slope = jnp.where(delta < 0.03, near, 1.0 - jnp.exp(-delta))
        d_pre = (LN2 * d_rate + d_drive * act) * slope
        dpre_ref[0, rows, at] = d_pre.astype(BF16)
        dact_ref[0, rows, at] = skip_ref[:, at] * d_scanned + d_drive * delta
        if count is None:
            sum_acc[0, :, at] += d_pre
            sum_acc[1, :, at] += d_scanned * act
        else:
            sum_acc[0, :, at] += jnp.where(count, d_pre, 0.0)
            sum_acc[1, :, at] += jnp.where(count, d_scanned * act, 0.0)

    def backward(i, lam, da, low, through, before, low_before, through_before, count=None):
        rows = rows_of(i)
        waiting = list(range(parts))
        for r in reversed(range(CHUNK)):
            c = c_ref[0, i * CHUNK + r]
            db = dc = None
            for j in range(tiles):
                step = spread_row(d_ref, rows, r, j, states)
                upstream = spread_row(up, rows, r, j, states)
                adjoint = lam[j] + upstream * c
                db_j = adjoint * spread_row(drive, rows, r, j, states)
                dc_j = upstream * history[kept(i, r + 1), column(j)]
                db, dc = (db_j, dc_j) if db is None else (db + db_j, dc + dc_j)
                low[r * states : (r + 1) * states, column(j)] = adjoint.astype(BF16)
                lam[j] = adjoint * jnp.exp2(step * rate[j])
                flow = lam[j] * history[kept(i, r), column(j)]
                through[r * states : (r + 1) * states, column(j)] = (flow * rate[j]).astype(BF16)
                da[j] = da[j] + flow * step
            db_acc[i * CHUNK + r] += db
            dc_acc[i * CHUNK + r] += dc
            if waiting and (CHUNK - 1 - r) % max(1, CHUNK // parts) == 1:
                sum_back(before, low_before, through_before, waiting.pop(0), count)
        for part in waiting:
            sum_back(before, low_before, through_before, part, count)
        return lam, da

    def backward_pair(pair, carry):
        lam, da = (list(part) for part in carry)
        i = chunks - 1 - 2 * pair
        lam, da = backward(i, lam, da, low_a, through_a, jnp.minimum(i + 1, chunks - 1), low_b, through_b, pair > 0)
        lam, da = backward(i - 1, lam, da, low_b, through_b, i, low_a, through_a)
        return tuple(lam), tuple(da)

    zeros = tuple(jnp.zeros((states, LANES), F32) for _ in range(tiles))
    _, da = lax.fori_loop(
        0, chunks // 2, backward_pair, (tuple(end_ref[0, :, column(j)] for j in range(tiles)), zeros)
    )
    for part in range(parts):
        sum_back(0, low_b, through_b, part)
    for j in range(tiles):
        da_ref[0, :, column(j)] = da[j]
    sums_ref[0, 0:1, :] = jnp.sum(sum_acc[0], axis=0, keepdims=True)
    sums_ref[0, 1:2, :] = jnp.sum(sum_acc[1], axis=0, keepdims=True)
    sums_ref[0, 2:8, :] = jnp.zeros((6, width), F32)

    @pl.when(pl.program_id(1) == pl.num_programs(1) - 1)
    def _():
        db_ref[0] = jnp.sum(db_acc[...], axis=-1)
        dc_ref[0] = jnp.sum(dc_acc[...], axis=-1)

    @pl.when(tick == pl.num_programs(0) * n_blocks - 1)
    def _():
        drain((tick - 1) // n_blocks, lax.rem(tick - 1, n_blocks), 1 - slot)
        drain(seg, block, slot)
        for p in range(1, n_dp):
            source = lax.rem(my_dp + p, n_dp)
            pltpu.make_async_remote_copy(
                src_ref=gated_all.at[source], dst_ref=gated_all.at[source],
                send_sem=gated_sent.at[0, 0], recv_sem=gated_got.at[source],
                device_id={"dp": source}, device_id_type=MESH,
            ).wait_recv()
        for p in range(1, n_seq if hosted else 1):
            source = lax.rem(my_seq + p, n_seq)
            pltpu.make_async_remote_copy(
                src_ref=gate_all.at[source], dst_ref=gate_all.at[source],
                send_sem=gate_sent.at[0, 0], recv_sem=gate_got.at[source],
                device_id={"seq": source}, device_id_type=MESH,
            ).wait_recv()


def scan_both(delta, act, gate_in, d_gated, b_wide, c_wide, c_diag, b_diag, ones_diag, a_mat, d_skip, start, end):
    segs, length, inner = delta.shape
    states = a_mat.shape[0]
    width = widest(inner, 768)
    tokens = pl.BlockSpec((1, length, width), lambda s, e: (s, 0, e))
    wide = pl.BlockSpec((1, length, states, LANES), lambda s, e: (s, 0, 0, 0))
    diag = pl.BlockSpec((1,) + c_diag.shape[1:], lambda s, e: (s, 0, 0, 0))
    state = pl.BlockSpec((1, states, width), lambda s, e: (s, 0, e))
    narrow = pl.BlockSpec((1, length, states), lambda s, e: (s, 0, 0))
    by_token = jax.ShapeDtypeStruct((segs, length, inner), F32)
    by_token_low = jax.ShapeDtypeStruct((segs, length, inner), BF16)
    by_state = jax.ShapeDtypeStruct((segs, length, states), F32)
    low = pltpu.VMEM((CHUNK * states, width), BF16)
    lanes = pltpu.VMEM((length, states, LANES), F32)
    n_dp, n_seq = lax.axis_size("dp"), lax.axis_size("seq")
    channels = inner // n_seq
    hosted = channels % LANES == 0 and width % channels == 0
    dma = pltpu.SemaphoreType.DMA
    out = pltpu.VMEM((2, length, width), BF16)
    return pl.pallas_call(
        functools.partial(scan_kernel, hosted, inner // width),
        grid=(segs, inner // width),
        in_specs=[
            tokens, tokens, tokens, tokens, wide, wide, diag, diag,
            pl.BlockSpec(ones_diag.shape, lambda s, e: (0, 0)),
            pl.BlockSpec((states, width), lambda s, e: (0, e)),
            pl.BlockSpec((1, width), lambda s, e: (0, e)),
            state, state,
        ],
        out_specs=[
            tokens, tokens, tokens, tokens, narrow, narrow, state,
            pl.BlockSpec((1, 8, width), lambda s, e: (s, 0, e)),
            pl.BlockSpec(memory_space=pl.ANY),
            pl.BlockSpec(memory_space=pl.ANY),
        ],
        out_shape=[
            by_token_low, by_token_low, by_token_low, by_token, by_state, by_state,
            jax.ShapeDtypeStruct((segs, states, inner), F32),
            jax.ShapeDtypeStruct((segs, 8, inner), F32),
            jax.ShapeDtypeStruct((n_dp, segs, length, inner), BF16),
            jax.ShapeDtypeStruct((n_seq, segs, length, channels), BF16),
        ],
        scratch_shapes=[
            pltpu.VMEM(((length + 1) * states, width), F32),
            pltpu.VMEM((1, length, width), F32),
            pltpu.VMEM((1, length, width), F32),
            low, low, low, low, lanes, lanes,
            pltpu.VMEM((2, CHUNK, width), F32),
            out, out,
            dma((2, n_dp)), dma((n_dp,)), dma((2, n_seq)), dma((n_seq,)), dma((2, 1 + n_seq)),
        ],
        compiler_params=pltpu.CompilerParams(
            collective_id=2, has_side_effects=True, vmem_limit_bytes=VMEM_BYTES
        ),
        cost_estimate=pl.CostEstimate(
            flops=20 * delta.size * states, bytes_accessed=24 * delta.size, transcendentals=2 * delta.size * states
        ),
        name="scan_both",
    )(delta, act, gate_in, d_gated, b_wide, c_wide, c_diag, b_diag, ones_diag, a_mat, d_skip[None], start, end)


def diagonal_blocks(value):
    segs, length, states = value.shape
    spread = value.reshape(segs, length // CHUNK, CHUNK, 1, states)
    spread = spread * jnp.eye(CHUNK, dtype=value.dtype)[:, :, None]
    return spread.reshape(segs, length // CHUNK, CHUNK, CHUNK * states).astype(BF16)


def body(
    tokens, conv_state, entry_state, norm_gain, in_proj, conv_weight, conv_bias, x_proj,
    dt_proj, dt_bias, a_log, d_skip, out_proj, cotangent,
):
    segs, length, width = tokens.shape
    inner = in_proj.shape[1] // 2
    rank, states, taps = dt_proj.shape[0], a_log.shape[0], conv_weight.shape[0]
    halo = taps - 1
    count = segs * length
    n_seq = lax.axis_size("seq")
    mine = lax.axis_index("seq")
    is_first = mine == 0

    def flat(value):
        return value.reshape((count,) + value.shape[2:])

    def split(value):
        return value.reshape((segs, length) + value.shape[1:])

    token_float = flat(tokens).astype(F32)
    inverse = lax.rsqrt(jnp.mean(token_float * token_float, axis=-1, keepdims=True) + EPS)
    normed = (token_float * inverse * norm_gain).astype(BF16)
    cot = flat(cotangent)
    normed_all = lax.all_gather(normed, "seq", axis=0, tiled=True)
    cot_columns = swap_columns(cot, "dp")
    conv_in = matmul(normed, in_proj[:, :inner]).astype(BF16)
    gate_in = matmul(normed, in_proj[:, inner:])
    d_gated = matmul_nt(cot, out_proj)
    conv_in = split(conv_in)
    before = jnp.where(is_first, conv_state, shifted(conv_in[:, length - halo :], "seq", 1))
    padded = jnp.concatenate([before, conv_in], axis=1).astype(F32)
    conv_out = conv_bias + sum(conv_weight[tap] * padded[:, tap : tap + length] for tap in range(taps))
    activated = (conv_out * jax.nn.sigmoid(conv_out)).astype(BF16)
    coeffs = matmul(flat(activated), x_proj)
    dt_low = coeffs[:, :rank].astype(BF16)
    b_in = split(coeffs[:, rank : rank + states])
    c_in = split(coeffs[:, rank + states :])
    pre_delta = matmul(dt_low, dt_proj) + dt_bias
    delta = split(jax.nn.softplus(pre_delta))
    a_mat = -jnp.exp(a_log)
    gate_in, d_gated = split(gate_in), split(d_gated)

    b_wide = jnp.broadcast_to(b_in[..., None], b_in.shape + (LANES,))
    c_wide = jnp.broadcast_to(c_in[..., None], c_in.shape + (LANES,))
    ends, entry_mu = block_ends(delta, activated, gate_in, d_gated, b_wide, c_wide, a_mat)
    total = jnp.sum(delta, axis=1, keepdims=True)
    start, end = carry(ends, entry_mu, total, entry_state, a_mat)
    d_entry = from_first(entry_mu + jnp.exp(total * a_mat) * end, "seq")
    ones_diag = diagonal_blocks(jnp.ones((1, CHUNK, states), F32))[0, 0]
    gated, d_gate, d_pre_low, d_act, d_b, d_c, d_amat, sums, gated_all, gate_columns = scan_both(
        delta, activated, gate_in, d_gated, b_wide, c_wide,
        diagonal_blocks(c_in), diagonal_blocks(b_in), ones_diag, a_mat, d_skip, start, end,
    )
    gated, d_gate, d_pre_low, d_act = flat(gated), flat(d_gate), flat(d_pre_low), flat(d_act)
    gated_all = gated_all.reshape(-1, inner)
    gate_columns = gate_columns.reshape(n_seq * count, -1)
    if (inner // n_seq) % LANES:
        gate_columns = swap_columns(d_gate, "seq")
    output = token_float + matmul(gated, out_proj)

    sums = jnp.sum(sums, axis=0)
    d_dt_bias, d_d_skip = sums[0], sums[1]
    d_dt_proj = matmul_tn(dt_low, d_pre_low)
    d_dt_low = matmul_nt(d_pre_low, dt_proj)
    d_coeffs = jnp.concatenate([d_dt_low, flat(d_b), flat(d_c)], axis=-1).astype(BF16)
    d_x_proj = matmul_tn(d_coeffs, flat(activated))
    d_a_log = jnp.sum(d_amat, axis=0) * a_mat
    d_act = split(d_act + matmul_nt(d_coeffs, x_proj))
    conv_sigmoid = jax.nn.sigmoid(conv_out)
    d_conv_out = d_act * (conv_sigmoid * (1.0 + conv_out * (1.0 - conv_sigmoid)))
    d_conv_bias = jnp.sum(d_conv_out, axis=(0, 1))
    d_conv_weight = jnp.stack(
        [jnp.sum(d_conv_out * padded[:, tap : tap + length], axis=(0, 1)) for tap in range(taps)]
    )
    halo_grad = sum(
        conv_weight[tap] * jnp.pad(d_conv_out[:, : halo - tap], ((0, 0), (tap, 0), (0, 0))) for tap in range(halo)
    )
    returned = shifted(halo_grad, "seq", -1)
    tail = jnp.pad(d_conv_out, ((0, 0), (0, halo), (0, 0)))
    d_conv_in = sum(conv_weight[tap] * tail[:, halo - tap : halo - tap + length] for tap in range(taps))
    d_conv_in = d_conv_in + jnp.pad(returned, ((0, 0), (length - halo, 0), (0, 0)))
    d_conv_in = flat(d_conv_in).astype(BF16)
    d_conv_state = from_first(halo_grad, "seq")

    n_dp = lax.axis_size("dp")
    small = jnp.concatenate([d_x_proj, d_dt_proj, d_a_log, d_dt_bias[None], d_d_skip[None]], axis=0)
    small = jnp.pad(small, ((0, -small.shape[0] % 16), (0, 0))).astype(BF16)
    small_columns = swap_columns(small, "seq")
    edges = jnp.concatenate([d_conv_weight, d_conv_bias[None]], axis=0)
    edges = jnp.pad(edges, ((0, -edges.shape[0] % 16), (0, 0))).astype(BF16)
    conv_columns = swap_columns(jnp.concatenate([d_conv_in, edges], axis=0), "seq").reshape(n_seq, -1, inner // n_seq)
    edge_columns = conv_columns[:, count:]
    conv_columns = conv_columns[:, :count].reshape(n_seq * count, -1)

    def blocks(value, axis):
        return value.reshape((lax.axis_size(axis), -1) + value.shape[1:])

    out_part = sum_scatter(blocks(matmul_tn(gated_all, cot_columns), "seq"), "seq")
    d_out_proj = gather_rows(out_part.astype(BF16)[None], "dp").transpose(1, 0, 2).reshape(out_part.shape[0], -1)
    d_out_proj = d_out_proj.astype(F32)

    gate_part = sum_scatter(blocks(matmul_tn(normed_all, gate_columns), "dp"), "dp").astype(BF16)
    conv_part = sum_scatter(blocks(matmul_tn(normed_all, conv_columns), "dp"), "dp").astype(BF16)
    half = n_seq // 2
    even = mine % 2 == 0
    straight = [(i, i // 2 + (0 if i % 2 == 0 else half)) for i in range(n_seq)]
    crossed = [(i, i // 2 + (half if i % 2 == 0 else 0)) for i in range(n_seq)]
    first = lax.ppermute(jnp.where(even, conv_part, gate_part), "seq", straight)
    second = lax.ppermute(jnp.where(even, gate_part, conv_part), "seq", crossed)
    low_half = mine < half
    d_in_part = jnp.concatenate(
        [jnp.where(low_half, first, second), jnp.where(low_half, second, first)], axis=1
    )
    d_in_proj = gather_rows(d_in_part, "dp").astype(F32)

    d_normed = matmul_nt(d_conv_in, in_proj[:, :inner]) + matmul_nt(d_gate, in_proj[:, inner:])
    d_norm_gain = jnp.sum(d_normed * token_float * inverse, axis=0)
    scaled = d_normed * norm_gain
    cubed = inverse * inverse * inverse
    d_tokens = (
        cot.astype(F32)
        + inverse * scaled
        - token_float * cubed * jnp.mean(scaled * token_float, axis=-1, keepdims=True)
    )
    gain = sum_scatter(blocks(d_norm_gain, "seq"), "seq")
    channels = inner // n_seq
    per_device = jnp.concatenate(
        [
            jnp.sum(small_columns.reshape(n_seq, -1, channels).astype(F32), axis=0),
            jnp.sum(edge_columns.astype(F32), axis=0),
            jnp.pad(gain, (0, -gain.shape[0] % channels)).reshape(-1, channels),
        ],
        axis=0,
    )
    per_device = per_device.astype(BF16)
    summed = jnp.sum(gather_rows(per_device[None], "dp").astype(F32), axis=0)
    edges = summed[small.shape[0] : small.shape[0] + edges.shape[0]]
    d_norm_gain = summed[small.shape[0] + edges.shape[0] :].reshape(-1)[: gain.shape[0]]
    small = summed

    return (
        split(output),
        split(d_tokens),
        d_conv_state,
        d_entry,
        d_norm_gain,
        d_in_proj,
        edges[:taps],
        edges[taps],
        small[: rank + 2 * states].T,
        small[rank + 2 * states : 2 * rank + 2 * states],
        small[2 * rank + 3 * states],
        small[2 * rank + 2 * states : 2 * rank + 3 * states],
        small[2 * rank + 3 * states + 1],
        d_out_proj,
    )


def solution(mesh):
    by_token, by_segment, whole = P("dp", "seq", None), P("dp", None, None), P()
    return jax.shard_map(
        body,
        mesh=mesh,
        in_specs=(by_token, by_segment, by_segment) + (whole,) * 10 + (by_token,),
        out_specs=(
            by_token, by_token, by_segment, by_segment, P("seq"), P(None, "seq"), P(None, "seq"), P("seq"),
            P("seq", None), P(None, "seq"), P("seq"), P(None, "seq"), P("seq"), P("seq", None),
        ),
        check_vma=False,
    )
```

```python
import functools
import math

import jax
import jax.numpy as jnp
from jax import lax
from jax.experimental import pallas as pl
from jax.experimental.pallas import tpu as pltpu
from jax.sharding import PartitionSpec as P

EPS = 1e-05
LANES = 128
CHUNK = 16
LOG2E = math.log2(math.e)
LN2 = math.log(2.0)
BF16 = jnp.bfloat16
F32 = jnp.float32
VMEM_BYTES = 56 * 2**20


def silu_parts(value):
    sigmoid = jax.nn.sigmoid(value)
    return value * sigmoid, sigmoid * (1.0 + value * (1.0 - sigmoid))


def matmul(left, right):
    return lax.dot_general(left, right, (((1,), (0,)), ((), ())), preferred_element_type=F32)


def matmul_nt(left, right):
    return lax.dot_general(left, right, (((1,), (1,)), ((), ())), preferred_element_type=F32)


def matmul_tn(left, right):
    return lax.dot_general(left, right, (((0,), (0,)), ((), ())), preferred_element_type=F32)


def partner_route(axis, step):
    count = lax.axis_size(axis)
    if count & (count - 1) == 0:
        return [(i, i ^ step) for i in range(count)]
    return [(i, (i + step) % count) for i in range(count)]


def partners(axis, step):
    count, mine = lax.axis_size(axis), lax.axis_index(axis)
    if count & (count - 1) == 0:
        return mine ^ step, mine ^ step
    return (mine + step) % count, (mine + count - step) % count


def swap_columns(block, axis):
    count = lax.axis_size(axis)
    rows, width = block.shape[0], block.shape[1] // count
    gathered = jnp.zeros((count * rows, width), block.dtype)
    for step in range(count):
        target, source = partners(axis, step)
        piece = lax.dynamic_slice_in_dim(block, target * width, width, 1)
        if step:
            piece = lax.ppermute(piece, axis, partner_route(axis, step))
        gathered = lax.dynamic_update_slice_in_dim(gathered, piece, source * rows, 0)
    return gathered


def swap_rows(block, axis):
    count = lax.axis_size(axis)
    rows, width = block.shape[0] // count, block.shape[1]
    gathered = jnp.zeros((rows, count * width), block.dtype)
    for step in range(count):
        target, source = partners(axis, step)
        piece = lax.dynamic_slice_in_dim(block, target * rows, rows, 0)
        if step:
            piece = lax.ppermute(piece, axis, partner_route(axis, step))
        gathered = lax.dynamic_update_slice_in_dim(gathered, piece, source * width, 1)
    return gathered


def sum_scatter(blocks, axis):
    count, mine = lax.axis_size(axis), lax.axis_index(axis)
    if count & (count - 1):
        return lax.psum_scatter(blocks, axis, scatter_dimension=0)
    levels = count.bit_length() - 1
    held = blocks.reshape((2,) * levels + blocks.shape[1:])
    for level in range(levels):
        bit = (mine >> level) & 1
        at = levels - 1 - level
        sent = lax.dynamic_index_in_dim(held, 1 - bit, at, keepdims=False).astype(BF16)
        arrived = lax.ppermute(sent, axis, [(i, i ^ (1 << level)) for i in range(count)])
        held = lax.dynamic_index_in_dim(held, bit, at, keepdims=False).astype(F32) + arrived.astype(F32)
    return held


def gather_rows(block, axis):
    count = lax.axis_size(axis)
    rows = block.shape[0]
    gathered = jnp.zeros((count * rows,) + block.shape[1:], block.dtype)
    for step in range(count):
        _, source = partners(axis, step)
        piece = lax.ppermute(block, axis, partner_route(axis, step)) if step else block
        gathered = lax.dynamic_update_slice_in_dim(gathered, piece, source * rows, 0)
    return gathered


def shifted(block, axis, distance):
    devices = range(lax.axis_size(axis))
    route = [(i - distance, i) for i in devices if i - distance in devices]
    return lax.ppermute(block, axis, route)


def from_first(block, axis):
    count, mine = lax.axis_size(axis), lax.axis_index(axis)
    reach = 1
    while reach < count:
        route = [(i, i + reach) for i in range(min(reach, count - reach))]
        arrived = lax.ppermute(block, axis, route)
        block = jnp.where(mine < reach, block, arrived)
        reach *= 2
    return block


MESH = pl.DeviceIdType.MESH


def carry_kernel(
    pieces, end_ref, mu_ref, total_ref, entry_ref, a_ref, start_ref, lam_ref, back,
    ahead, from_left, from_right, sent_right, sent_left, got_left, got_right,
):
    count, mine = lax.axis_size("seq"), lax.axis_index("seq")
    width = end_ref.shape[2] // pieces
    has_left, has_right = mine > 0, mine < count - 1
    left, right = jnp.maximum(mine - 1, 0), jnp.minimum(mine + 1, count - 1)

    barrier = pltpu.get_barrier_semaphore()

    @pl.when(has_left)
    def _():
        pl.semaphore_signal(barrier, inc=1, device_id={"seq": left}, device_id_type=MESH)

    @pl.when(has_right)
    def _():
        pl.semaphore_signal(barrier, inc=1, device_id={"seq": right}, device_id_type=MESH)

    pl.semaphore_wait(barrier, has_left.astype(jnp.int32) + has_right.astype(jnp.int32))

    def at(piece):
        return pl.ds(pl.multiple_of(piece * width, LANES), width)

    def to_right(piece):
        return pltpu.make_async_remote_copy(
            src_ref=ahead.at[:, :, at(piece)], dst_ref=from_left.at[:, :, at(piece)],
            send_sem=sent_right.at[piece], recv_sem=got_left.at[piece],
            device_id={"seq": right}, device_id_type=MESH,
        )

    def to_left(piece):
        return pltpu.make_async_remote_copy(
            src_ref=back.at[:, :, at(piece)], dst_ref=from_right.at[:, :, at(piece)],
            send_sem=sent_left.at[piece], recv_sem=got_right.at[piece],
            device_id={"seq": left}, device_id_type=MESH,
        )

    def decay(piece):
        return jnp.exp(total_ref[:, :, at(piece)] * a_ref[:, at(piece)][None])

    def step(tick, nothing):
        piece = tick - mine

        @pl.when(jnp.logical_and(piece >= 0, piece < pieces))
        def _():
            @pl.when(has_left)
            def _():
                to_right(piece).wait_recv()
                start_ref[:, :, at(piece)] = from_left[:, :, at(piece)]

            @pl.when(jnp.logical_not(has_left))
            def _():
                start_ref[:, :, at(piece)] = entry_ref[:, :, at(piece)]

            @pl.when(has_right)
            def _():
                ahead[:, :, at(piece)] = end_ref[:, :, at(piece)] + decay(piece) * start_ref[:, :, at(piece)]
                to_right(piece).start()

        other = tick - (count - 1 - mine)

        @pl.when(jnp.logical_and(other >= 0, other < pieces))
        def _():
            @pl.when(has_right)
            def _():
                to_left(other).wait_recv()
                lam_ref[:, :, at(other)] = from_right[:, :, at(other)]

            @pl.when(jnp.logical_not(has_right))
            def _():
                lam_ref[:, :, at(other)] = jnp.zeros(lam_ref.shape[:2] + (width,), F32)

            back[:, :, at(other)] = mu_ref[:, :, at(other)] + decay(other) * lam_ref[:, :, at(other)]

            @pl.when(has_left)
            def _():
                to_left(other).start()

        return nothing

    lax.fori_loop(0, pieces + count - 1, step, 0)

    def finish(piece, nothing):
        @pl.when(has_right)
        def _():
            to_right(piece).wait_send()

        @pl.when(has_left)
        def _():
            to_left(piece).wait_send()

        return nothing

    lax.fori_loop(0, pieces, finish, 0)


def carry(ends, entry_mu, total, entry_state, a_mat):
    pieces = 6
    while ends.shape[2] % (pieces * LANES):
        pieces -= 1
    shape = jax.ShapeDtypeStruct(ends.shape, F32)
    held = pltpu.VMEM(ends.shape, F32)
    vmem = pl.BlockSpec(memory_space=pltpu.VMEM)
    return pl.pallas_call(
        functools.partial(carry_kernel, pieces),
        in_specs=[vmem] * 5,
        out_specs=[vmem] * 3,
        out_shape=[shape, shape, shape],
        scratch_shapes=[held] * 3 + [pltpu.SemaphoreType.DMA((pieces,))] * 4,
        compiler_params=pltpu.CompilerParams(
            collective_id=1, has_side_effects=True, vmem_limit_bytes=32 * 2**20
        ),
        name="carry",
    )(ends, entry_mu, total, entry_state, a_mat)


def aligned(inner, axis="seq"):
    channels = inner // lax.axis_size(axis)
    return channels % LANES == 0 and widest(inner, 768) % channels == 0


def spread_row(ref, rows, at, tile, states):
    row = ref.at[0, rows][at : at + 1, tile * LANES : (tile + 1) * LANES]
    return jnp.broadcast_to(row, (states, LANES))


def column(tile):
    return slice(tile * LANES, (tile + 1) * LANES)


def ends_kernel(d_ref, act_ref, gate_ref, dg_ref, b_ref, c_ref, a_ref, end_ref, mu_ref, drive, up):
    states = a_ref.shape[0]
    length, width = d_ref.shape[1:]
    tiles = width // LANES
    rate = [a_ref[:, column(j)] * LOG2E for j in range(tiles)]
    drive[0] = d_ref[0] * act_ref[0].astype(F32)
    gate = gate_ref[0]
    up[0] = dg_ref[0] * (gate * jax.nn.sigmoid(gate))

    def chunk(i, carry):
        h, p, mu = (list(part) for part in carry)
        rows = pl.ds(pl.multiple_of(i * CHUNK, CHUNK), CHUNK)
        for r in range(CHUNK):
            b, c = b_ref[0, i * CHUNK + r], c_ref[0, i * CHUNK + r]
            for j in range(tiles):
                decay = jnp.exp2(spread_row(d_ref, rows, r, j, states) * rate[j])
                h[j] = h[j] * decay + spread_row(drive, rows, r, j, states) * b
                p[j] = p[j] * decay
                mu[j] = mu[j] + p[j] * (spread_row(up, rows, r, j, states) * c)
        return tuple(h), tuple(p), tuple(mu)

    zeros = tuple(jnp.zeros((states, LANES), F32) for _ in range(tiles))
    ones = tuple(jnp.ones((states, LANES), F32) for _ in range(tiles))
    h, _, mu = lax.fori_loop(0, length // CHUNK, chunk, (zeros, ones, zeros))
    for j in range(tiles):
        end_ref[0, :, column(j)] = h[j]
        mu_ref[0, :, column(j)] = mu[j]


def widest(inner, most):
    width = most
    while inner % width:
        width -= LANES
    return width


def block_ends(delta, act, gate_in, d_gated, b_wide, c_wide, a_mat):
    segs, length, inner = delta.shape
    states = a_mat.shape[0]
    width = widest(inner, 512)
    tokens = pl.BlockSpec((1, length, width), lambda s, e: (s, 0, e))
    wide = pl.BlockSpec((1, length, states, LANES), lambda s, e: (s, 0, 0, 0))
    state = pl.BlockSpec((1, states, width), lambda s, e: (s, 0, e))
    shape = jax.ShapeDtypeStruct((segs, states, inner), F32)
    return pl.pallas_call(
        ends_kernel,
        grid=(segs, inner // width),
        in_specs=[tokens] * 4 + [wide, wide, pl.BlockSpec((states, width), lambda s, e: (0, e))],
        out_specs=[state, state],
        out_shape=[shape, shape],
        scratch_shapes=[pltpu.VMEM((1, length, width), F32)] * 2,
        compiler_params=pltpu.CompilerParams(vmem_limit_bytes=VMEM_BYTES),
        cost_estimate=pl.CostEstimate(
            flops=9 * delta.size * states, bytes_accessed=12 * delta.size, transcendentals=delta.size * states
        ),
        name="block_ends",
    )(delta, act, gate_in, d_gated, b_wide, c_wide, a_mat)


def scan_kernel(
    hosted, n_blocks_static, d_ref, act_ref, gate_ref, dg_ref, b_ref, c_ref, c_diag, b_diag, ones_ref, a_ref, skip_ref, start_ref, end_ref, first_ref,
    gated_ref, dgate_ref, dpre_ref, dact_ref, db_ref, dc_ref, da_ref, sums_ref, gated_all, gate_all, first_all,
    history, drive, up, low_a, low_b, through_a, through_b, db_acc, dc_acc, sum_acc,
    gated_out, gate_out, gated_sent, gated_got, gate_sent, gate_got, own_sem, first_sent, first_got,
):
    states = a_ref.shape[0]
    length, width = d_ref.shape[1:]
    tiles, chunks = width // LANES, length // CHUNK
    span = math.gcd(width, 256)
    parts = width // span
    rate = [a_ref[:, column(j)] * LOG2E for j in range(tiles)]
    seg, block, n_blocks = pl.program_id(0), pl.program_id(1), pl.num_programs(1)
    n_dp, n_seq = lax.axis_size("dp"), lax.axis_size("seq")
    my_dp, my_seq = lax.axis_index("dp"), lax.axis_index("seq")
    tick = seg * n_blocks + block
    slot = lax.rem(tick, 2)
    channels = n_blocks_static * width // n_seq
    owners = width // channels if hosted else 0

    first_own = pltpu.make_async_copy(first_ref, first_all, first_got.at[0])
    first_far = pltpu.make_async_remote_copy(
        src_ref=first_all, dst_ref=first_all, send_sem=first_sent.at[0], recv_sem=first_got.at[0],
        device_id={"seq": jnp.minimum(my_seq + 1, n_seq - 1)}, device_id_type=MESH,
    )

    @pl.when(tick == 0)
    def _():
        barrier = pltpu.get_barrier_semaphore()
        for p in range(1, n_dp):
            pl.semaphore_signal(barrier, inc=1, device_id={"dp": lax.rem(my_dp + p, n_dp)}, device_id_type=MESH)
        for p in range(1, n_seq):
            pl.semaphore_signal(barrier, inc=1, device_id={"seq": lax.rem(my_seq + p, n_seq)}, device_id_type=MESH)
        pl.semaphore_wait(barrier, n_dp + n_seq - 2)

        @pl.when(my_seq == 0)
        def _():
            first_own.start()

    @pl.when(tick == jnp.minimum(my_seq, pl.num_programs(0) * n_blocks - 1))
    def _():
        @pl.when(my_seq == 0)
        def _():
            first_own.wait()

        @pl.when(my_seq != 0)
        def _():
            first_far.wait_recv()

        @pl.when(my_seq != n_seq - 1)
        def _():
            first_far.start()

    def gated_copies(s, e, slot):
        at = (my_dp, s, slice(None), pl.ds(pl.multiple_of(e * width, LANES), width))
        own = pltpu.make_async_copy(gated_out.at[slot], gated_all.at[at], own_sem.at[slot, 0])
        far = [
            pltpu.make_async_remote_copy(
                src_ref=gated_out.at[slot], dst_ref=gated_all.at[at],
                send_sem=gated_sent.at[slot, p], recv_sem=gated_got.at[my_dp],
                device_id={"dp": lax.rem(my_dp + p, n_dp)}, device_id_type=MESH,
            )
            for p in range(1, n_dp)
        ]
        return own, far

    def gate_copies(s, e, slot):
        for q in range(owners):
            owner = e * owners + q
            source = gate_out.at[slot, :, q * channels : (q + 1) * channels]
            own = pltpu.make_async_copy(source, gate_all.at[my_seq, s], own_sem.at[slot, 1 + q])
            far = pltpu.make_async_remote_copy(
                src_ref=source, dst_ref=gate_all.at[my_seq, s],
                send_sem=gate_sent.at[slot, q], recv_sem=gate_got.at[my_seq],
                device_id={"seq": owner}, device_id_type=MESH,
            )
            yield owner, own, far

    def send(s, e, slot):
        own, far = gated_copies(s, e, slot)
        own.start()
        for copy in far:
            copy.start()
        for owner, own, far in gate_copies(s, e, slot):
            pl.when(owner == my_seq)(own.start)
            pl.when(owner != my_seq)(far.start)

    def drain(s, e, slot):
        own, far = gated_copies(s, e, slot)
        own.wait()
        for copy in far:
            copy.wait_send()
        for owner, own, far in gate_copies(s, e, slot):
            pl.when(owner == my_seq)(own.wait)
            pl.when(owner != my_seq)(far.wait_send)

    @pl.when(tick >= 2)
    def _():
        drain((tick - 2) // n_blocks, lax.rem(tick - 2, n_blocks), slot)

    history[0:states, :] = start_ref[0]
    drive[0] = d_ref[0] * act_ref[0].astype(F32)
    gate_block = gate_ref[0]
    up[0] = dg_ref[0] * (gate_block * jax.nn.sigmoid(gate_block))
    sum_acc[...] = jnp.zeros_like(sum_acc)

    def rows_of(i):
        return pl.ds(pl.multiple_of(i * CHUNK, CHUNK), CHUNK)

    def kept(i, r):
        return pl.ds(pl.multiple_of((i * CHUNK + r) * states, states), states)

    def sum_y(i, low, part):
        at, rows = slice(part * span, (part + 1) * span), rows_of(i)
        produced = jnp.dot(c_diag[0, i], low[:, at], preferred_element_type=F32)
        scanned = produced + skip_ref[:, at] * act_ref[0, rows, at].astype(F32)
        gate = gate_ref[0, rows, at]
        sigmoid = jax.nn.sigmoid(gate)
        gated = (scanned * (gate * sigmoid)).astype(BF16)
        slope = sigmoid * (1.0 + gate * (1.0 - sigmoid))
        d_gate = (dg_ref[0, rows, at] * scanned * slope).astype(BF16)
        gated_ref[0, rows, at] = gated
        dgate_ref[0, rows, at] = d_gate
        gated_out[slot, rows, at] = gated
        if hosted:
            gate_out[slot, rows, at] = d_gate

    def forward(i, h, low, before, low_before):
        rows = rows_of(i)
        waiting = list(range(parts))
        for r in range(CHUNK):
            b = b_ref[0, i * CHUNK + r]
            for j in range(tiles):
                decay = jnp.exp2(spread_row(d_ref, rows, r, j, states) * rate[j])
                h[j] = h[j] * decay + spread_row(drive, rows, r, j, states) * b
                history[kept(i, r + 1), column(j)] = h[j]
                low[r * states : (r + 1) * states, column(j)] = h[j].astype(BF16)
            if waiting and r % max(1, CHUNK // parts) == 1:
                sum_y(before, low_before, waiting.pop(0))
        for part in waiting:
            sum_y(before, low_before, part)
        return h

    def forward_pair(pair, carry):
        h = forward(2 * pair, list(carry), low_a, jnp.maximum(2 * pair - 1, 0), low_b)
        return tuple(forward(2 * pair + 1, h, low_b, 2 * pair, low_a))

    lax.fori_loop(0, chunks // 2, forward_pair, tuple(start_ref[0, :, column(j)] for j in range(tiles)))
    for part in range(parts):
        sum_y(chunks - 1, low_b, part)
    send(seg, block, slot)

    @pl.when(pl.program_id(1) == 0)
    def _():
        db_acc[...] = jnp.zeros_like(db_acc)
        dc_acc[...] = jnp.zeros_like(dc_acc)

    def sum_back(i, low, through, part, count=None):
        at, rows = slice(part * span, (part + 1) * span), rows_of(i)
        d_drive = jnp.dot(b_diag[0, i], low[:, at], preferred_element_type=F32)
        d_rate = jnp.dot(ones_ref[...], through[:, at], preferred_element_type=F32)
        delta, act, d_scanned = d_ref[0, rows, at], act_ref[0, rows, at].astype(F32), up[0, rows, at]
        near = delta * (1.0 - delta * (0.5 - delta * (1.0 / 6.0 - delta * (1.0 / 24.0))))
        slope = jnp.where(delta < 0.03, near, 1.0 - jnp.exp(-delta))
        d_pre = (LN2 * d_rate + d_drive * act) * slope
        dpre_ref[0, rows, at] = d_pre.astype(BF16)
        dact_ref[0, rows, at] = skip_ref[:, at] * d_scanned + d_drive * delta
        if count is None:
            sum_acc[0, :, at] += d_pre
            sum_acc[1, :, at] += d_scanned * act
        else:
            sum_acc[0, :, at] += jnp.where(count, d_pre, 0.0)
            sum_acc[1, :, at] += jnp.where(count, d_scanned * act, 0.0)

    def backward(i, lam, da, low, through, before, low_before, through_before, count=None):
        rows = rows_of(i)
        waiting = list(range(parts))
        for r in reversed(range(CHUNK)):
            c = c_ref[0, i * CHUNK + r]
            db = dc = None
            for j in range(tiles):
                step = spread_row(d_ref, rows, r, j, states)
                upstream = spread_row(up, rows, r, j, states)
                adjoint = lam[j] + upstream * c
                db_j = adjoint * spread_row(drive, rows, r, j, states)
                dc_j = upstream * history[kept(i, r + 1), column(j)]
                db, dc = (db_j, dc_j) if db is None else (db + db_j, dc + dc_j)
                low[r * states : (r + 1) * states, column(j)] = adjoint.astype(BF16)
                lam[j] = adjoint * jnp.exp2(step * rate[j])
                flow = lam[j] * history[kept(i, r), column(j)]
                through[r * states : (r + 1) * states, column(j)] = (flow * rate[j]).astype(BF16)
                da[j] = da[j] + flow * step
            db_acc[i * CHUNK + r] += db
            dc_acc[i * CHUNK + r] += dc
            if waiting and (CHUNK - 1 - r) % max(1, CHUNK // parts) == 1:
                sum_back(before, low_before, through_before, waiting.pop(0), count)
        for part in waiting:
            sum_back(before, low_before, through_before, part, count)
        return lam, da

    def backward_pair(pair, carry):
        lam, da = (list(part) for part in carry)
        i = chunks - 1 - 2 * pair
        lam, da = backward(i, lam, da, low_a, through_a, jnp.minimum(i + 1, chunks - 1), low_b, through_b, pair > 0)
        lam, da = backward(i - 1, lam, da, low_b, through_b, i, low_a, through_a)
        return tuple(lam), tuple(da)

    zeros = tuple(jnp.zeros((states, LANES), F32) for _ in range(tiles))
    _, da = lax.fori_loop(
        0, chunks // 2, backward_pair, (tuple(end_ref[0, :, column(j)] for j in range(tiles)), zeros)
    )
    for part in range(parts):
        sum_back(0, low_b, through_b, part)
    for j in range(tiles):
        da_ref[0, :, column(j)] = da[j]
    sums_ref[0, 0:1, :] = jnp.sum(sum_acc[0], axis=0, keepdims=True)
    sums_ref[0, 1:2, :] = jnp.sum(sum_acc[1], axis=0, keepdims=True)
    sums_ref[0, 2:8, :] = jnp.zeros((6, width), F32)

    @pl.when(pl.program_id(1) == pl.num_programs(1) - 1)
    def _():
        db_ref[0] = jnp.sum(db_acc[...], axis=-1)
        dc_ref[0] = jnp.sum(dc_acc[...], axis=-1)

    @pl.when(tick == pl.num_programs(0) * n_blocks - 1)
    def _():
        drain((tick - 1) // n_blocks, lax.rem(tick - 1, n_blocks), 1 - slot)
        drain(seg, block, slot)
        for p in range(1, n_dp):
            source = lax.rem(my_dp + p, n_dp)
            pltpu.make_async_remote_copy(
                src_ref=gated_all.at[source], dst_ref=gated_all.at[source],
                send_sem=gated_sent.at[0, 0], recv_sem=gated_got.at[source],
                device_id={"dp": source}, device_id_type=MESH,
            ).wait_recv()

        @pl.when(my_seq != n_seq - 1)
        def _():
            first_far.wait_send()

        for p in range(1, n_seq if hosted else 1):
            source = lax.rem(my_seq + p, n_seq)
            pltpu.make_async_remote_copy(
                src_ref=gate_all.at[source], dst_ref=gate_all.at[source],
                send_sem=gate_sent.at[0, 0], recv_sem=gate_got.at[source],
                device_id={"seq": source}, device_id_type=MESH,
            ).wait_recv()


def scan_both(delta, act, gate_in, d_gated, b_wide, c_wide, c_diag, b_diag, ones_diag, a_mat, d_skip, start, end, first):
    segs, length, inner = delta.shape
    states = a_mat.shape[0]
    width = widest(inner, 768)
    tokens = pl.BlockSpec((1, length, width), lambda s, e: (s, 0, e))
    wide = pl.BlockSpec((1, length, states, LANES), lambda s, e: (s, 0, 0, 0))
    diag = pl.BlockSpec((1,) + c_diag.shape[1:], lambda s, e: (s, 0, 0, 0))
    state = pl.BlockSpec((1, states, width), lambda s, e: (s, 0, e))
    narrow = pl.BlockSpec((1, length, states), lambda s, e: (s, 0, 0))
    by_token = jax.ShapeDtypeStruct((segs, length, inner), F32)
    by_token_low = jax.ShapeDtypeStruct((segs, length, inner), BF16)
    by_state = jax.ShapeDtypeStruct((segs, length, states), F32)
    low = pltpu.VMEM((CHUNK * states, width), BF16)
    lanes = pltpu.VMEM((length, states, LANES), F32)
    n_dp, n_seq = lax.axis_size("dp"), lax.axis_size("seq")
    channels = inner // n_seq
    hosted = aligned(inner)
    dma = pltpu.SemaphoreType.DMA
    out = pltpu.VMEM((2, length, width), BF16)
    return pl.pallas_call(
        functools.partial(scan_kernel, hosted, inner // width),
        grid=(segs, inner // width),
        in_specs=[
            tokens, tokens, tokens, tokens, wide, wide, diag, diag,
            pl.BlockSpec(ones_diag.shape, lambda s, e: (0, 0)),
            pl.BlockSpec((states, width), lambda s, e: (0, e)),
            pl.BlockSpec((1, width), lambda s, e: (0, e)),
            state, state,
            pl.BlockSpec(memory_space=pl.ANY),
        ],
        out_specs=[
            tokens, tokens, tokens, tokens, narrow, narrow, state,
            pl.BlockSpec((1, 8, width), lambda s, e: (s, 0, e)),
            pl.BlockSpec(memory_space=pl.ANY),
            pl.BlockSpec(memory_space=pl.ANY),
            pl.BlockSpec(memory_space=pl.ANY),
        ],
        out_shape=[
            by_token_low, by_token_low, by_token_low, by_token, by_state, by_state,
            jax.ShapeDtypeStruct((segs, states, inner), F32),
            jax.ShapeDtypeStruct((segs, 8, inner), F32),
            jax.ShapeDtypeStruct((n_dp, segs, length, inner), BF16),
            jax.ShapeDtypeStruct((n_seq, segs, length, channels), BF16),
            jax.ShapeDtypeStruct(first.shape, F32),
        ],
        scratch_shapes=[
            pltpu.VMEM(((length + 1) * states, width), F32),
            pltpu.VMEM((1, length, width), F32),
            pltpu.VMEM((1, length, width), F32),
            low, low, low, low, lanes, lanes,
            pltpu.VMEM((2, CHUNK, width), F32),
            out, out,
            dma((2, n_dp)), dma((n_dp,)), dma((2, n_seq)), dma((n_seq,)), dma((2, 1 + n_seq)),
            dma((1,)), dma((1,)),
        ],
        compiler_params=pltpu.CompilerParams(
            collective_id=2, has_side_effects=True, vmem_limit_bytes=VMEM_BYTES
        ),
        cost_estimate=pl.CostEstimate(
            flops=20 * delta.size * states, bytes_accessed=24 * delta.size, transcendentals=2 * delta.size * states
        ),
        name="scan_both",
    )(delta, act, gate_in, d_gated, b_wide, c_wide, c_diag, b_diag, ones_diag, a_mat, d_skip[None], start, end, first)


def finish_kernel(
    gain_at, conv_hbm, gate_hbm, columns_hbm, normed_hbm, proj_hbm, tokens_hbm, cot_hbm, small_hbm, halo_hbm, gain_ref,
    d_tokens, d_in, small_out, halo_out,
    conv, gate, gate_columns, conv_columns, normed, proj, tokens, cot, small, d_normed,
    partial, arrived, placed, small_low, small_dp, small_mid, small_seq,
    load, normed_load, proj_load, swap_sent, swap_got, swap_own, add_sent, add_got, put_sent, put_got, put_own,
    copy_sent, copy_got, mid_sent, mid_got, far_sent, far_got, last_sent, last_got, halo_sent, halo_got,
):
    n_dp, n_seq = lax.axis_size("dp"), lax.axis_size("seq")
    my_dp, my_seq = lax.axis_index("dp"), lax.axis_index("seq")
    half = n_seq // 2
    count, inner = conv_hbm.shape
    width = tokens.shape[1]
    channels = inner // n_seq
    chunks = channels // LANES
    rows_dp = width // n_dp
    rows_small = small_low.shape[0] // n_dp
    dp_peers = [lax.rem(my_dp + p, n_dp) for p in range(n_dp)]
    seq_peers = [lax.rem(my_seq + p, n_seq) for p in range(n_seq)]

    def remote(src, dst, sent, got, **to):
        return pltpu.make_async_remote_copy(
            src_ref=src, dst_ref=dst, send_sem=sent, recv_sem=got, device_id=to, device_id_type=MESH
        )

    loads = [
        pltpu.make_async_copy(src, dst, load.at[k])
        for k, (src, dst) in enumerate(
            [(columns_hbm, gate_columns), (conv_hbm, conv), (gate_hbm, gate), (tokens_hbm, tokens), (cot_hbm, cot),
             (small_hbm, small_low)]
        )
    ]
    load_columns, load_conv, load_gate, load_tokens, load_cot, load_small = loads
    load_normed = [pltpu.make_async_copy(normed_hbm.at[s], normed.at[s], normed_load.at[s]) for s in range(n_seq)]
    depth = proj.shape[2]

    def load_proj(k):
        return pltpu.make_async_copy(proj_hbm.at[:, k * depth : (k + 1) * depth], proj.at[k % 2], proj_load.at[k % 2])

    load_columns.start()
    for copy in load_normed:
        copy.start()
    load_conv.start()
    load_proj(0).start()
    for copy in (load_gate, load_tokens, load_cot, load_small):
        copy.start()

    barrier = pltpu.get_barrier_semaphore()
    for p in range(1, n_dp):
        pl.semaphore_signal(barrier, inc=1, device_id={"dp": dp_peers[p]}, device_id_type=MESH)
    for p in range(1, n_seq):
        pl.semaphore_signal(barrier, inc=1, device_id={"seq": seq_peers[p]}, device_id_type=MESH)
    pl.semaphore_wait(barrier, n_dp + n_seq - 2)

    def column_of(device, c):
        return pl.ds(pl.multiple_of(device * channels + c * LANES, LANES), LANES)

    def swap(c, p):
        return remote(
            conv_hbm.at[:, column_of(seq_peers[p], c)], conv_columns.at[c, my_seq],
            swap_sent.at[c, p], swap_got.at[c, my_seq], seq=seq_peers[p],
        )

    own_swaps = [
        pltpu.make_async_copy(conv_hbm.at[:, column_of(my_seq, c)], conv_columns.at[c, my_seq], swap_own.at[c])
        for c in range(chunks)
    ]
    for c in range(chunks):
        own_swaps[c].start()
        for p in range(1, n_seq):
            swap(c, p).start()

    def halo(p):
        return remote(halo_hbm, halo_out, halo_sent.at[p], halo_got.at[0], seq=p)

    halo_own = pltpu.make_async_copy(halo_hbm, halo_out, halo_got.at[0])

    @pl.when(my_seq == 0)
    def _():
        halo_own.start()
        for p in range(1, n_seq):
            halo(p).start()

    def product(c, columns):
        tile = 768 if width % 768 == 0 else 256

        def some_rows(r, nothing):
            at = pl.ds(pl.multiple_of(r * tile, tile), tile)
            total = jnp.dot(normed[0, at, :], columns(0), preferred_element_type=F32)
            for s in range(1, n_seq):
                total += jnp.dot(normed[s, at, :], columns(s), preferred_element_type=F32)
            partial[c, at, :] = total.astype(BF16)
            return nothing

        lax.fori_loop(0, width // tile, some_rows, 0)

    def rows_of(device):
        return pl.ds(pl.multiple_of(device * rows_dp, 16), rows_dp)

    def add(c, p):
        return remote(
            partial.at[c, rows_of(dp_peers[p])], arrived.at[c, my_dp], add_sent.at[c, p], add_got.at[c, my_dp],
            dp=dp_peers[p],
        )

    def scatter(c):
        for p in range(1, n_dp):
            add(c, p).start()

    def place(c):
        k, is_gate = c % chunks, c < chunks
        keeper = my_seq // 2 + (half if is_gate else 0)
        side = lax.rem(my_seq, 2)
        at = (rows_of(my_dp), pl.ds(pl.multiple_of(side * channels + k * LANES, LANES), LANES))
        own = pltpu.make_async_copy(placed.at[c], d_in.at[at], put_own.at[c])
        far = remote(placed.at[c], d_in.at[at], put_sent.at[c], put_got.at[k, side], seq=keeper)
        return keeper, own, far

    def gather_add(c):
        total = partial[c, rows_of(my_dp), :].astype(F32)
        for p in range(1, n_dp):
            remote(
                partial.at[c, rows_of(my_dp)], arrived.at[c, dp_peers[p]], add_sent.at[c, p],
                add_got.at[c, dp_peers[p]], dp=dp_peers[p],
            ).wait_recv()
            total += arrived[c, dp_peers[p]].astype(F32)
        placed[c] = total.astype(BF16)
        keeper, own, far = place(c)
        pl.when(keeper == my_seq)(own.start)
        pl.when(keeper != my_seq)(far.start)

    def spread(k, side, p):
        at = (rows_of(my_dp), slice(side * channels + k * LANES, side * channels + (k + 1) * LANES))
        return remote(
            d_in.at[at], d_in.at[at], copy_sent.at[k, side, p], copy_got.at[k, side, my_dp], dp=dp_peers[p]
        )

    def pass_on(c):
        k, is_gate = c % chunks, c < chunks

        @pl.when((my_seq >= half) == is_gate)
        def _():
            for side in range(2):
                source = 2 * lax.rem(my_seq, half) + side
                at = (rows_of(my_dp), slice(side * channels + k * LANES, side * channels + (k + 1) * LANES))

                @pl.when(source == my_seq)
                def _():
                    place(c)[1].wait()

                @pl.when(source != my_seq)
                def _():
                    remote(placed.at[c], d_in.at[at], put_sent.at[c], put_got.at[k, side], seq=source).wait_recv()

                for p in range(1, n_dp):
                    spread(k, side, p).start()

    load_columns.wait()
    for copy in load_normed:
        copy.wait()
    for c in range(chunks):
        product(c, lambda s, c=c: gate_columns[s, :, c * LANES : (c + 1) * LANES])
        scatter(c)

    load_conv.wait()
    load_gate.wait()
    steps = 2 * inner // depth
    for k in range(steps):
        if k + 1 < steps:
            load_proj(k + 1).start()
        load_proj(k).wait()
        source, at = (conv, k * depth) if k * depth < inner else (gate, k * depth - inner)

        def some_columns(n, nothing, k=k, source=source, at=at):
            cols = pl.ds(pl.multiple_of(n * 256, 256), 256)
            term = lax.dot_general(
                source[:, at : at + depth], proj[k % 2, cols, :], (((1,), (1,)), ((), ())), preferred_element_type=F32
            )
            d_normed[:, cols] = term if k == 0 else d_normed[:, cols] + term
            return nothing

        lax.fori_loop(0, width // 256, some_columns, 0)
        if k == steps // 2:
            for c in range(chunks):
                gather_add(c)

    load_tokens.wait()
    load_cot.wait()
    gain = gain_ref[...]

    def some_tokens(r, total):
        at = pl.ds(pl.multiple_of(r * 32, 32), 32)
        token = tokens[at, :].astype(F32)
        inverse = lax.rsqrt(jnp.mean(token * token, axis=-1, keepdims=True) + EPS)
        scaled = d_normed[at, :] * gain
        mean = jnp.mean(scaled * token, axis=-1, keepdims=True)
        d_tokens[at, :] = cot[at, :].astype(F32) + inverse * scaled - token * (inverse * inverse * inverse * mean)
        return total + jnp.sum(d_normed[at, :] * token * inverse, axis=0, keepdims=True)

    d_gain = lax.fori_loop(0, count // 32, some_tokens, jnp.zeros((1, width), F32))
    load_small.wait()
    first = gain_at // 16 * 16
    small[...] = small_low[first : first + 16, :].astype(F32)
    for row in range(width // channels):
        for s in range(n_seq):
            at = gain_at - first + row
            small[at : at + 1, s * channels : (s + 1) * channels] = d_gain[:, row * channels : (row + 1) * channels]
    small_low[first : first + 16, :] = small[...].astype(BF16)

    def small_rows(device):
        return pl.ds(pl.multiple_of(device * rows_small, 16), rows_small)

    def small_add(p):
        return remote(
            small_low.at[small_rows(dp_peers[p])], small_dp.at[my_dp], mid_sent.at[p], mid_got.at[my_dp], dp=dp_peers[p]
        )

    for p in range(1, n_dp):
        small_add(p).start()
    for c in range(chunks):
        pass_on(c)

    total = small_low[small_rows(my_dp), :].astype(F32)
    for p in range(1, n_dp):
        remote(
            small_low.at[small_rows(my_dp)], small_dp.at[dp_peers[p]], mid_sent.at[p], mid_got.at[dp_peers[p]],
            dp=dp_peers[p],
        ).wait_recv()
        total += small_dp[dp_peers[p]].astype(F32)
    small_mid[...] = total.astype(BF16)

    def small_swap(p):
        at = pl.ds(pl.multiple_of(seq_peers[p] * channels, LANES), channels)
        return remote(
            small_mid.at[:, at], small_seq.at[my_seq], far_sent.at[p], far_got.at[my_seq], seq=seq_peers[p]
        )

    for p in range(1, n_seq):
        small_swap(p).start()

    def convolved(c):
        own_swaps[c].wait()
        for p in range(1, n_seq):
            remote(
                conv_hbm.at[:, column_of(my_seq, c)], conv_columns.at[c, seq_peers[p]], swap_sent.at[c, p],
                swap_got.at[c, seq_peers[p]], seq=seq_peers[p],
            ).wait_recv()
        product(chunks + c, lambda s: conv_columns[c, s])
        scatter(chunks + c)

    convolved(0)
    total = small_mid[:, pl.ds(pl.multiple_of(my_seq * channels, LANES), channels)].astype(F32)
    for p in range(1, n_seq):
        remote(
            small_mid.at[:, 0:channels], small_seq.at[seq_peers[p]], far_sent.at[p], far_got.at[seq_peers[p]],
            seq=seq_peers[p],
        ).wait_recv()
        total += small_seq[seq_peers[p]].astype(F32)
    small_out[small_rows(my_dp), :] = total.astype(BF16)

    def small_spread(p):
        at = small_rows(my_dp)
        return remote(small_out.at[at], small_out.at[at], last_sent.at[p], last_got.at[my_dp], dp=dp_peers[p])

    for p in range(1, n_dp):
        small_spread(p).start()

    for c in range(1, chunks):
        convolved(c)
        gather_add(chunks + c - 1)
        if c >= 2:
            pass_on(chunks + c - 2)
    gather_add(2 * chunks - 1)
    if chunks >= 2:
        pass_on(2 * chunks - 2)
    pass_on(2 * chunks - 1)

    for c in range(chunks):
        for p in range(1, n_seq):
            swap(c, p).wait_send()
    for c in range(2 * chunks):
        for p in range(1, n_dp):
            add(c, p).wait_send()
        keeper, own, far = place(c)

        @pl.when(keeper != my_seq)
        def _(far=far):
            far.wait_send()

    for k in range(chunks):
        for side in range(2):
            at = slice(side * channels + k * LANES, side * channels + (k + 1) * LANES)
            for p in range(1, n_dp):
                spread(k, side, p).wait_send()
                peer = dp_peers[p]
                remote(
                    d_in.at[rows_of(peer), at], d_in.at[rows_of(peer), at], copy_sent.at[k, side, p],
                    copy_got.at[k, side, peer], dp=peer,
                ).wait_recv()
    for p in range(1, n_dp):
        small_add(p).wait_send()
        small_spread(p).wait_send()
        peer = dp_peers[p]
        remote(
            small_out.at[small_rows(peer)], small_out.at[small_rows(peer)], last_sent.at[p], last_got.at[peer], dp=peer
        ).wait_recv()
    for p in range(1, n_seq):
        small_swap(p).wait_send()

    @pl.when(my_seq == 0)
    def _():
        halo_own.wait()
        for p in range(1, n_seq):
            halo(p).wait_send()

    @pl.when(my_seq != 0)
    def _():
        halo(1).wait_recv()


def finish(d_conv_in, d_gate, gate_columns, normed_all, in_proj, tokens, cot, small, gain_at, halo_grad, norm_gain):
    n_dp, n_seq = lax.axis_size("dp"), lax.axis_size("seq")
    count, inner = d_conv_in.shape
    width = tokens.shape[1]
    channels = inner // n_seq
    chunks = channels // LANES
    rows = small.shape[0]
    depth = 1024 if inner % 1024 == 0 else LANES
    dma = pltpu.SemaphoreType.DMA
    vmem = pltpu.VMEM
    anywhere = pl.BlockSpec(memory_space=pl.ANY)
    inside = pl.BlockSpec(memory_space=pltpu.VMEM)
    return pl.pallas_call(
        functools.partial(finish_kernel, gain_at),
        in_specs=[anywhere] * 9 + [inside],
        out_specs=[inside, anywhere, inside, anywhere],
        out_shape=[
            jax.ShapeDtypeStruct((count, width), F32),
            jax.ShapeDtypeStruct((width, 2 * channels), BF16),
            jax.ShapeDtypeStruct((rows, channels), BF16),
            jax.ShapeDtypeStruct(halo_grad.shape, F32),
        ],
        scratch_shapes=[
            vmem((count, inner), BF16), vmem((count, inner), BF16),
            vmem((n_seq, count, channels), BF16), vmem((chunks, n_seq, count, LANES), BF16),
            vmem((n_seq, width, count), BF16), vmem((2, width, depth), BF16),
            vmem((count, width), BF16), vmem((count, width), BF16), vmem((16, inner), F32),
            vmem((count, width), F32),
            vmem((2 * chunks, width, LANES), BF16), vmem((2 * chunks, n_dp, width // n_dp, LANES), BF16),
            vmem((2 * chunks, width // n_dp, LANES), BF16),
            vmem((rows, inner), BF16), vmem((n_dp, rows // n_dp, inner), BF16), vmem((rows // n_dp, inner), BF16),
            vmem((n_seq, rows // n_dp, channels), BF16),
            dma((6,)), dma((n_seq,)), dma((2,)),
            dma((chunks, n_seq)), dma((chunks, n_seq)), dma((chunks,)),
            dma((2 * chunks, n_dp)), dma((2 * chunks, n_dp)),
            dma((2 * chunks,)), dma((chunks, 2)), dma((2 * chunks,)),
            dma((chunks, 2, n_dp)), dma((chunks, 2, n_dp)),
            dma((n_dp,)), dma((n_dp,)), dma((n_seq,)), dma((n_seq,)), dma((n_dp,)), dma((n_dp,)),
            dma((n_seq,)), dma((1,)),
        ],
        compiler_params=pltpu.CompilerParams(
            collective_id=3, has_side_effects=True, vmem_limit_bytes=60 * 2**20
        ),
        cost_estimate=pl.CostEstimate(
            flops=12 * count * width * inner, bytes_accessed=40 * count * width, transcendentals=0
        ),
        name="finish",
    )(
        d_conv_in, d_gate, gate_columns, normed_all, in_proj, tokens, cot, small, halo_grad, norm_gain[None],
    )


def diagonal_blocks(value):
    segs, length, states = value.shape
    spread = jnp.tile(jnp.eye(states, dtype=BF16), (1, CHUNK))
    tiled = matmul(value.reshape(segs * length, states).astype(BF16), spread)
    mask = jnp.repeat(jnp.eye(CHUNK, dtype=F32), states, axis=1)
    return (tiled.reshape(segs, length // CHUNK, CHUNK, CHUNK * states) * mask).astype(BF16)


def norm_kernel(token_ref, gain_ref, normed_ref, turned_ref):
    token = token_ref[...].astype(F32)
    inverse = lax.rsqrt(jnp.mean(token * token, axis=-1, keepdims=True) + EPS)
    normed = token * inverse * gain_ref[...]
    normed_ref[...] = normed.astype(BF16)
    turned_ref[...] = normed.T.astype(BF16)


def norm(tokens, norm_gain):
    count, width = tokens.shape
    rows = 128
    return pl.pallas_call(
        norm_kernel,
        grid=(count // rows,),
        in_specs=[pl.BlockSpec((rows, width), lambda r: (r, 0)), pl.BlockSpec((1, width), lambda r: (0, 0))],
        out_specs=[pl.BlockSpec((rows, width), lambda r: (r, 0)), pl.BlockSpec((width, rows), lambda r: (0, r))],
        out_shape=[jax.ShapeDtypeStruct((count, width), BF16), jax.ShapeDtypeStruct((width, count), BF16)],
        compiler_params=pltpu.CompilerParams(vmem_limit_bytes=32 * 2**20),
        name="norm",
    )(tokens, norm_gain[None])


def body(
    tokens, conv_state, entry_state, norm_gain, in_proj, conv_weight, conv_bias, x_proj,
    dt_proj, dt_bias, a_log, d_skip, out_proj, cotangent,
):
    segs, length, width = tokens.shape
    inner = in_proj.shape[1] // 2
    rank, states, taps = dt_proj.shape[0], a_log.shape[0], conv_weight.shape[0]
    halo = taps - 1
    count = segs * length
    n_seq = lax.axis_size("seq")
    mine = lax.axis_index("seq")
    is_first = mine == 0

    def flat(value):
        return value.reshape((count,) + value.shape[2:])

    def split(value):
        return value.reshape((segs, length) + value.shape[1:])

    token_float = flat(tokens).astype(F32)
    inverse = lax.rsqrt(jnp.mean(token_float * token_float, axis=-1, keepdims=True) + EPS)
    normed, normed_turned = norm(flat(tokens), norm_gain)
    cot = flat(cotangent)
    fast = aligned(inner)
    if fast:
        normed_all = lax.all_gather(normed_turned, "seq", axis=0, tiled=False)
    else:
        normed_all = lax.all_gather(normed, "seq", axis=0, tiled=True)
    cot_rows = swap_rows(cot.T, "dp")
    conv_in = matmul(normed, in_proj[:, :inner]).astype(BF16)
    gate_in = matmul(normed, in_proj[:, inner:])
    d_gated = matmul_nt(cot, out_proj)
    conv_in = split(conv_in)
    before = jnp.where(is_first, conv_state, shifted(conv_in[:, length - halo :], "seq", 1))
    padded = jnp.concatenate([before, conv_in], axis=1).astype(F32)
    conv_out = conv_bias + sum(conv_weight[tap] * padded[:, tap : tap + length] for tap in range(taps))
    activated = (conv_out * jax.nn.sigmoid(conv_out)).astype(BF16)
    coeffs = matmul(flat(activated), x_proj)
    dt_low = coeffs[:, :rank].astype(BF16)
    b_in = split(coeffs[:, rank : rank + states])
    c_in = split(coeffs[:, rank + states :])
    pre_delta = matmul(dt_low, dt_proj) + dt_bias
    delta = split(jax.nn.softplus(pre_delta))
    a_mat = -jnp.exp(a_log)
    gate_in, d_gated = split(gate_in), split(d_gated)

    b_wide = jnp.broadcast_to(b_in[..., None], b_in.shape + (LANES,))
    c_wide = jnp.broadcast_to(c_in[..., None], c_in.shape + (LANES,))
    ends, entry_mu = block_ends(delta, activated, gate_in, d_gated, b_wide, c_wide, a_mat)
    total = jnp.sum(delta, axis=1, keepdims=True)
    start, end, first = carry(ends, entry_mu, total, entry_state, a_mat)
    start, normed_all = lax.optimization_barrier((start, normed_all))
    ones_diag = diagonal_blocks(jnp.ones((1, CHUNK, states), F32))[0, 0]
    gated, d_gate, d_pre_low, d_act, d_b, d_c, d_amat, sums, gated_all, gate_columns, d_entry = scan_both(
        delta, activated, gate_in, d_gated, b_wide, c_wide,
        diagonal_blocks(c_in), diagonal_blocks(b_in), ones_diag, a_mat, d_skip, start, end, first,
    )
    gated, d_gate, d_pre_low, d_act = flat(gated), flat(d_gate), flat(d_pre_low), flat(d_act)
    gated_all = gated_all.reshape(-1, inner)
    gate_columns = gate_columns.reshape(n_seq * count, -1)
    if (inner // n_seq) % LANES:
        gate_columns = swap_columns(d_gate, "seq")
    output = token_float + matmul(gated, out_proj)
    out_part = matmul(cot_rows, gated_all).astype(BF16)
    out_part = lax.psum_scatter(out_part, "seq", scatter_dimension=1, tiled=True)
    d_out_proj = lax.all_gather(out_part, "dp", axis=0, tiled=True).T.astype(F32)

    sums = jnp.sum(sums, axis=0)
    d_dt_bias, d_d_skip = sums[0], sums[1]
    d_dt_proj = matmul_tn(dt_low, d_pre_low)
    d_dt_low = matmul_nt(d_pre_low, dt_proj)
    d_coeffs = jnp.concatenate([d_dt_low, flat(d_b), flat(d_c)], axis=-1).astype(BF16)
    d_x_proj = matmul_tn(d_coeffs, flat(activated))
    d_a_log = jnp.sum(d_amat, axis=0) * a_mat
    d_act = split(d_act + matmul_nt(d_coeffs, x_proj))
    conv_sigmoid = jax.nn.sigmoid(conv_out)
    d_conv_out = d_act * (conv_sigmoid * (1.0 + conv_out * (1.0 - conv_sigmoid)))
    d_conv_bias = jnp.sum(d_conv_out, axis=(0, 1))
    d_conv_weight = jnp.stack(
        [jnp.sum(d_conv_out * padded[:, tap : tap + length], axis=(0, 1)) for tap in range(taps)]
    )
    halo_grad = sum(
        conv_weight[tap] * jnp.pad(d_conv_out[:, : halo - tap], ((0, 0), (tap, 0), (0, 0))) for tap in range(halo)
    )
    returned = shifted(halo_grad, "seq", -1)
    tail = jnp.pad(d_conv_out, ((0, 0), (0, halo), (0, 0)))
    d_conv_in = sum(conv_weight[tap] * tail[:, halo - tap : halo - tap + length] for tap in range(taps))
    d_conv_in = d_conv_in + jnp.pad(returned, ((0, 0), (length - halo, 0), (0, 0)))
    d_conv_in = flat(d_conv_in).astype(BF16)
    if fast:
        small = jnp.concatenate(
            [
                part.astype(BF16)
                for part in (
                    d_x_proj, d_dt_proj, d_a_log, d_dt_bias[None], d_d_skip[None], d_conv_weight, d_conv_bias[None]
                )
            ],
            axis=0,
        )
        edge_at = 2 * rank + 3 * states + 2
        channels = inner // n_seq
        gain_rows = width // channels
        gain_at = small.shape[0]
        if gain_at % 16 + gain_rows > 16:
            gain_at += -gain_at % 16
        rows = gain_at + gain_rows
        rows += -rows % (16 * lax.axis_size("dp"))
        small = jnp.pad(small, ((0, rows - small.shape[0]), (0, 0)))
        d_tokens, d_in_proj, small, d_conv_state = finish(
            d_conv_in, d_gate, gate_columns.reshape(n_seq, count, channels), normed_all, in_proj, flat(tokens), cot,
            small, gain_at, halo_grad, norm_gain,
        )
        d_in_proj, small = d_in_proj.astype(F32), small.astype(F32)
        edges = small[edge_at:gain_at]
        d_norm_gain = small[gain_at : gain_at + gain_rows].reshape(n_seq, -1)
        d_norm_gain = lax.dynamic_index_in_dim(d_norm_gain, mine, 0, keepdims=False)
    else:
        d_conv_state = from_first(halo_grad, "seq")

        n_dp = lax.axis_size("dp")
        small = jnp.concatenate([d_x_proj, d_dt_proj, d_a_log, d_dt_bias[None], d_d_skip[None]], axis=0)
        small = jnp.pad(small, ((0, -small.shape[0] % 16), (0, 0))).astype(BF16)
        small_columns = swap_columns(small, "seq")
        edges = jnp.concatenate([d_conv_weight, d_conv_bias[None]], axis=0)
        edges = jnp.pad(edges, ((0, -edges.shape[0] % 16), (0, 0))).astype(BF16)
        conv_columns = swap_columns(jnp.concatenate([d_conv_in, edges], axis=0), "seq").reshape(n_seq, -1, inner // n_seq)
        edge_columns = conv_columns[:, count:]
        conv_columns = conv_columns[:, :count].reshape(n_seq * count, -1)

        def blocks(value, axis):
            return value.reshape((lax.axis_size(axis), -1) + value.shape[1:])

        gate_part = sum_scatter(blocks(matmul_tn(normed_all, gate_columns), "dp"), "dp").astype(BF16)
        conv_part = sum_scatter(blocks(matmul_tn(normed_all, conv_columns), "dp"), "dp").astype(BF16)
        half = n_seq // 2
        even = mine % 2 == 0
        straight = [(i, i // 2 + (0 if i % 2 == 0 else half)) for i in range(n_seq)]
        crossed = [(i, i // 2 + (half if i % 2 == 0 else 0)) for i in range(n_seq)]
        first = lax.ppermute(jnp.where(even, conv_part, gate_part), "seq", straight)
        second = lax.ppermute(jnp.where(even, gate_part, conv_part), "seq", crossed)
        low_half = mine < half
        d_in_part = jnp.concatenate(
            [jnp.where(low_half, first, second), jnp.where(low_half, second, first)], axis=1
        )
        d_in_proj = gather_rows(d_in_part, "dp").astype(F32)

        d_normed = matmul_nt(d_conv_in, in_proj[:, :inner]) + matmul_nt(d_gate, in_proj[:, inner:])
        d_norm_gain = jnp.sum(d_normed * token_float * inverse, axis=0)
        scaled = d_normed * norm_gain
        cubed = inverse * inverse * inverse
        d_tokens = (
            cot.astype(F32)
            + inverse * scaled
            - token_float * cubed * jnp.mean(scaled * token_float, axis=-1, keepdims=True)
        )
        gain = sum_scatter(blocks(d_norm_gain, "seq"), "seq")
        channels = inner // n_seq
        per_device = jnp.concatenate(
            [
                jnp.sum(small_columns.reshape(n_seq, -1, channels).astype(F32), axis=0),
                jnp.sum(edge_columns.astype(F32), axis=0),
                jnp.pad(gain, (0, -gain.shape[0] % channels)).reshape(-1, channels),
            ],
            axis=0,
        )
        per_device = per_device.astype(BF16)
        summed = jnp.sum(gather_rows(per_device[None], "dp").astype(F32), axis=0)
        edges = summed[small.shape[0] : small.shape[0] + edges.shape[0]]
        d_norm_gain = summed[small.shape[0] + edges.shape[0] :].reshape(-1)[: gain.shape[0]]
        small = summed

    return (
        split(output),
        split(d_tokens),
        d_conv_state,
        d_entry,
        d_norm_gain,
        d_in_proj,
        edges[:taps],
        edges[taps],
        small[: rank + 2 * states].T,
        small[rank + 2 * states : 2 * rank + 2 * states],
        small[2 * rank + 3 * states],
        small[2 * rank + 2 * states : 2 * rank + 3 * states],
        small[2 * rank + 3 * states + 1],
        d_out_proj,
    )


def solution(mesh):
    by_token, by_segment, whole = P("dp", "seq", None), P("dp", None, None), P()
    return jax.shard_map(
        body,
        mesh=mesh,
        in_specs=(by_token, by_segment, by_segment) + (whole,) * 10 + (by_token,),
        out_specs=(
            by_token, by_token, by_segment, by_segment, P("seq"), P(None, "seq"), P(None, "seq"), P("seq"),
            P("seq", None), P(None, "seq"), P("seq"), P(None, "seq"), P("seq"), P("seq", None),
        ),
        check_vma=False,
    )
```

```python
import functools
import math

import jax
import jax.numpy as jnp
from jax import lax
from jax.experimental import pallas as pl
from jax.experimental.pallas import tpu as pltpu
from jax.sharding import PartitionSpec as P

EPS = 1e-05
LANES = 128
CHUNK = 16
LOG2E = math.log2(math.e)
LN2 = math.log(2.0)
BF16 = jnp.bfloat16
F32 = jnp.float32
VMEM_BYTES = 56 * 2**20


def silu_parts(value):
    sigmoid = jax.nn.sigmoid(value)
    return value * sigmoid, sigmoid * (1.0 + value * (1.0 - sigmoid))


def matmul(left, right):
    return lax.dot_general(left, right, (((1,), (0,)), ((), ())), preferred_element_type=F32)


def matmul_nt(left, right):
    return lax.dot_general(left, right, (((1,), (1,)), ((), ())), preferred_element_type=F32)


def matmul_tn(left, right):
    return lax.dot_general(left, right, (((0,), (0,)), ((), ())), preferred_element_type=F32)


def partner_route(axis, step):
    count = lax.axis_size(axis)
    if count & (count - 1) == 0:
        return [(i, i ^ step) for i in range(count)]
    return [(i, (i + step) % count) for i in range(count)]


def partners(axis, step):
    count, mine = lax.axis_size(axis), lax.axis_index(axis)
    if count & (count - 1) == 0:
        return mine ^ step, mine ^ step
    return (mine + step) % count, (mine + count - step) % count


def swap_columns(block, axis):
    count = lax.axis_size(axis)
    rows, width = block.shape[0], block.shape[1] // count
    gathered = jnp.zeros((count * rows, width), block.dtype)
    for step in range(count):
        target, source = partners(axis, step)
        piece = lax.dynamic_slice_in_dim(block, target * width, width, 1)
        if step:
            piece = lax.ppermute(piece, axis, partner_route(axis, step))
        gathered = lax.dynamic_update_slice_in_dim(gathered, piece, source * rows, 0)
    return gathered


def swap_rows(block, axis):
    count = lax.axis_size(axis)
    rows, width = block.shape[0] // count, block.shape[1]
    gathered = jnp.zeros((rows, count * width), block.dtype)
    for step in range(count):
        target, source = partners(axis, step)
        piece = lax.dynamic_slice_in_dim(block, target * rows, rows, 0)
        if step:
            piece = lax.ppermute(piece, axis, partner_route(axis, step))
        gathered = lax.dynamic_update_slice_in_dim(gathered, piece, source * width, 1)
    return gathered


def sum_scatter(blocks, axis):
    count, mine = lax.axis_size(axis), lax.axis_index(axis)
    if count & (count - 1):
        return lax.psum_scatter(blocks, axis, scatter_dimension=0)
    levels = count.bit_length() - 1
    held = blocks.reshape((2,) * levels + blocks.shape[1:])
    for level in range(levels):
        bit = (mine >> level) & 1
        at = levels - 1 - level
        sent = lax.dynamic_index_in_dim(held, 1 - bit, at, keepdims=False).astype(BF16)
        arrived = lax.ppermute(sent, axis, [(i, i ^ (1 << level)) for i in range(count)])
        held = lax.dynamic_index_in_dim(held, bit, at, keepdims=False).astype(F32) + arrived.astype(F32)
    return held


def gather_rows(block, axis):
    count = lax.axis_size(axis)
    rows = block.shape[0]
    gathered = jnp.zeros((count * rows,) + block.shape[1:], block.dtype)
    for step in range(count):
        _, source = partners(axis, step)
        piece = lax.ppermute(block, axis, partner_route(axis, step)) if step else block
        gathered = lax.dynamic_update_slice_in_dim(gathered, piece, source * rows, 0)
    return gathered


def shifted(block, axis, distance):
    devices = range(lax.axis_size(axis))
    route = [(i - distance, i) for i in devices if i - distance in devices]
    return lax.ppermute(block, axis, route)


def from_first(block, axis):
    count, mine = lax.axis_size(axis), lax.axis_index(axis)
    reach = 1
    while reach < count:
        route = [(i, i + reach) for i in range(min(reach, count - reach))]
        arrived = lax.ppermute(block, axis, route)
        block = jnp.where(mine < reach, block, arrived)
        reach *= 2
    return block


MESH = pl.DeviceIdType.MESH


def carry_kernel(
    pieces, end_ref, mu_ref, total_ref, entry_ref, a_ref, start_ref, lam_ref, back,
    ahead, from_left, from_right, sent_right, sent_left, got_left, got_right,
):
    count, mine = lax.axis_size("seq"), lax.axis_index("seq")
    width = end_ref.shape[2] // pieces
    has_left, has_right = mine > 0, mine < count - 1
    left, right = jnp.maximum(mine - 1, 0), jnp.minimum(mine + 1, count - 1)

    barrier = pltpu.get_barrier_semaphore()

    @pl.when(has_left)
    def _():
        pl.semaphore_signal(barrier, inc=1, device_id={"seq": left}, device_id_type=MESH)

    @pl.when(has_right)
    def _():
        pl.semaphore_signal(barrier, inc=1, device_id={"seq": right}, device_id_type=MESH)

    pl.semaphore_wait(barrier, has_left.astype(jnp.int32) + has_right.astype(jnp.int32))

    def at(piece):
        return pl.ds(pl.multiple_of(piece * width, LANES), width)

    def to_right(piece):
        return pltpu.make_async_remote_copy(
            src_ref=ahead.at[:, :, at(piece)], dst_ref=from_left.at[:, :, at(piece)],
            send_sem=sent_right.at[piece], recv_sem=got_left.at[piece],
            device_id={"seq": right}, device_id_type=MESH,
        )

    def to_left(piece):
        return pltpu.make_async_remote_copy(
            src_ref=back.at[:, :, at(piece)], dst_ref=from_right.at[:, :, at(piece)],
            send_sem=sent_left.at[piece], recv_sem=got_right.at[piece],
            device_id={"seq": left}, device_id_type=MESH,
        )

    def decay(piece):
        return jnp.exp(total_ref[:, :, at(piece)] * a_ref[:, at(piece)][None])

    def step(tick, nothing):
        piece = tick - mine

        @pl.when(jnp.logical_and(piece >= 0, piece < pieces))
        def _():
            @pl.when(has_left)
            def _():
                to_right(piece).wait_recv()
                start_ref[:, :, at(piece)] = from_left[:, :, at(piece)]

            @pl.when(jnp.logical_not(has_left))
            def _():
                start_ref[:, :, at(piece)] = entry_ref[:, :, at(piece)]

            @pl.when(has_right)
            def _():
                ahead[:, :, at(piece)] = end_ref[:, :, at(piece)] + decay(piece) * start_ref[:, :, at(piece)]
                to_right(piece).start()

        other = tick - (count - 1 - mine)

        @pl.when(jnp.logical_and(other >= 0, other < pieces))
        def _():
            @pl.when(has_right)
            def _():
                to_left(other).wait_recv()
                lam_ref[:, :, at(other)] = from_right[:, :, at(other)]

            @pl.when(jnp.logical_not(has_right))
            def _():
                lam_ref[:, :, at(other)] = jnp.zeros(lam_ref.shape[:2] + (width,), F32)

            back[:, :, at(other)] = mu_ref[:, :, at(other)] + decay(other) * lam_ref[:, :, at(other)]

            @pl.when(has_left)
            def _():
                to_left(other).start()

        return nothing

    lax.fori_loop(0, pieces + count - 1, step, 0)

    def finish(piece, nothing):
        @pl.when(has_right)
        def _():
            to_right(piece).wait_send()

        @pl.when(has_left)
        def _():
            to_left(piece).wait_send()

        return nothing

    lax.fori_loop(0, pieces, finish, 0)


def carry(ends, entry_mu, total, entry_state, a_mat):
    pieces = 6
    while ends.shape[2] % (pieces * LANES):
        pieces -= 1
    shape = jax.ShapeDtypeStruct(ends.shape, F32)
    held = pltpu.VMEM(ends.shape, F32)
    vmem = pl.BlockSpec(memory_space=pltpu.VMEM)
    return pl.pallas_call(
        functools.partial(carry_kernel, pieces),
        in_specs=[vmem] * 5,
        out_specs=[vmem] * 3,
        out_shape=[shape, shape, shape],
        scratch_shapes=[held] * 3 + [pltpu.SemaphoreType.DMA((pieces,))] * 4,
        compiler_params=pltpu.CompilerParams(
            collective_id=1, has_side_effects=True, vmem_limit_bytes=32 * 2**20
        ),
        name="carry",
    )(ends, entry_mu, total, entry_state, a_mat)


def aligned(inner, axis="seq"):
    channels = inner // lax.axis_size(axis)
    return channels % LANES == 0 and widest(inner, 768) % channels == 0


def spread_row(ref, rows, at, tile, states):
    row = ref.at[0, rows][at : at + 1, tile * LANES : (tile + 1) * LANES]
    return jnp.broadcast_to(row, (states, LANES))


def column(tile):
    return slice(tile * LANES, (tile + 1) * LANES)


def ends_kernel(d_ref, act_ref, gate_ref, dg_ref, b_ref, c_ref, a_ref, end_ref, mu_ref, drive, up):
    states = a_ref.shape[0]
    length, width = d_ref.shape[1:]
    tiles = width // LANES
    rate = [a_ref[:, column(j)] * LOG2E for j in range(tiles)]
    drive[0] = d_ref[0] * act_ref[0].astype(F32)
    gate = gate_ref[0]
    up[0] = dg_ref[0] * (gate * jax.nn.sigmoid(gate))

    def chunk(i, carry):
        h, p, mu = (list(part) for part in carry)
        rows = pl.ds(pl.multiple_of(i * CHUNK, CHUNK), CHUNK)
        for r in range(CHUNK):
            b, c = b_ref[0, i * CHUNK + r], c_ref[0, i * CHUNK + r]
            for j in range(tiles):
                decay = jnp.exp2(spread_row(d_ref, rows, r, j, states) * rate[j])
                h[j] = h[j] * decay + spread_row(drive, rows, r, j, states) * b
                p[j] = p[j] * decay
                mu[j] = mu[j] + p[j] * (spread_row(up, rows, r, j, states) * c)
        return tuple(h), tuple(p), tuple(mu)

    zeros = tuple(jnp.zeros((states, LANES), F32) for _ in range(tiles))
    ones = tuple(jnp.ones((states, LANES), F32) for _ in range(tiles))
    h, _, mu = lax.fori_loop(0, length // CHUNK, chunk, (zeros, ones, zeros))
    for j in range(tiles):
        end_ref[0, :, column(j)] = h[j]
        mu_ref[0, :, column(j)] = mu[j]


def widest(inner, most):
    width = most
    while inner % width:
        width -= LANES
    return width


def block_ends(delta, act, gate_in, d_gated, b_wide, c_wide, a_mat):
    segs, length, inner = delta.shape
    states = a_mat.shape[0]
    width = widest(inner, 512)
    tokens = pl.BlockSpec((1, length, width), lambda s, e: (s, 0, e))
    wide = pl.BlockSpec((1, length, states, LANES), lambda s, e: (s, 0, 0, 0))
    state = pl.BlockSpec((1, states, width), lambda s, e: (s, 0, e))
    shape = jax.ShapeDtypeStruct((segs, states, inner), F32)
    return pl.pallas_call(
        ends_kernel,
        grid=(segs, inner // width),
        in_specs=[tokens] * 4 + [wide, wide, pl.BlockSpec((states, width), lambda s, e: (0, e))],
        out_specs=[state, state],
        out_shape=[shape, shape],
        scratch_shapes=[pltpu.VMEM((1, length, width), F32)] * 2,
        compiler_params=pltpu.CompilerParams(vmem_limit_bytes=VMEM_BYTES),
        cost_estimate=pl.CostEstimate(
            flops=9 * delta.size * states, bytes_accessed=12 * delta.size, transcendentals=delta.size * states
        ),
        name="block_ends",
    )(delta, act, gate_in, d_gated, b_wide, c_wide, a_mat)


def scan_kernel(
    hosted, n_blocks_static, n_ticks, d_ref, act_ref, gate_ref, dg_ref, b_ref, c_ref, c_diag, b_diag, ones_ref, a_ref, skip_ref, start_ref, end_ref, first_ref,
    gated_ref, dgate_ref, dpre_ref, dact_ref, db_ref, dc_ref, da_ref, sums_ref, gated_all, gate_all, first_all,
    history, drive, up, low_a, low_b, through_a, through_b, db_acc, dc_acc, sum_acc,
    gated_out, gate_out, gated_sent, gated_got, gate_sent, gate_got, own_sem, first_sent, first_got,
    near_got, relay_sent, relay_got,
):
    states = a_ref.shape[0]
    length, width = d_ref.shape[1:]
    tiles, chunks = width // LANES, length // CHUNK
    span = math.gcd(width, 256)
    parts = width // span
    rate = [a_ref[:, column(j)] * LOG2E for j in range(tiles)]
    seg, block, n_blocks = pl.program_id(0), pl.program_id(1), pl.num_programs(1)
    n_dp, n_seq = lax.axis_size("dp"), lax.axis_size("seq")
    my_dp, my_seq = lax.axis_index("dp"), lax.axis_index("seq")
    tick = seg * n_blocks + block
    slot = lax.rem(tick, 2)
    channels = n_blocks_static * width // n_seq
    owners = width // channels if hosted else 0
    relayed = n_dp == 4

    first_own = pltpu.make_async_copy(first_ref, first_all, first_got.at[0])
    first_far = pltpu.make_async_remote_copy(
        src_ref=first_all, dst_ref=first_all, send_sem=first_sent.at[0], recv_sem=first_got.at[0],
        device_id={"seq": jnp.minimum(my_seq + 1, n_seq - 1)}, device_id_type=MESH,
    )

    @pl.when(tick == 0)
    def _():
        barrier = pltpu.get_barrier_semaphore()
        for p in range(1, n_dp):
            pl.semaphore_signal(barrier, inc=1, device_id={"dp": lax.rem(my_dp + p, n_dp)}, device_id_type=MESH)
        for p in range(1, n_seq):
            pl.semaphore_signal(barrier, inc=1, device_id={"seq": lax.rem(my_seq + p, n_seq)}, device_id_type=MESH)
        pl.semaphore_wait(barrier, n_dp + n_seq - 2)

        @pl.when(my_seq == 0)
        def _():
            first_own.start()

    @pl.when(tick == jnp.minimum(my_seq * max(1, n_ticks // n_seq), n_ticks - 1))
    def _():
        @pl.when(my_seq == 0)
        def _():
            first_own.wait()

        @pl.when(my_seq != 0)
        def _():
            first_far.wait_recv()

        @pl.when(my_seq != n_seq - 1)
        def _():
            first_far.start()

    def gated_copies(s, e, slot):
        at = (my_dp, s, slice(None), pl.ds(pl.multiple_of(e * width, LANES), width))
        own = pltpu.make_async_copy(gated_out.at[slot], gated_all.at[at], own_sem.at[slot, 0])
        if relayed:
            ids = [(my_dp ^ (1 + way), near_got.at[way, s * n_blocks + e], way) for way in range(2)]
        else:
            ids = [(lax.rem(my_dp + p, n_dp), gated_got.at[my_dp], p) for p in range(1, n_dp)]
        far = [
            pltpu.make_async_remote_copy(
                src_ref=gated_out.at[slot], dst_ref=gated_all.at[at],
                send_sem=gated_sent.at[slot, p], recv_sem=got,
                device_id={"dp": peer}, device_id_type=MESH,
            )
            for peer, got, p in ids
        ]
        return own, far

    def passed(s, e, way):
        rows = slice(way * (length // 2), (way + 1) * (length // 2))
        at = (my_dp ^ (1 + way), s, rows, pl.ds(pl.multiple_of(e * width, LANES), width))
        return pltpu.make_async_remote_copy(
            src_ref=gated_all.at[at], dst_ref=gated_all.at[at],
            send_sem=relay_sent.at[way, s * n_blocks + e], recv_sem=relay_got.at[way],
            device_id={"dp": my_dp ^ (2 - way)}, device_id_type=MESH,
        )

    def relay(t):
        s, e = t // n_blocks, lax.rem(t, n_blocks)
        for way in range(2):
            peer = my_dp ^ (1 + way)
            at = (peer, s, slice(None), pl.ds(pl.multiple_of(e * width, LANES), width))
            pltpu.make_async_remote_copy(
                src_ref=gated_out.at[0], dst_ref=gated_all.at[at],
                send_sem=gated_sent.at[0, way], recv_sem=near_got.at[way, t],
                device_id={"dp": peer}, device_id_type=MESH,
            ).wait_recv()
            passed(s, e, way).start()

    def gate_copies(s, e, slot):
        for q in range(owners):
            owner = e * owners + q
            source = gate_out.at[slot, :, q * channels : (q + 1) * channels]
            own = pltpu.make_async_copy(source, gate_all.at[my_seq, s], own_sem.at[slot, 1 + q])
            far = pltpu.make_async_remote_copy(
                src_ref=source, dst_ref=gate_all.at[my_seq, s],
                send_sem=gate_sent.at[slot, q], recv_sem=gate_got.at[my_seq],
                device_id={"seq": owner}, device_id_type=MESH,
            )
            yield owner, own, far

    def send(s, e, slot):
        own, far = gated_copies(s, e, slot)
        own.start()
        for copy in far:
            copy.start()
        for owner, own, far in gate_copies(s, e, slot):
            pl.when(owner == my_seq)(own.start)
            pl.when(owner != my_seq)(far.start)

    def drain(s, e, slot):
        own, far = gated_copies(s, e, slot)
        own.wait()
        for copy in far:
            copy.wait_send()
        for owner, own, far in gate_copies(s, e, slot):
            pl.when(owner == my_seq)(own.wait)
            pl.when(owner != my_seq)(far.wait_send)

    @pl.when(tick >= 2)
    def _():
        drain((tick - 2) // n_blocks, lax.rem(tick - 2, n_blocks), slot)

    history[0:states, :] = start_ref[0]
    drive[0] = d_ref[0] * act_ref[0].astype(F32)
    gate_block = gate_ref[0]
    up[0] = dg_ref[0] * (gate_block * jax.nn.sigmoid(gate_block))
    sum_acc[...] = jnp.zeros_like(sum_acc)

    def rows_of(i):
        return pl.ds(pl.multiple_of(i * CHUNK, CHUNK), CHUNK)

    def kept(i, r):
        return pl.ds(pl.multiple_of((i * CHUNK + r) * states, states), states)

    def sum_y(i, low, part):
        at, rows = slice(part * span, (part + 1) * span), rows_of(i)
        produced = jnp.dot(c_diag[0, i], low[:, at], preferred_element_type=F32)
        scanned = produced + skip_ref[:, at] * act_ref[0, rows, at].astype(F32)
        gate = gate_ref[0, rows, at]
        sigmoid = jax.nn.sigmoid(gate)
        gated = (scanned * (gate * sigmoid)).astype(BF16)
        slope = sigmoid * (1.0 + gate * (1.0 - sigmoid))
        d_gate = (dg_ref[0, rows, at] * scanned * slope).astype(BF16)
        gated_ref[0, rows, at] = gated
        dgate_ref[0, rows, at] = d_gate
        gated_out[slot, rows, at] = gated
        if hosted:
            gate_out[slot, rows, at] = d_gate

    def forward(i, h, low, before, low_before):
        rows = rows_of(i)
        waiting = list(range(parts))
        for r in range(CHUNK):
            b = b_ref[0, i * CHUNK + r]
            for j in range(tiles):
                decay = jnp.exp2(spread_row(d_ref, rows, r, j, states) * rate[j])
                h[j] = h[j] * decay + spread_row(drive, rows, r, j, states) * b
                history[kept(i, r + 1), column(j)] = h[j]
                low[r * states : (r + 1) * states, column(j)] = h[j].astype(BF16)
            if waiting and r % max(1, CHUNK // parts) == 1:
                sum_y(before, low_before, waiting.pop(0))
        for part in waiting:
            sum_y(before, low_before, part)
        return h

    def forward_pair(pair, carry):
        h = forward(2 * pair, list(carry), low_a, jnp.maximum(2 * pair - 1, 0), low_b)
        return tuple(forward(2 * pair + 1, h, low_b, 2 * pair, low_a))

    lax.fori_loop(0, chunks // 2, forward_pair, tuple(start_ref[0, :, column(j)] for j in range(tiles)))
    for part in range(parts):
        sum_y(chunks - 1, low_b, part)
    send(seg, block, slot)
    if relayed:

        @pl.when(tick >= 1)
        def _():
            relay(tick - 1)

    @pl.when(pl.program_id(1) == 0)
    def _():
        db_acc[...] = jnp.zeros_like(db_acc)
        dc_acc[...] = jnp.zeros_like(dc_acc)

    def sum_back(i, low, through, part, count=None):
        at, rows = slice(part * span, (part + 1) * span), rows_of(i)
        d_drive = jnp.dot(b_diag[0, i], low[:, at], preferred_element_type=F32)
        d_rate = jnp.dot(ones_ref[...], through[:, at], preferred_element_type=F32)
        delta, act, d_scanned = d_ref[0, rows, at], act_ref[0, rows, at].astype(F32), up[0, rows, at]
        near = delta * (1.0 - delta * (0.5 - delta * (1.0 / 6.0 - delta * (1.0 / 24.0))))
        slope = jnp.where(delta < 0.03, near, 1.0 - jnp.exp(-delta))
        d_pre = (LN2 * d_rate + d_drive * act) * slope
        dpre_ref[0, rows, at] = d_pre.astype(BF16)
        dact_ref[0, rows, at] = skip_ref[:, at] * d_scanned + d_drive * delta
        if count is None:
            sum_acc[0, :, at] += d_pre
            sum_acc[1, :, at] += d_scanned * act
        else:
            sum_acc[0, :, at] += jnp.where(count, d_pre, 0.0)
            sum_acc[1, :, at] += jnp.where(count, d_scanned * act, 0.0)

    def backward(i, lam, da, low, through, before, low_before, through_before, count=None):
        rows = rows_of(i)
        waiting = list(range(parts))
        for r in reversed(range(CHUNK)):
            c = c_ref[0, i * CHUNK + r]
            db = dc = None
            for j in range(tiles):
                step = spread_row(d_ref, rows, r, j, states)
                upstream = spread_row(up, rows, r, j, states)
                adjoint = lam[j] + upstream * c
                db_j = adjoint * spread_row(drive, rows, r, j, states)
                dc_j = upstream * history[kept(i, r + 1), column(j)]
                db, dc = (db_j, dc_j) if db is None else (db + db_j, dc + dc_j)
                low[r * states : (r + 1) * states, column(j)] = adjoint.astype(BF16)
                lam[j] = adjoint * jnp.exp2(step * rate[j])
                flow = lam[j] * history[kept(i, r), column(j)]
                through[r * states : (r + 1) * states, column(j)] = (flow * rate[j]).astype(BF16)
                da[j] = da[j] + flow * step
            db_acc[i * CHUNK + r] += db
            dc_acc[i * CHUNK + r] += dc
            if waiting and (CHUNK - 1 - r) % max(1, CHUNK // parts) == 1:
                sum_back(before, low_before, through_before, waiting.pop(0), count)
        for part in waiting:
            sum_back(before, low_before, through_before, part, count)
        return lam, da

    def backward_pair(pair, carry):
        lam, da = (list(part) for part in carry)
        i = chunks - 1 - 2 * pair
        lam, da = backward(i, lam, da, low_a, through_a, jnp.minimum(i + 1, chunks - 1), low_b, through_b, pair > 0)
        lam, da = backward(i - 1, lam, da, low_b, through_b, i, low_a, through_a)
        return tuple(lam), tuple(da)

    zeros = tuple(jnp.zeros((states, LANES), F32) for _ in range(tiles))
    _, da = lax.fori_loop(
        0, chunks // 2, backward_pair, (tuple(end_ref[0, :, column(j)] for j in range(tiles)), zeros)
    )
    for part in range(parts):
        sum_back(0, low_b, through_b, part)
    for j in range(tiles):
        da_ref[0, :, column(j)] = da[j]
    sums_ref[0, 0:1, :] = jnp.sum(sum_acc[0], axis=0, keepdims=True)
    sums_ref[0, 1:2, :] = jnp.sum(sum_acc[1], axis=0, keepdims=True)
    sums_ref[0, 2:8, :] = jnp.zeros((6, width), F32)

    @pl.when(pl.program_id(1) == pl.num_programs(1) - 1)
    def _():
        db_ref[0] = jnp.sum(db_acc[...], axis=-1)
        dc_ref[0] = jnp.sum(dc_acc[...], axis=-1)

    @pl.when(tick == pl.num_programs(0) * n_blocks - 1)
    def _():
        drain((tick - 1) // n_blocks, lax.rem(tick - 1, n_blocks), 1 - slot)
        if relayed:
            relay(tick)
        drain(seg, block, slot)
        if relayed:

            def finish_relay(t, nothing):
                for way in range(2):
                    passed(t // n_blocks_static, lax.rem(t, n_blocks_static), way).wait_send()
                return nothing

            lax.fori_loop(0, n_ticks, finish_relay, 0)
            across = my_dp ^ 3
            for way in range(2):
                at = (across, slice(None), slice(way * (length // 2), (way + 1) * (length // 2)))
                pltpu.make_async_remote_copy(
                    src_ref=gated_all.at[at], dst_ref=gated_all.at[at],
                    send_sem=gated_sent.at[0, 0], recv_sem=relay_got.at[way],
                    device_id={"dp": across}, device_id_type=MESH,
                ).wait_recv()
        for p in range(1, 1 if relayed else n_dp):
            source = lax.rem(my_dp + p, n_dp)
            pltpu.make_async_remote_copy(
                src_ref=gated_all.at[source], dst_ref=gated_all.at[source],
                send_sem=gated_sent.at[0, 0], recv_sem=gated_got.at[source],
                device_id={"dp": source}, device_id_type=MESH,
            ).wait_recv()

        @pl.when(my_seq != n_seq - 1)
        def _():
            first_far.wait_send()

        for p in range(1, n_seq if hosted else 1):
            source = lax.rem(my_seq + p, n_seq)
            pltpu.make_async_remote_copy(
                src_ref=gate_all.at[source], dst_ref=gate_all.at[source],
                send_sem=gate_sent.at[0, 0], recv_sem=gate_got.at[source],
                device_id={"seq": source}, device_id_type=MESH,
            ).wait_recv()


def scan_both(delta, act, gate_in, d_gated, b_wide, c_wide, c_diag, b_diag, ones_diag, a_mat, d_skip, start, end, first):
    segs, length, inner = delta.shape
    states = a_mat.shape[0]
    width = widest(inner, 768)
    tokens = pl.BlockSpec((1, length, width), lambda s, e: (s, 0, e))
    wide = pl.BlockSpec((1, length, states, LANES), lambda s, e: (s, 0, 0, 0))
    diag = pl.BlockSpec((1,) + c_diag.shape[1:], lambda s, e: (s, 0, 0, 0))
    state = pl.BlockSpec((1, states, width), lambda s, e: (s, 0, e))
    narrow = pl.BlockSpec((1, length, states), lambda s, e: (s, 0, 0))
    by_token = jax.ShapeDtypeStruct((segs, length, inner), F32)
    by_token_low = jax.ShapeDtypeStruct((segs, length, inner), BF16)
    by_state = jax.ShapeDtypeStruct((segs, length, states), F32)
    low = pltpu.VMEM((CHUNK * states, width), BF16)
    lanes = pltpu.VMEM((length, states, LANES), F32)
    n_dp, n_seq = lax.axis_size("dp"), lax.axis_size("seq")
    channels = inner // n_seq
    hosted = aligned(inner)
    dma = pltpu.SemaphoreType.DMA
    out = pltpu.VMEM((2, length, width), BF16)
    return pl.pallas_call(
        functools.partial(scan_kernel, hosted, inner // width, segs * (inner // width)),
        grid=(segs, inner // width),
        in_specs=[
            tokens, tokens, tokens, tokens, wide, wide, diag, diag,
            pl.BlockSpec(ones_diag.shape, lambda s, e: (0, 0)),
            pl.BlockSpec((states, width), lambda s, e: (0, e)),
            pl.BlockSpec((1, width), lambda s, e: (0, e)),
            state, state,
            pl.BlockSpec(memory_space=pl.ANY),
        ],
        out_specs=[
            tokens, tokens, tokens, tokens, narrow, narrow, state,
            pl.BlockSpec((1, 8, width), lambda s, e: (s, 0, e)),
            pl.BlockSpec(memory_space=pl.ANY),
            pl.BlockSpec(memory_space=pl.ANY),
            pl.BlockSpec(memory_space=pl.ANY),
        ],
        out_shape=[
            by_token_low, by_token_low, by_token_low, by_token, by_state, by_state,
            jax.ShapeDtypeStruct((segs, states, inner), F32),
            jax.ShapeDtypeStruct((segs, 8, inner), F32),
            jax.ShapeDtypeStruct((n_dp, segs, length, inner), BF16),
            jax.ShapeDtypeStruct((n_seq, segs, length, channels), BF16),
            jax.ShapeDtypeStruct(first.shape, F32),
        ],
        scratch_shapes=[
            pltpu.VMEM(((length + 1) * states, width), F32),
            pltpu.VMEM((1, length, width), F32),
            pltpu.VMEM((1, length, width), F32),
            low, low, low, low, lanes, lanes,
            pltpu.VMEM((2, CHUNK, width), F32),
            out, out,
            dma((2, n_dp)), dma((n_dp,)), dma((2, n_seq)), dma((n_seq,)), dma((2, 1 + n_seq)),
            dma((1,)), dma((1,)),
            dma((2, segs * (inner // width))), dma((2, segs * (inner // width))), dma((2,)),
        ],
        compiler_params=pltpu.CompilerParams(
            collective_id=2, has_side_effects=True, vmem_limit_bytes=VMEM_BYTES
        ),
        cost_estimate=pl.CostEstimate(
            flops=20 * delta.size * states, bytes_accessed=24 * delta.size, transcendentals=2 * delta.size * states
        ),
        name="scan_both",
    )(delta, act, gate_in, d_gated, b_wide, c_wide, c_diag, b_diag, ones_diag, a_mat, d_skip[None], start, end, first)


def finish_kernel(
    conv_hbm, gate_hbm, columns_hbm, normed_hbm, proj_hbm, tokens_hbm, cot_hbm, small_hbm, halo_hbm, gain_ref,
    d_tokens, d_in, small_out, halo_out,
    conv, gate, gate_columns, conv_columns, normed, proj, tokens, cot, small, d_normed,
    partial, arrived, placed, small_dp, small_mid, small_seq,
    load, normed_load, proj_load, swap_sent, swap_got, swap_own, add_sent, add_got, put_sent, put_got, put_own,
    copy_sent, copy_got, mid_sent, mid_got, far_sent, far_got, last_sent, last_got, halo_sent, halo_got,
):
    n_dp, n_seq = lax.axis_size("dp"), lax.axis_size("seq")
    my_dp, my_seq = lax.axis_index("dp"), lax.axis_index("seq")
    half = n_seq // 2
    count, inner = conv_hbm.shape
    width = tokens.shape[1]
    channels = inner // n_seq
    chunks = channels // LANES
    rows_dp = width // n_dp
    rows_small = small_hbm.shape[0] // n_dp
    gain_rows = small_mid.shape[0] - rows_small
    dp_peers = [lax.rem(my_dp + p, n_dp) for p in range(n_dp)]
    seq_peers = [lax.rem(my_seq + p, n_seq) for p in range(n_seq)]

    def remote(src, dst, sent, got, **to):
        return pltpu.make_async_remote_copy(
            src_ref=src, dst_ref=dst, send_sem=sent, recv_sem=got, device_id=to, device_id_type=MESH
        )

    loads = [
        pltpu.make_async_copy(src, dst, load.at[k])
        for k, (src, dst) in enumerate(
            [(columns_hbm, gate_columns), (conv_hbm, conv), (gate_hbm, gate), (tokens_hbm, tokens), (cot_hbm, cot),
             (small_hbm.at[pl.ds(pl.multiple_of(my_dp * rows_small, 16), rows_small)], small)]
        )
    ]
    load_columns, load_conv, load_gate, load_tokens, load_cot, load_small = loads
    load_normed = [pltpu.make_async_copy(normed_hbm.at[s], normed.at[s], normed_load.at[s]) for s in range(n_seq)]
    depth = proj.shape[2]

    def load_proj(k):
        return pltpu.make_async_copy(proj_hbm.at[:, k * depth : (k + 1) * depth], proj.at[k % 2], proj_load.at[k % 2])

    load_columns.start()
    for copy in load_normed:
        copy.start()
    load_conv.start()
    load_proj(0).start()
    for copy in (load_gate, load_tokens, load_cot, load_small):
        copy.start()

    barrier = pltpu.get_barrier_semaphore()
    for p in range(1, n_dp):
        pl.semaphore_signal(barrier, inc=1, device_id={"dp": dp_peers[p]}, device_id_type=MESH)
    for p in range(1, n_seq):
        pl.semaphore_signal(barrier, inc=1, device_id={"seq": seq_peers[p]}, device_id_type=MESH)
    pl.semaphore_wait(barrier, n_dp + n_seq - 2)

    def column_of(device, c):
        return pl.ds(pl.multiple_of(device * channels + c * LANES, LANES), LANES)

    def swap(c, p):
        return remote(
            conv_hbm.at[:, column_of(seq_peers[p], c)], conv_columns.at[c, my_seq],
            swap_sent.at[c, p], swap_got.at[c, my_seq], seq=seq_peers[p],
        )

    own_swaps = [
        pltpu.make_async_copy(conv_hbm.at[:, column_of(my_seq, c)], conv_columns.at[c, my_seq], swap_own.at[c])
        for c in range(chunks)
    ]

    def start_swap(c):
        own_swaps[c].start()
        for p in range(1, n_seq):
            swap(c, p).start()

    start_swap(0)

    def halo(p):
        return remote(halo_hbm, halo_out, halo_sent.at[p], halo_got.at[0], seq=p)

    halo_own = pltpu.make_async_copy(halo_hbm, halo_out, halo_got.at[0])

    @pl.when(my_seq == 0)
    def _():
        halo_own.start()
        for p in range(1, n_seq):
            halo(p).start()

    def small_rows(device):
        return pl.ds(pl.multiple_of(device * rows_small, 16), rows_small)

    def small_add(p):
        return remote(
            small_hbm.at[small_rows(dp_peers[p])], small_dp.at[my_dp], mid_sent.at[p], mid_got.at[my_dp], dp=dp_peers[p]
        )

    for p in range(1, n_dp):
        small_add(p).start()
    def product(c, columns):
        tile = 768 if width % 768 == 0 else 256

        def some_rows(r, nothing):
            at = pl.ds(pl.multiple_of(r * tile, tile), tile)
            total = jnp.dot(normed[0, at, :], columns(0), preferred_element_type=F32)
            for s in range(1, n_seq):
                total += jnp.dot(normed[s, at, :], columns(s), preferred_element_type=F32)
            partial[c, at, :] = total.astype(BF16)
            return nothing

        lax.fori_loop(0, width // tile, some_rows, 0)

    def rows_of(device):
        return pl.ds(pl.multiple_of(device * rows_dp, 16), rows_dp)

    def add(c, p):
        return remote(
            partial.at[c, rows_of(dp_peers[p])], arrived.at[c, my_dp], add_sent.at[c, p], add_got.at[c, my_dp],
            dp=dp_peers[p],
        )

    def scatter(c):
        for p in range(1, n_dp):
            add(c, p).start()

    def place(c):
        k, is_gate = c % chunks, c < chunks
        keeper = my_seq // 2 + (half if is_gate else 0)
        side = lax.rem(my_seq, 2)
        at = (rows_of(my_dp), pl.ds(pl.multiple_of(side * channels + k * LANES, LANES), LANES))
        own = pltpu.make_async_copy(placed.at[c], d_in.at[at], put_own.at[c])
        far = remote(placed.at[c], d_in.at[at], put_sent.at[c], put_got.at[k, side], seq=keeper)
        return keeper, own, far

    def gather_add(c):
        total = partial[c, rows_of(my_dp), :].astype(F32)
        for p in range(1, n_dp):
            remote(
                partial.at[c, rows_of(my_dp)], arrived.at[c, dp_peers[p]], add_sent.at[c, p],
                add_got.at[c, dp_peers[p]], dp=dp_peers[p],
            ).wait_recv()
            total += arrived[c, dp_peers[p]].astype(F32)
        placed[c] = total.astype(BF16)
        keeper, own, far = place(c)
        pl.when(keeper == my_seq)(own.start)
        pl.when(keeper != my_seq)(far.start)

    def spread(k, side, p):
        at = (rows_of(my_dp), slice(side * channels + k * LANES, side * channels + (k + 1) * LANES))
        return remote(
            d_in.at[at], d_in.at[at], copy_sent.at[k, side, p], copy_got.at[k, side, my_dp], dp=dp_peers[p]
        )

    def pass_on(c):
        k, is_gate = c % chunks, c < chunks

        @pl.when((my_seq >= half) == is_gate)
        def _():
            for side in range(2):
                source = 2 * lax.rem(my_seq, half) + side
                at = (rows_of(my_dp), slice(side * channels + k * LANES, side * channels + (k + 1) * LANES))

                @pl.when(source == my_seq)
                def _():
                    place(c)[1].wait()

                @pl.when(source != my_seq)
                def _():
                    remote(placed.at[c], d_in.at[at], put_sent.at[c], put_got.at[k, side], seq=source).wait_recv()

                for p in range(1, n_dp):
                    spread(k, side, p).start()

    load_columns.wait()
    for copy in load_normed:
        copy.wait()
    for c in range(chunks):
        product(c, lambda s, c=c: gate_columns[s, :, c * LANES : (c + 1) * LANES])
        scatter(c)
    if chunks > 1:
        start_swap(1)

    load_conv.wait()
    load_gate.wait()
    steps = 2 * inner // depth
    for k in range(steps):
        if k + 1 < steps:
            load_proj(k + 1).start()
        load_proj(k).wait()
        source, at = (conv, k * depth) if k * depth < inner else (gate, k * depth - inner)

        def some_columns(n, nothing, k=k, source=source, at=at):
            cols = pl.ds(pl.multiple_of(n * 256, 256), 256)
            term = lax.dot_general(
                source[:, at : at + depth], proj[k % 2, cols, :], (((1,), (1,)), ((), ())), preferred_element_type=F32
            )
            d_normed[:, cols] = term if k == 0 else d_normed[:, cols] + term
            return nothing

        lax.fori_loop(0, width // 256, some_columns, 0)
        if k == steps // 2:
            for c in range(chunks):
                gather_add(c)
            for c in range(2, chunks):
                start_swap(c)

    load_tokens.wait()
    load_cot.wait()
    gain = gain_ref[...]

    def some_tokens(r, total):
        at = pl.ds(pl.multiple_of(r * 32, 32), 32)
        token = tokens[at, :].astype(F32)
        inverse = lax.rsqrt(jnp.mean(token * token, axis=-1, keepdims=True) + EPS)
        scaled = d_normed[at, :] * gain
        mean = jnp.mean(scaled * token, axis=-1, keepdims=True)
        d_tokens[at, :] = cot[at, :].astype(F32) + inverse * scaled - token * (inverse * inverse * inverse * mean)
        return total + jnp.sum(d_normed[at, :] * token * inverse, axis=0, keepdims=True)

    d_gain = lax.fori_loop(0, count // 32, some_tokens, jnp.zeros((1, width), F32))
    load_small.wait()
    gains = jnp.concatenate([d_gain[:, r * channels : (r + 1) * channels] for r in range(width // channels)], axis=0)
    gains = jnp.pad(gains, ((0, gain_rows - width // channels), (0, 0)))
    for s in range(n_seq):
        small_mid[rows_small:, s * channels : (s + 1) * channels] = gains.astype(BF16)
    for c in range(chunks):
        pass_on(c)

    total = small[...].astype(F32)
    for p in range(1, n_dp):
        remote(
            small, small_dp.at[dp_peers[p]], mid_sent.at[p], mid_got.at[dp_peers[p]],
            dp=dp_peers[p],
        ).wait_recv()
        total += small_dp[dp_peers[p]].astype(F32)
    small_mid[0:rows_small, :] = total.astype(BF16)

    def small_swap(p):
        at = pl.ds(pl.multiple_of(seq_peers[p] * channels, LANES), channels)
        return remote(
            small_mid.at[:, at], small_seq.at[my_seq], far_sent.at[p], far_got.at[my_seq], seq=seq_peers[p]
        )

    for p in range(1, n_seq):
        small_swap(p).start()

    def convolved(c):
        own_swaps[c].wait()
        for p in range(1, n_seq):
            remote(
                conv_hbm.at[:, column_of(my_seq, c)], conv_columns.at[c, seq_peers[p]], swap_sent.at[c, p],
                swap_got.at[c, seq_peers[p]], seq=seq_peers[p],
            ).wait_recv()
        product(chunks + c, lambda s: conv_columns[c, s])
        scatter(chunks + c)

    convolved(0)
    gather_add(chunks)
    for c in range(1, chunks):
        convolved(c)
        pass_on(chunks + c - 1)
        gather_add(chunks + c)
    total = small_mid[:, pl.ds(pl.multiple_of(my_seq * channels, LANES), channels)].astype(F32)
    for p in range(1, n_seq):
        remote(
            small_mid.at[:, 0:channels], small_seq.at[seq_peers[p]], far_sent.at[p], far_got.at[seq_peers[p]],
            seq=seq_peers[p],
        ).wait_recv()
        total += small_seq[seq_peers[p]].astype(F32)
    small_out[my_dp] = total.astype(BF16)

    def small_spread(p):
        return remote(small_out.at[my_dp], small_out.at[my_dp], last_sent.at[p], last_got.at[my_dp], dp=dp_peers[p])

    for p in range(1, n_dp):
        small_spread(p).start()
    pass_on(2 * chunks - 1)

    for c in range(chunks):
        for p in range(1, n_seq):
            swap(c, p).wait_send()
    for c in range(2 * chunks):
        for p in range(1, n_dp):
            add(c, p).wait_send()
        keeper, own, far = place(c)

        @pl.when(keeper != my_seq)
        def _(far=far):
            far.wait_send()

    for k in range(chunks):
        for side in range(2):
            at = slice(side * channels + k * LANES, side * channels + (k + 1) * LANES)
            for p in range(1, n_dp):
                spread(k, side, p).wait_send()
                peer = dp_peers[p]
                remote(
                    d_in.at[rows_of(peer), at], d_in.at[rows_of(peer), at], copy_sent.at[k, side, p],
                    copy_got.at[k, side, peer], dp=peer,
                ).wait_recv()
    for p in range(1, n_dp):
        small_add(p).wait_send()
        small_spread(p).wait_send()
        peer = dp_peers[p]
        remote(
            small_out.at[peer], small_out.at[peer], last_sent.at[p], last_got.at[peer], dp=peer
        ).wait_recv()
    for p in range(1, n_seq):
        small_swap(p).wait_send()

    @pl.when(my_seq == 0)
    def _():
        halo_own.wait()
        for p in range(1, n_seq):
            halo(p).wait_send()

    @pl.when(my_seq != 0)
    def _():
        halo(1).wait_recv()


def finish(d_conv_in, d_gate, gate_columns, normed_all, in_proj, tokens, cot, small, halo_grad, norm_gain):
    n_dp, n_seq = lax.axis_size("dp"), lax.axis_size("seq")
    count, inner = d_conv_in.shape
    width = tokens.shape[1]
    channels = inner // n_seq
    chunks = channels // LANES
    rows = small.shape[0] // n_dp
    gain_rows = -(-width // channels // 16) * 16
    depth = 1024 if inner % 1024 == 0 else LANES
    dma = pltpu.SemaphoreType.DMA
    vmem = pltpu.VMEM
    anywhere = pl.BlockSpec(memory_space=pl.ANY)
    inside = pl.BlockSpec(memory_space=pltpu.VMEM)
    return pl.pallas_call(
        finish_kernel,
        in_specs=[anywhere] * 9 + [inside],
        out_specs=[inside, anywhere, inside, anywhere],
        out_shape=[
            jax.ShapeDtypeStruct((count, width), F32),
            jax.ShapeDtypeStruct((width, 2 * channels), BF16),
            jax.ShapeDtypeStruct((n_dp, rows + gain_rows, channels), BF16),
            jax.ShapeDtypeStruct(halo_grad.shape, F32),
        ],
        scratch_shapes=[
            vmem((count, inner), BF16), vmem((count, inner), BF16),
            vmem((n_seq, count, channels), BF16), vmem((chunks, n_seq, count, LANES), BF16),
            vmem((n_seq, width, count), BF16), vmem((2, width, depth), BF16),
            vmem((count, width), BF16), vmem((count, width), BF16), vmem((rows, inner), BF16),
            vmem((count, width), F32),
            vmem((2 * chunks, width, LANES), BF16), vmem((2 * chunks, n_dp, width // n_dp, LANES), BF16),
            vmem((2 * chunks, width // n_dp, LANES), BF16),
            vmem((n_dp, rows, inner), BF16), vmem((rows + gain_rows, inner), BF16),
            vmem((n_seq, rows + gain_rows, channels), BF16),
            dma((6,)), dma((n_seq,)), dma((2,)),
            dma((chunks, n_seq)), dma((chunks, n_seq)), dma((chunks,)),
            dma((2 * chunks, n_dp)), dma((2 * chunks, n_dp)),
            dma((2 * chunks,)), dma((chunks, 2)), dma((2 * chunks,)),
            dma((chunks, 2, n_dp)), dma((chunks, 2, n_dp)),
            dma((n_dp,)), dma((n_dp,)), dma((n_seq,)), dma((n_seq,)), dma((n_dp,)), dma((n_dp,)),
            dma((n_seq,)), dma((1,)),
        ],
        compiler_params=pltpu.CompilerParams(
            collective_id=3, has_side_effects=True, vmem_limit_bytes=60 * 2**20
        ),
        cost_estimate=pl.CostEstimate(
            flops=12 * count * width * inner, bytes_accessed=40 * count * width, transcendentals=0
        ),
        name="finish",
    )(
        d_conv_in, d_gate, gate_columns, normed_all, in_proj, tokens, cot, small, halo_grad, norm_gain[None],
    )


def diagonal_blocks(value):
    segs, length, states = value.shape
    spread = jnp.tile(jnp.eye(states, dtype=BF16), (1, CHUNK))
    tiled = matmul(value.reshape(segs * length, states).astype(BF16), spread)
    mask = jnp.repeat(jnp.eye(CHUNK, dtype=F32), states, axis=1)
    return (tiled.reshape(segs, length // CHUNK, CHUNK, CHUNK * states) * mask).astype(BF16)


def norm_kernel(token_ref, gain_ref, normed_ref, turned_ref):
    token = token_ref[...].astype(F32)
    inverse = lax.rsqrt(jnp.mean(token * token, axis=-1, keepdims=True) + EPS)
    normed = token * inverse * gain_ref[...]
    normed_ref[...] = normed.astype(BF16)
    turned_ref[...] = normed.T.astype(BF16)


def norm(tokens, norm_gain):
    count, width = tokens.shape
    rows = 128
    return pl.pallas_call(
        norm_kernel,
        grid=(count // rows,),
        in_specs=[pl.BlockSpec((rows, width), lambda r: (r, 0)), pl.BlockSpec((1, width), lambda r: (0, 0))],
        out_specs=[pl.BlockSpec((rows, width), lambda r: (r, 0)), pl.BlockSpec((width, rows), lambda r: (0, r))],
        out_shape=[jax.ShapeDtypeStruct((count, width), BF16), jax.ShapeDtypeStruct((width, count), BF16)],
        compiler_params=pltpu.CompilerParams(vmem_limit_bytes=32 * 2**20),
        name="norm",
    )(tokens, norm_gain[None])


def body(
    tokens, conv_state, entry_state, norm_gain, in_proj, conv_weight, conv_bias, x_proj,
    dt_proj, dt_bias, a_log, d_skip, out_proj, cotangent,
):
    segs, length, width = tokens.shape
    inner = in_proj.shape[1] // 2
    rank, states, taps = dt_proj.shape[0], a_log.shape[0], conv_weight.shape[0]
    halo = taps - 1
    count = segs * length
    n_seq = lax.axis_size("seq")
    mine = lax.axis_index("seq")
    is_first = mine == 0

    def flat(value):
        return value.reshape((count,) + value.shape[2:])

    def split(value):
        return value.reshape((segs, length) + value.shape[1:])

    token_float = flat(tokens).astype(F32)
    inverse = lax.rsqrt(jnp.mean(token_float * token_float, axis=-1, keepdims=True) + EPS)
    normed, normed_turned = norm(flat(tokens), norm_gain)
    cot = flat(cotangent)
    fast = aligned(inner)
    if fast:
        normed_all = lax.all_gather(normed_turned, "seq", axis=0, tiled=False)
    else:
        normed_all = lax.all_gather(normed, "seq", axis=0, tiled=True)
    cot_rows = swap_rows(cot.T, "dp")
    conv_in = matmul(normed, in_proj[:, :inner]).astype(BF16)
    gate_in = matmul(normed, in_proj[:, inner:])
    d_gated = matmul_nt(cot, out_proj)
    conv_in = split(conv_in)
    before = jnp.where(is_first, conv_state, shifted(conv_in[:, length - halo :], "seq", 1))
    padded = jnp.concatenate([before, conv_in], axis=1).astype(F32)
    conv_out = conv_bias + sum(conv_weight[tap] * padded[:, tap : tap + length] for tap in range(taps))
    activated = (conv_out * jax.nn.sigmoid(conv_out)).astype(BF16)
    coeffs = matmul(flat(activated), x_proj)
    dt_low = coeffs[:, :rank].astype(BF16)
    b_in = split(coeffs[:, rank : rank + states])
    c_in = split(coeffs[:, rank + states :])
    pre_delta = matmul(dt_low, dt_proj) + dt_bias
    delta = split(jax.nn.softplus(pre_delta))
    a_mat = -jnp.exp(a_log)
    gate_in, d_gated = split(gate_in), split(d_gated)

    b_wide = jnp.broadcast_to(b_in[..., None], b_in.shape + (LANES,))
    c_wide = jnp.broadcast_to(c_in[..., None], c_in.shape + (LANES,))
    ends, entry_mu = block_ends(delta, activated, gate_in, d_gated, b_wide, c_wide, a_mat)
    total = jnp.sum(delta, axis=1, keepdims=True)
    start, end, first = carry(ends, entry_mu, total, entry_state, a_mat)
    start, normed_all = lax.optimization_barrier((start, normed_all))
    ones_diag = diagonal_blocks(jnp.ones((1, CHUNK, states), F32))[0, 0]
    gated, d_gate, d_pre_low, d_act, d_b, d_c, d_amat, sums, gated_all, gate_columns, d_entry = scan_both(
        delta, activated, gate_in, d_gated, b_wide, c_wide,
        diagonal_blocks(c_in), diagonal_blocks(b_in), ones_diag, a_mat, d_skip, start, end, first,
    )
    gated, d_gate, d_pre_low, d_act = flat(gated), flat(d_gate), flat(d_pre_low), flat(d_act)
    gated_all = gated_all.reshape(-1, inner)
    gate_columns = gate_columns.reshape(n_seq * count, -1)
    if (inner // n_seq) % LANES:
        gate_columns = swap_columns(d_gate, "seq")
    output = token_float + matmul(gated, out_proj)
    out_part = matmul(cot_rows, gated_all).astype(BF16)
    out_part = lax.psum_scatter(out_part, "seq", scatter_dimension=1, tiled=True)
    d_out_proj = lax.all_gather(out_part, "dp", axis=0, tiled=True).T.astype(F32)

    sums = jnp.sum(sums, axis=0)
    d_dt_bias, d_d_skip = sums[0], sums[1]
    d_dt_proj = matmul_tn(dt_low, d_pre_low)
    d_dt_low = matmul_nt(d_pre_low, dt_proj)
    d_coeffs = jnp.concatenate([d_dt_low, flat(d_b), flat(d_c)], axis=-1).astype(BF16)
    d_x_proj = matmul_tn(d_coeffs, flat(activated))
    d_a_log = jnp.sum(d_amat, axis=0) * a_mat
    d_act = split(d_act + matmul_nt(d_coeffs, x_proj))
    conv_sigmoid = jax.nn.sigmoid(conv_out)
    d_conv_out = d_act * (conv_sigmoid * (1.0 + conv_out * (1.0 - conv_sigmoid)))
    d_conv_bias = jnp.sum(d_conv_out, axis=(0, 1))
    d_conv_weight = jnp.stack(
        [jnp.sum(d_conv_out * padded[:, tap : tap + length], axis=(0, 1)) for tap in range(taps)]
    )
    halo_grad = sum(
        conv_weight[tap] * jnp.pad(d_conv_out[:, : halo - tap], ((0, 0), (tap, 0), (0, 0))) for tap in range(halo)
    )
    returned = shifted(halo_grad, "seq", -1)
    tail = jnp.pad(d_conv_out, ((0, 0), (0, halo), (0, 0)))
    d_conv_in = sum(conv_weight[tap] * tail[:, halo - tap : halo - tap + length] for tap in range(taps))
    d_conv_in = d_conv_in + jnp.pad(returned, ((0, 0), (length - halo, 0), (0, 0)))
    d_conv_in = flat(d_conv_in).astype(BF16)
    if fast:
        small = jnp.concatenate(
            [
                part.astype(BF16)
                for part in (
                    d_x_proj, d_dt_proj, d_a_log, d_dt_bias[None], d_d_skip[None], d_conv_weight, d_conv_bias[None]
                )
            ],
            axis=0,
        )
        edge_at = 2 * rank + 3 * states + 2
        channels = inner // n_seq
        small = jnp.pad(small, ((0, -small.shape[0] % (16 * lax.axis_size("dp"))), (0, 0)))
        rows = small.shape[0] // lax.axis_size("dp")
        d_tokens, d_in_proj, small, d_conv_state = finish(
            d_conv_in, d_gate, gate_columns.reshape(n_seq, count, channels), normed_all, in_proj, flat(tokens), cot,
            small, halo_grad, norm_gain,
        )
        d_in_proj, small = d_in_proj.astype(F32), small.astype(F32)
        gain = jnp.sum(small[:, rows : rows + width // channels], axis=0)
        small = small[:, :rows].reshape(-1, channels)
        edges = small[edge_at:]
        d_norm_gain = lax.dynamic_index_in_dim(gain.reshape(n_seq, -1), mine, 0, keepdims=False)
    else:
        d_conv_state = from_first(halo_grad, "seq")

        n_dp = lax.axis_size("dp")
        small = jnp.concatenate([d_x_proj, d_dt_proj, d_a_log, d_dt_bias[None], d_d_skip[None]], axis=0)
        small = jnp.pad(small, ((0, -small.shape[0] % 16), (0, 0))).astype(BF16)
        small_columns = swap_columns(small, "seq")
        edges = jnp.concatenate([d_conv_weight, d_conv_bias[None]], axis=0)
        edges = jnp.pad(edges, ((0, -edges.shape[0] % 16), (0, 0))).astype(BF16)
        conv_columns = swap_columns(jnp.concatenate([d_conv_in, edges], axis=0), "seq").reshape(n_seq, -1, inner // n_seq)
        edge_columns = conv_columns[:, count:]
        conv_columns = conv_columns[:, :count].reshape(n_seq * count, -1)

        def blocks(value, axis):
            return value.reshape((lax.axis_size(axis), -1) + value.shape[1:])

        gate_part = sum_scatter(blocks(matmul_tn(normed_all, gate_columns), "dp"), "dp").astype(BF16)
        conv_part = sum_scatter(blocks(matmul_tn(normed_all, conv_columns), "dp"), "dp").astype(BF16)
        half = n_seq // 2
        even = mine % 2 == 0
        straight = [(i, i // 2 + (0 if i % 2 == 0 else half)) for i in range(n_seq)]
        crossed = [(i, i // 2 + (half if i % 2 == 0 else 0)) for i in range(n_seq)]
        first = lax.ppermute(jnp.where(even, conv_part, gate_part), "seq", straight)
        second = lax.ppermute(jnp.where(even, gate_part, conv_part), "seq", crossed)
        low_half = mine < half
        d_in_part = jnp.concatenate(
            [jnp.where(low_half, first, second), jnp.where(low_half, second, first)], axis=1
        )
        d_in_proj = gather_rows(d_in_part, "dp").astype(F32)

        d_normed = matmul_nt(d_conv_in, in_proj[:, :inner]) + matmul_nt(d_gate, in_proj[:, inner:])
        d_norm_gain = jnp.sum(d_normed * token_float * inverse, axis=0)
        scaled = d_normed * norm_gain
        cubed = inverse * inverse * inverse
        d_tokens = (
            cot.astype(F32)
            + inverse * scaled
            - token_float * cubed * jnp.mean(scaled * token_float, axis=-1, keepdims=True)
        )
        gain = sum_scatter(blocks(d_norm_gain, "seq"), "seq")
        channels = inner // n_seq
        per_device = jnp.concatenate(
            [
                jnp.sum(small_columns.reshape(n_seq, -1, channels).astype(F32), axis=0),
                jnp.sum(edge_columns.astype(F32), axis=0),
                jnp.pad(gain, (0, -gain.shape[0] % channels)).reshape(-1, channels),
            ],
            axis=0,
        )
        per_device = per_device.astype(BF16)
        summed = jnp.sum(gather_rows(per_device[None], "dp").astype(F32), axis=0)
        edges = summed[small.shape[0] : small.shape[0] + edges.shape[0]]
        d_norm_gain = summed[small.shape[0] + edges.shape[0] :].reshape(-1)[: gain.shape[0]]
        small = summed

    return (
        split(output),
        split(d_tokens),
        d_conv_state,
        d_entry,
        d_norm_gain,
        d_in_proj,
        edges[:taps],
        edges[taps],
        small[: rank + 2 * states].T,
        small[rank + 2 * states : 2 * rank + 2 * states],
        small[2 * rank + 3 * states],
        small[2 * rank + 2 * states : 2 * rank + 3 * states],
        small[2 * rank + 3 * states + 1],
        d_out_proj,
    )


def solution(mesh):
    by_token, by_segment, whole = P("dp", "seq", None), P("dp", None, None), P()
    return jax.shard_map(
        body,
        mesh=mesh,
        in_specs=(by_token, by_segment, by_segment) + (whole,) * 10 + (by_token,),
        out_specs=(
            by_token, by_token, by_segment, by_segment, P("seq"), P(None, "seq"), P(None, "seq"), P("seq"),
            P("seq", None), P(None, "seq"), P("seq"), P(None, "seq"), P("seq"), P("seq", None),
        ),
        check_vma=False,
    )
```

```python
import functools
import math

import jax
import jax.numpy as jnp
from jax import lax
from jax.experimental import pallas as pl
from jax.experimental.pallas import tpu as pltpu
from jax.sharding import PartitionSpec as P

EPS = 1e-05
LANES = 128
CHUNK = 16
LOG2E = math.log2(math.e)
LN2 = math.log(2.0)
BF16 = jnp.bfloat16
F32 = jnp.float32
VMEM_BYTES = 56 * 2**20


def silu_parts(value):
    sigmoid = jax.nn.sigmoid(value)
    return value * sigmoid, sigmoid * (1.0 + value * (1.0 - sigmoid))


def matmul(left, right):
    return lax.dot_general(left, right, (((1,), (0,)), ((), ())), preferred_element_type=F32)


def matmul_nt(left, right):
    return lax.dot_general(left, right, (((1,), (1,)), ((), ())), preferred_element_type=F32)


def matmul_tn(left, right):
    return lax.dot_general(left, right, (((0,), (0,)), ((), ())), preferred_element_type=F32)


def partner_route(axis, step):
    count = lax.axis_size(axis)
    if count & (count - 1) == 0:
        return [(i, i ^ step) for i in range(count)]
    return [(i, (i + step) % count) for i in range(count)]


def partners(axis, step):
    count, mine = lax.axis_size(axis), lax.axis_index(axis)
    if count & (count - 1) == 0:
        return mine ^ step, mine ^ step
    return (mine + step) % count, (mine + count - step) % count


def swap_columns(block, axis):
    count = lax.axis_size(axis)
    rows, width = block.shape[0], block.shape[1] // count
    gathered = jnp.zeros((count * rows, width), block.dtype)
    for step in range(count):
        target, source = partners(axis, step)
        piece = lax.dynamic_slice_in_dim(block, target * width, width, 1)
        if step:
            piece = lax.ppermute(piece, axis, partner_route(axis, step))
        gathered = lax.dynamic_update_slice_in_dim(gathered, piece, source * rows, 0)
    return gathered


def swap_rows(block, axis):
    count = lax.axis_size(axis)
    rows, width = block.shape[0] // count, block.shape[1]
    gathered = jnp.zeros((rows, count * width), block.dtype)
    for step in range(count):
        target, source = partners(axis, step)
        piece = lax.dynamic_slice_in_dim(block, target * rows, rows, 0)
        if step:
            piece = lax.ppermute(piece, axis, partner_route(axis, step))
        gathered = lax.dynamic_update_slice_in_dim(gathered, piece, source * width, 1)
    return gathered


def sum_scatter(blocks, axis):
    count, mine = lax.axis_size(axis), lax.axis_index(axis)
    if count & (count - 1):
        return lax.psum_scatter(blocks, axis, scatter_dimension=0)
    levels = count.bit_length() - 1
    held = blocks.reshape((2,) * levels + blocks.shape[1:])
    for level in range(levels):
        bit = (mine >> level) & 1
        at = levels - 1 - level
        sent = lax.dynamic_index_in_dim(held, 1 - bit, at, keepdims=False).astype(BF16)
        arrived = lax.ppermute(sent, axis, [(i, i ^ (1 << level)) for i in range(count)])
        held = lax.dynamic_index_in_dim(held, bit, at, keepdims=False).astype(F32) + arrived.astype(F32)
    return held


def gather_rows(block, axis):
    count = lax.axis_size(axis)
    rows = block.shape[0]
    gathered = jnp.zeros((count * rows,) + block.shape[1:], block.dtype)
    for step in range(count):
        _, source = partners(axis, step)
        piece = lax.ppermute(block, axis, partner_route(axis, step)) if step else block
        gathered = lax.dynamic_update_slice_in_dim(gathered, piece, source * rows, 0)
    return gathered


def shifted(block, axis, distance):
    devices = range(lax.axis_size(axis))
    route = [(i - distance, i) for i in devices if i - distance in devices]
    return lax.ppermute(block, axis, route)


def from_first(block, axis):
    count, mine = lax.axis_size(axis), lax.axis_index(axis)
    reach = 1
    while reach < count:
        route = [(i, i + reach) for i in range(min(reach, count - reach))]
        arrived = lax.ppermute(block, axis, route)
        block = jnp.where(mine < reach, block, arrived)
        reach *= 2
    return block


MESH = pl.DeviceIdType.MESH


def carry_kernel(
    pieces, end_ref, mu_ref, total_ref, entry_ref, a_ref, start_ref, lam_ref, back,
    ahead, from_left, from_right, sent_right, sent_left, got_left, got_right,
):
    count, mine = lax.axis_size("seq"), lax.axis_index("seq")
    width = end_ref.shape[2] // pieces
    has_left, has_right = mine > 0, mine < count - 1
    left, right = jnp.maximum(mine - 1, 0), jnp.minimum(mine + 1, count - 1)

    barrier = pltpu.get_barrier_semaphore()

    @pl.when(has_left)
    def _():
        pl.semaphore_signal(barrier, inc=1, device_id={"seq": left}, device_id_type=MESH)

    @pl.when(has_right)
    def _():
        pl.semaphore_signal(barrier, inc=1, device_id={"seq": right}, device_id_type=MESH)

    pl.semaphore_wait(barrier, has_left.astype(jnp.int32) + has_right.astype(jnp.int32))

    def at(piece):
        return pl.ds(pl.multiple_of(piece * width, LANES), width)

    def to_right(piece):
        return pltpu.make_async_remote_copy(
            src_ref=ahead.at[:, :, at(piece)], dst_ref=from_left.at[:, :, at(piece)],
            send_sem=sent_right.at[piece], recv_sem=got_left.at[piece],
            device_id={"seq": right}, device_id_type=MESH,
        )

    def to_left(piece):
        return pltpu.make_async_remote_copy(
            src_ref=back.at[:, :, at(piece)], dst_ref=from_right.at[:, :, at(piece)],
            send_sem=sent_left.at[piece], recv_sem=got_right.at[piece],
            device_id={"seq": left}, device_id_type=MESH,
        )

    def decay(piece):
        return jnp.exp(total_ref[:, :, at(piece)] * a_ref[:, at(piece)][None])

    def step(tick, nothing):
        piece = tick - mine

        @pl.when(jnp.logical_and(piece >= 0, piece < pieces))
        def _():
            @pl.when(has_left)
            def _():
                to_right(piece).wait_recv()
                start_ref[:, :, at(piece)] = from_left[:, :, at(piece)]

            @pl.when(jnp.logical_not(has_left))
            def _():
                start_ref[:, :, at(piece)] = entry_ref[:, :, at(piece)]

            @pl.when(has_right)
            def _():
                ahead[:, :, at(piece)] = end_ref[:, :, at(piece)] + decay(piece) * start_ref[:, :, at(piece)]
                to_right(piece).start()

        other = tick - (count - 1 - mine)

        @pl.when(jnp.logical_and(other >= 0, other < pieces))
        def _():
            @pl.when(has_right)
            def _():
                to_left(other).wait_recv()
                lam_ref[:, :, at(other)] = from_right[:, :, at(other)]

            @pl.when(jnp.logical_not(has_right))
            def _():
                lam_ref[:, :, at(other)] = jnp.zeros(lam_ref.shape[:2] + (width,), F32)

            back[:, :, at(other)] = mu_ref[:, :, at(other)] + decay(other) * lam_ref[:, :, at(other)]

            @pl.when(has_left)
            def _():
                to_left(other).start()

        return nothing

    lax.fori_loop(0, pieces + count - 1, step, 0)

    def finish(piece, nothing):
        @pl.when(has_right)
        def _():
            to_right(piece).wait_send()

        @pl.when(has_left)
        def _():
            to_left(piece).wait_send()

        return nothing

    lax.fori_loop(0, pieces, finish, 0)


def carry(ends, entry_mu, total, entry_state, a_mat):
    pieces = 4
    while ends.shape[2] % (pieces * LANES):
        pieces -= 1
    shape = jax.ShapeDtypeStruct(ends.shape, F32)
    held = pltpu.VMEM(ends.shape, F32)
    vmem = pl.BlockSpec(memory_space=pltpu.VMEM)
    return pl.pallas_call(
        functools.partial(carry_kernel, pieces),
        in_specs=[vmem] * 5,
        out_specs=[vmem] * 3,
        out_shape=[shape, shape, shape],
        scratch_shapes=[held] * 3 + [pltpu.SemaphoreType.DMA((pieces,))] * 4,
        compiler_params=pltpu.CompilerParams(
            collective_id=1, has_side_effects=True, vmem_limit_bytes=32 * 2**20
        ),
        name="carry",
    )(ends, entry_mu, total, entry_state, a_mat)


def aligned(inner, axis="seq"):
    channels = inner // lax.axis_size(axis)
    return channels % LANES == 0 and widest(inner, 1536) % channels == 0


def spread_row(ref, rows, at, tile, states):
    row = ref.at[0, rows][at : at + 1, tile * LANES : (tile + 1) * LANES]
    return jnp.broadcast_to(row, (states, LANES))


def column(tile):
    return slice(tile * LANES, (tile + 1) * LANES)


def ends_kernel(d_ref, act_ref, gate_ref, dg_ref, b_ref, c_ref, a_ref, end_ref, mu_ref, drive, up):
    states = a_ref.shape[0]
    length, width = d_ref.shape[1:]
    tiles = width // LANES
    rate = [a_ref[:, column(j)] * LOG2E for j in range(tiles)]
    drive[0] = d_ref[0] * act_ref[0].astype(F32)
    gate = gate_ref[0]
    up[0] = dg_ref[0] * (gate * jax.nn.sigmoid(gate))

    def chunk(i, carry):
        h, p, mu = (list(part) for part in carry)
        rows = pl.ds(pl.multiple_of(i * CHUNK, CHUNK), CHUNK)
        for r in range(CHUNK):
            b, c = b_ref[0, i * CHUNK + r], c_ref[0, i * CHUNK + r]
            for j in range(tiles):
                decay = jnp.exp2(spread_row(d_ref, rows, r, j, states) * rate[j])
                h[j] = h[j] * decay + spread_row(drive, rows, r, j, states) * b
                p[j] = p[j] * decay
                mu[j] = mu[j] + p[j] * (spread_row(up, rows, r, j, states) * c)
        return tuple(h), tuple(p), tuple(mu)

    zeros = tuple(jnp.zeros((states, LANES), F32) for _ in range(tiles))
    ones = tuple(jnp.ones((states, LANES), F32) for _ in range(tiles))
    h, _, mu = lax.fori_loop(0, length // CHUNK, chunk, (zeros, ones, zeros))
    for j in range(tiles):
        end_ref[0, :, column(j)] = h[j]
        mu_ref[0, :, column(j)] = mu[j]


def widest(inner, most):
    width = most
    while inner % width:
        width -= LANES
    return width


def block_ends(delta, act, gate_in, d_gated, b_wide, c_wide, a_mat):
    segs, length, inner = delta.shape
    states = a_mat.shape[0]
    width = widest(inner, 768)
    tokens = pl.BlockSpec((1, length, width), lambda s, e: (s, 0, e))
    wide = pl.BlockSpec((1, length, states, LANES), lambda s, e: (s, 0, 0, 0))
    state = pl.BlockSpec((1, states, width), lambda s, e: (s, 0, e))
    shape = jax.ShapeDtypeStruct((segs, states, inner), F32)
    return pl.pallas_call(
        ends_kernel,
        grid=(segs, inner // width),
        in_specs=[tokens] * 4 + [wide, wide, pl.BlockSpec((states, width), lambda s, e: (0, e))],
        out_specs=[state, state],
        out_shape=[shape, shape],
        scratch_shapes=[pltpu.VMEM((1, length, width), F32)] * 2,
        compiler_params=pltpu.CompilerParams(vmem_limit_bytes=VMEM_BYTES),
        cost_estimate=pl.CostEstimate(
            flops=9 * delta.size * states, bytes_accessed=12 * delta.size, transcendentals=delta.size * states
        ),
        name="block_ends",
    )(delta, act, gate_in, d_gated, b_wide, c_wide, a_mat)


def scan_kernel(
    hosted, n_blocks_static, n_ticks, d_ref, act_ref, gate_ref, dg_ref, b_ref, c_ref, c_diag, b_diag, ones_ref, a_ref, skip_ref, start_ref, end_ref, first_ref,
    gated_ref, dgate_ref, dpre_ref, dact_ref, db_ref, dc_ref, da_ref, sums_ref, gated_all, gate_all, first_all,
    history, drive, up, low_a, low_b, through_a, through_b, db_acc, dc_acc, sum_acc,
    gated_out, gate_out, gated_sent, gated_got, gate_sent, gate_got, own_sem, first_sent, first_got,
    near_got, relay_sent, relay_got,
):
    states = a_ref.shape[0]
    length, width = d_ref.shape[1:]
    tiles, chunks = width // LANES, length // CHUNK
    span = math.gcd(width, 256)
    parts = width // span
    rate = [a_ref[:, column(j)] * LOG2E for j in range(tiles)]
    seg, block, n_blocks = pl.program_id(0), pl.program_id(1), pl.num_programs(1)
    n_dp, n_seq = lax.axis_size("dp"), lax.axis_size("seq")
    my_dp, my_seq = lax.axis_index("dp"), lax.axis_index("seq")
    tick = seg * n_blocks + block
    slot = lax.rem(tick, 2)
    channels = n_blocks_static * width // n_seq
    owners = width // channels if hosted else 0
    relayed = n_dp == 4

    first_own = pltpu.make_async_copy(first_ref, first_all, first_got.at[0])
    first_far = pltpu.make_async_remote_copy(
        src_ref=first_all, dst_ref=first_all, send_sem=first_sent.at[0], recv_sem=first_got.at[0],
        device_id={"seq": jnp.minimum(my_seq + 1, n_seq - 1)}, device_id_type=MESH,
    )

    @pl.when(tick == 0)
    def _():
        barrier = pltpu.get_barrier_semaphore()
        for p in range(1, n_dp):
            pl.semaphore_signal(barrier, inc=1, device_id={"dp": lax.rem(my_dp + p, n_dp)}, device_id_type=MESH)
        for p in range(1, n_seq):
            pl.semaphore_signal(barrier, inc=1, device_id={"seq": lax.rem(my_seq + p, n_seq)}, device_id_type=MESH)
        pl.semaphore_wait(barrier, n_dp + n_seq - 2)

        @pl.when(my_seq == 0)
        def _():
            first_own.start()

    @pl.when(tick == jnp.minimum(my_seq * max(1, n_ticks // n_seq), n_ticks - 1))
    def _():
        @pl.when(my_seq == 0)
        def _():
            first_own.wait()

        @pl.when(my_seq != 0)
        def _():
            first_far.wait_recv()

        @pl.when(my_seq != n_seq - 1)
        def _():
            first_far.start()

    def gated_copies(s, e, slot):
        at = (my_dp, s, slice(None), pl.ds(pl.multiple_of(e * width, LANES), width))
        own = pltpu.make_async_copy(gated_out.at[slot], gated_all.at[at], own_sem.at[slot, 0])
        if relayed:
            ids = [(my_dp ^ (1 + way), near_got.at[way, s * n_blocks + e], way) for way in range(2)]
        else:
            ids = [(lax.rem(my_dp + p, n_dp), gated_got.at[my_dp], p) for p in range(1, n_dp)]
        far = [
            pltpu.make_async_remote_copy(
                src_ref=gated_out.at[slot], dst_ref=gated_all.at[at],
                send_sem=gated_sent.at[slot, p], recv_sem=got,
                device_id={"dp": peer}, device_id_type=MESH,
            )
            for peer, got, p in ids
        ]
        return own, far

    def passed(s, e, way):
        rows = slice(way * (length // 2), (way + 1) * (length // 2))
        at = (my_dp ^ (1 + way), s, rows, pl.ds(pl.multiple_of(e * width, LANES), width))
        return pltpu.make_async_remote_copy(
            src_ref=gated_all.at[at], dst_ref=gated_all.at[at],
            send_sem=relay_sent.at[way, s * n_blocks + e], recv_sem=relay_got.at[way],
            device_id={"dp": my_dp ^ (2 - way)}, device_id_type=MESH,
        )

    def relay(t):
        s, e = t // n_blocks, lax.rem(t, n_blocks)
        for way in range(2):
            peer = my_dp ^ (1 + way)
            at = (peer, s, slice(None), pl.ds(pl.multiple_of(e * width, LANES), width))
            pltpu.make_async_remote_copy(
                src_ref=gated_out.at[0], dst_ref=gated_all.at[at],
                send_sem=gated_sent.at[0, way], recv_sem=near_got.at[way, t],
                device_id={"dp": peer}, device_id_type=MESH,
            ).wait_recv()
            passed(s, e, way).start()

    def gate_copies(s, e, slot):
        for q in range(owners):
            owner = e * owners + q
            source = gate_out.at[slot, :, q * channels : (q + 1) * channels]
            own = pltpu.make_async_copy(source, gate_all.at[my_seq, s], own_sem.at[slot, 1 + q])
            far = pltpu.make_async_remote_copy(
                src_ref=source, dst_ref=gate_all.at[my_seq, s],
                send_sem=gate_sent.at[slot, q], recv_sem=gate_got.at[my_seq],
                device_id={"seq": owner}, device_id_type=MESH,
            )
            yield owner, own, far

    def send(s, e, slot):
        own, far = gated_copies(s, e, slot)
        own.start()
        for copy in far:
            copy.start()
        for owner, own, far in gate_copies(s, e, slot):
            pl.when(owner == my_seq)(own.start)
            pl.when(owner != my_seq)(far.start)

    def drain(s, e, slot):
        own, far = gated_copies(s, e, slot)
        own.wait()
        for copy in far:
            copy.wait_send()
        for owner, own, far in gate_copies(s, e, slot):
            pl.when(owner == my_seq)(own.wait)
            pl.when(owner != my_seq)(far.wait_send)

    @pl.when(tick >= 2)
    def _():
        drain((tick - 2) // n_blocks, lax.rem(tick - 2, n_blocks), slot)

    history[0:states, :] = start_ref[0]
    drive[0] = d_ref[0] * act_ref[0].astype(F32)
    gate_block = gate_ref[0]
    up[0] = dg_ref[0] * (gate_block * jax.nn.sigmoid(gate_block))
    sum_acc[...] = jnp.zeros_like(sum_acc)

    def rows_of(i):
        return pl.ds(pl.multiple_of(i * CHUNK, CHUNK), CHUNK)

    def kept(i, r):
        return pl.ds(pl.multiple_of((i * CHUNK + r) * states, states), states)

    def sum_y(i, low, part):
        at, rows = slice(part * span, (part + 1) * span), rows_of(i)
        produced = jnp.dot(c_diag[0, i], low[:, at], preferred_element_type=F32)
        scanned = produced + skip_ref[:, at] * act_ref[0, rows, at].astype(F32)
        gate = gate_ref[0, rows, at]
        sigmoid = jax.nn.sigmoid(gate)
        gated = (scanned * (gate * sigmoid)).astype(BF16)
        slope = sigmoid * (1.0 + gate * (1.0 - sigmoid))
        d_gate = (dg_ref[0, rows, at] * scanned * slope).astype(BF16)
        gated_ref[0, rows, at] = gated
        dgate_ref[0, rows, at] = d_gate
        gated_out[slot, rows, at] = gated
        if hosted:
            gate_out[slot, rows, at] = d_gate

    def forward(i, h, low, before, low_before):
        rows = rows_of(i)
        waiting = list(range(parts))
        for r in range(CHUNK):
            b = b_ref[0, i * CHUNK + r]
            for j in range(tiles):
                decay = jnp.exp2(spread_row(d_ref, rows, r, j, states) * rate[j])
                h[j] = h[j] * decay + spread_row(drive, rows, r, j, states) * b
                history[kept(i, r + 1), column(j)] = h[j]
                low[r * states : (r + 1) * states, column(j)] = h[j].astype(BF16)
            if waiting and r % max(1, CHUNK // parts) == 1:
                sum_y(before, low_before, waiting.pop(0))
        for part in waiting:
            sum_y(before, low_before, part)
        return h

    def forward_pair(pair, carry):
        h = forward(2 * pair, list(carry), low_a, jnp.maximum(2 * pair - 1, 0), low_b)
        return tuple(forward(2 * pair + 1, h, low_b, 2 * pair, low_a))

    lax.fori_loop(0, chunks // 2, forward_pair, tuple(start_ref[0, :, column(j)] for j in range(tiles)))
    for part in range(parts):
        sum_y(chunks - 1, low_b, part)
    send(seg, block, slot)
    if relayed:

        @pl.when(tick >= 1)
        def _():
            relay(tick - 1)

    @pl.when(pl.program_id(1) == 0)
    def _():
        db_acc[...] = jnp.zeros_like(db_acc)
        dc_acc[...] = jnp.zeros_like(dc_acc)

    def sum_back(i, low, through, part, count=None):
        at, rows = slice(part * span, (part + 1) * span), rows_of(i)
        d_drive = jnp.dot(b_diag[0, i], low[:, at], preferred_element_type=F32)
        d_rate = jnp.dot(ones_ref[...], through[:, at], preferred_element_type=F32)
        delta, act, d_scanned = d_ref[0, rows, at], act_ref[0, rows, at].astype(F32), up[0, rows, at]
        near = delta * (1.0 - delta * (0.5 - delta * (1.0 / 6.0 - delta * (1.0 / 24.0))))
        slope = jnp.where(delta < 0.03, near, 1.0 - jnp.exp(-delta))
        d_pre = (LN2 * d_rate + d_drive * act) * slope
        dpre_ref[0, rows, at] = d_pre.astype(BF16)
        dact_ref[0, rows, at] = skip_ref[:, at] * d_scanned + d_drive * delta
        if count is None:
            sum_acc[0, :, at] += d_pre
            sum_acc[1, :, at] += d_scanned * act
        else:
            sum_acc[0, :, at] += jnp.where(count, d_pre, 0.0)
            sum_acc[1, :, at] += jnp.where(count, d_scanned * act, 0.0)

    def backward(i, lam, da, low, through, before, low_before, through_before, count=None):
        rows = rows_of(i)
        waiting = list(range(parts))
        for r in reversed(range(CHUNK)):
            c = c_ref[0, i * CHUNK + r]
            db = dc = None
            for j in range(tiles):
                step = spread_row(d_ref, rows, r, j, states)
                upstream = spread_row(up, rows, r, j, states)
                adjoint = lam[j] + upstream * c
                db_j = adjoint * spread_row(drive, rows, r, j, states)
                dc_j = upstream * history[kept(i, r + 1), column(j)]
                db, dc = (db_j, dc_j) if db is None else (db + db_j, dc + dc_j)
                low[r * states : (r + 1) * states, column(j)] = adjoint.astype(BF16)
                lam[j] = adjoint * jnp.exp2(step * rate[j])
                flow = lam[j] * history[kept(i, r), column(j)]
                through[r * states : (r + 1) * states, column(j)] = (flow * rate[j]).astype(BF16)
                da[j] = da[j] + flow * step
            db_acc[i * CHUNK + r] += db
            dc_acc[i * CHUNK + r] += dc
            if waiting and (CHUNK - 1 - r) % max(1, CHUNK // parts) == 1:
                sum_back(before, low_before, through_before, waiting.pop(0), count)
        for part in waiting:
            sum_back(before, low_before, through_before, part, count)
        return lam, da

    def backward_pair(pair, carry):
        lam, da = (list(part) for part in carry)
        i = chunks - 1 - 2 * pair
        lam, da = backward(i, lam, da, low_a, through_a, jnp.minimum(i + 1, chunks - 1), low_b, through_b, pair > 0)
        lam, da = backward(i - 1, lam, da, low_b, through_b, i, low_a, through_a)
        return tuple(lam), tuple(da)

    zeros = tuple(jnp.zeros((states, LANES), F32) for _ in range(tiles))
    _, da = lax.fori_loop(
        0, chunks // 2, backward_pair, (tuple(end_ref[0, :, column(j)] for j in range(tiles)), zeros)
    )
    for part in range(parts):
        sum_back(0, low_b, through_b, part)
    for j in range(tiles):
        da_ref[0, :, column(j)] = da[j]
    sums_ref[0, 0:1, :] = jnp.sum(sum_acc[0], axis=0, keepdims=True)
    sums_ref[0, 1:2, :] = jnp.sum(sum_acc[1], axis=0, keepdims=True)
    sums_ref[0, 2:8, :] = jnp.zeros((6, width), F32)

    @pl.when(pl.program_id(1) == pl.num_programs(1) - 1)
    def _():
        db_ref[0] = jnp.sum(db_acc[...], axis=-1)
        dc_ref[0] = jnp.sum(dc_acc[...], axis=-1)

    @pl.when(tick == pl.num_programs(0) * n_blocks - 1)
    def _():
        drain((tick - 1) // n_blocks, lax.rem(tick - 1, n_blocks), 1 - slot)
        if relayed:
            relay(tick)
        drain(seg, block, slot)
        if relayed:

            def finish_relay(t, nothing):
                for way in range(2):
                    passed(t // n_blocks_static, lax.rem(t, n_blocks_static), way).wait_send()
                return nothing

            lax.fori_loop(0, n_ticks, finish_relay, 0)
            across = my_dp ^ 3
            for way in range(2):
                at = (across, slice(None), slice(way * (length // 2), (way + 1) * (length // 2)))
                pltpu.make_async_remote_copy(
                    src_ref=gated_all.at[at], dst_ref=gated_all.at[at],
                    send_sem=gated_sent.at[0, 0], recv_sem=relay_got.at[way],
                    device_id={"dp": across}, device_id_type=MESH,
                ).wait_recv()
        for p in range(1, 1 if relayed else n_dp):
            source = lax.rem(my_dp + p, n_dp)
            pltpu.make_async_remote_copy(
                src_ref=gated_all.at[source], dst_ref=gated_all.at[source],
                send_sem=gated_sent.at[0, 0], recv_sem=gated_got.at[source],
                device_id={"dp": source}, device_id_type=MESH,
            ).wait_recv()

        @pl.when(my_seq != n_seq - 1)
        def _():
            first_far.wait_send()

        for p in range(1, n_seq if hosted else 1):
            source = lax.rem(my_seq + p, n_seq)
            pltpu.make_async_remote_copy(
                src_ref=gate_all.at[source], dst_ref=gate_all.at[source],
                send_sem=gate_sent.at[0, 0], recv_sem=gate_got.at[source],
                device_id={"seq": source}, device_id_type=MESH,
            ).wait_recv()


def scan_both(delta, act, gate_in, d_gated, b_wide, c_wide, c_diag, b_diag, ones_diag, a_mat, d_skip, start, end, first):
    segs, length, inner = delta.shape
    states = a_mat.shape[0]
    width = widest(inner, 1536)
    tokens = pl.BlockSpec((1, length, width), lambda s, e: (s, 0, e))
    wide = pl.BlockSpec((1, length, states, LANES), lambda s, e: (s, 0, 0, 0))
    diag = pl.BlockSpec((1,) + c_diag.shape[1:], lambda s, e: (s, 0, 0, 0))
    state = pl.BlockSpec((1, states, width), lambda s, e: (s, 0, e))
    narrow = pl.BlockSpec((1, length, states), lambda s, e: (s, 0, 0))
    by_token = jax.ShapeDtypeStruct((segs, length, inner), F32)
    by_token_low = jax.ShapeDtypeStruct((segs, length, inner), BF16)
    by_state = jax.ShapeDtypeStruct((segs, length, states), F32)
    low = pltpu.VMEM((CHUNK * states, width), BF16)
    lanes = pltpu.VMEM((length, states, LANES), F32)
    n_dp, n_seq = lax.axis_size("dp"), lax.axis_size("seq")
    channels = inner // n_seq
    hosted = aligned(inner)
    dma = pltpu.SemaphoreType.DMA
    out = pltpu.VMEM((2, length, width), BF16)
    return pl.pallas_call(
        functools.partial(scan_kernel, hosted, inner // width, segs * (inner // width)),
        grid=(segs, inner // width),
        in_specs=[
            tokens, tokens, tokens, tokens, wide, wide, diag, diag,
            pl.BlockSpec(ones_diag.shape, lambda s, e: (0, 0)),
            pl.BlockSpec((states, width), lambda s, e: (0, e)),
            pl.BlockSpec((1, width), lambda s, e: (0, e)),
            state, state,
            pl.BlockSpec(memory_space=pl.ANY),
        ],
        out_specs=[
            tokens, tokens, tokens, tokens, narrow, narrow, state,
            pl.BlockSpec((1, 8, width), lambda s, e: (s, 0, e)),
            pl.BlockSpec(memory_space=pl.ANY),
            pl.BlockSpec(memory_space=pl.ANY),
            pl.BlockSpec(memory_space=pl.ANY),
        ],
        out_shape=[
            by_token_low, by_token_low, by_token_low, by_token, by_state, by_state,
            jax.ShapeDtypeStruct((segs, states, inner), F32),
            jax.ShapeDtypeStruct((segs, 8, inner), F32),
            jax.ShapeDtypeStruct((n_dp, segs, length, inner), BF16),
            jax.ShapeDtypeStruct((n_seq, segs, length, channels), BF16),
            jax.ShapeDtypeStruct(first.shape, F32),
        ],
        scratch_shapes=[
            pltpu.VMEM(((length + 1) * states, width), F32),
            pltpu.VMEM((1, length, width), F32),
            pltpu.VMEM((1, length, width), F32),
            low, low, low, low, lanes, lanes,
            pltpu.VMEM((2, CHUNK, width), F32),
            out, out,
            dma((2, n_dp)), dma((n_dp,)), dma((2, n_seq)), dma((n_seq,)), dma((2, 1 + n_seq)),
            dma((1,)), dma((1,)),
            dma((2, segs * (inner // width))), dma((2, segs * (inner // width))), dma((2,)),
        ],
        compiler_params=pltpu.CompilerParams(
            collective_id=2, has_side_effects=True, vmem_limit_bytes=VMEM_BYTES
        ),
        cost_estimate=pl.CostEstimate(
            flops=20 * delta.size * states, bytes_accessed=24 * delta.size, transcendentals=2 * delta.size * states
        ),
        name="scan_both",
    )(delta, act, gate_in, d_gated, b_wide, c_wide, c_diag, b_diag, ones_diag, a_mat, d_skip[None], start, end, first)


def finish_kernel(
    conv_hbm, gate_hbm, columns_hbm, normed_hbm, proj_hbm, tokens_hbm, cot_hbm, small_hbm, halo_hbm, gain_ref,
    d_tokens, d_in, small_out, halo_out,
    conv, gate, gate_columns, conv_columns, normed, proj, tokens, cot, small, d_normed,
    partial, arrived, placed, small_dp, small_mid, small_seq,
    load, normed_load, proj_load, swap_sent, swap_got, swap_own, add_sent, add_got, put_sent, put_got, put_own,
    copy_sent, copy_got, mid_sent, mid_got, far_sent, far_got, last_sent, last_got, halo_sent, halo_got,
):
    n_dp, n_seq = lax.axis_size("dp"), lax.axis_size("seq")
    my_dp, my_seq = lax.axis_index("dp"), lax.axis_index("seq")
    half = n_seq // 2
    count, inner = conv_hbm.shape
    width = tokens.shape[1]
    channels = inner // n_seq
    chunks = channels // LANES
    rows_dp = width // n_dp
    rows_small = small_hbm.shape[0] // n_dp
    gain_rows = small_mid.shape[0] - rows_small
    dp_peers = [lax.rem(my_dp + p, n_dp) for p in range(n_dp)]
    seq_peers = [lax.rem(my_seq + p, n_seq) for p in range(n_seq)]

    def remote(src, dst, sent, got, **to):
        return pltpu.make_async_remote_copy(
            src_ref=src, dst_ref=dst, send_sem=sent, recv_sem=got, device_id=to, device_id_type=MESH
        )

    loads = [
        pltpu.make_async_copy(src, dst, load.at[k])
        for k, (src, dst) in enumerate(
            [(columns_hbm, gate_columns), (conv_hbm, conv), (gate_hbm, gate), (tokens_hbm, tokens), (cot_hbm, cot),
             (small_hbm.at[pl.ds(pl.multiple_of(my_dp * rows_small, 16), rows_small)], small)]
        )
    ]
    load_columns, load_conv, load_gate, load_tokens, load_cot, load_small = loads
    load_normed = [pltpu.make_async_copy(normed_hbm.at[s], normed.at[s], normed_load.at[s]) for s in range(n_seq)]
    depth = proj.shape[2]

    def load_proj(k):
        return pltpu.make_async_copy(proj_hbm.at[:, k * depth : (k + 1) * depth], proj.at[k % 2], proj_load.at[k % 2])

    load_columns.start()
    for copy in load_normed:
        copy.start()
    load_conv.start()
    load_proj(0).start()
    for copy in (load_gate, load_tokens, load_cot, load_small):
        copy.start()

    barrier = pltpu.get_barrier_semaphore()
    for p in range(1, n_dp):
        pl.semaphore_signal(barrier, inc=1, device_id={"dp": dp_peers[p]}, device_id_type=MESH)
    for p in range(1, n_seq):
        pl.semaphore_signal(barrier, inc=1, device_id={"seq": seq_peers[p]}, device_id_type=MESH)
    pl.semaphore_wait(barrier, n_dp + n_seq - 2)

    def column_of(device, c):
        return pl.ds(pl.multiple_of(device * channels + c * LANES, LANES), LANES)

    def swap(c, p):
        return remote(
            conv_hbm.at[:, column_of(seq_peers[p], c)], conv_columns.at[c, my_seq],
            swap_sent.at[c, p], swap_got.at[c, my_seq], seq=seq_peers[p],
        )

    own_swaps = [
        pltpu.make_async_copy(conv_hbm.at[:, column_of(my_seq, c)], conv_columns.at[c, my_seq], swap_own.at[c])
        for c in range(chunks)
    ]

    def start_swap(c):
        own_swaps[c].start()
        for p in range(1, n_seq):
            swap(c, p).start()

    start_swap(0)

    def halo(p):
        return remote(halo_hbm, halo_out, halo_sent.at[p], halo_got.at[0], seq=p)

    halo_own = pltpu.make_async_copy(halo_hbm, halo_out, halo_got.at[0])

    @pl.when(my_seq == 0)
    def _():
        halo_own.start()
        for p in range(1, n_seq):
            halo(p).start()

    def small_rows(device):
        return pl.ds(pl.multiple_of(device * rows_small, 16), rows_small)

    def small_add(p):
        return remote(
            small_hbm.at[small_rows(dp_peers[p])], small_dp.at[my_dp], mid_sent.at[p], mid_got.at[my_dp], dp=dp_peers[p]
        )

    for p in range(1, n_dp):
        small_add(p).start()
    def product(c, columns):
        tile = 768 if width % 768 == 0 else 256

        def some_rows(r, nothing):
            at = pl.ds(pl.multiple_of(r * tile, tile), tile)
            total = jnp.dot(normed[0, at, :], columns(0), preferred_element_type=F32)
            for s in range(1, n_seq):
                total += jnp.dot(normed[s, at, :], columns(s), preferred_element_type=F32)
            partial[c, at, :] = total.astype(BF16)
            return nothing

        lax.fori_loop(0, width // tile, some_rows, 0)

    def rows_of(device):
        return pl.ds(pl.multiple_of(device * rows_dp, 16), rows_dp)

    def add(c, p):
        return remote(
            partial.at[c, rows_of(dp_peers[p])], arrived.at[c, my_dp], add_sent.at[c, p], add_got.at[c, my_dp],
            dp=dp_peers[p],
        )

    def scatter(c):
        for p in range(1, n_dp):
            add(c, p).start()

    def place(c):
        k, is_gate = c % chunks, c < chunks
        keeper = my_seq // 2 + (half if is_gate else 0)
        side = lax.rem(my_seq, 2)
        at = (rows_of(my_dp), pl.ds(pl.multiple_of(side * channels + k * LANES, LANES), LANES))
        own = pltpu.make_async_copy(placed.at[c], d_in.at[at], put_own.at[c])
        far = remote(placed.at[c], d_in.at[at], put_sent.at[c], put_got.at[k, side], seq=keeper)
        return keeper, own, far

    def gather_add(c):
        total = partial[c, rows_of(my_dp), :].astype(F32)
        for p in range(1, n_dp):
            remote(
                partial.at[c, rows_of(my_dp)], arrived.at[c, dp_peers[p]], add_sent.at[c, p],
                add_got.at[c, dp_peers[p]], dp=dp_peers[p],
            ).wait_recv()
            total += arrived[c, dp_peers[p]].astype(F32)
        placed[c] = total.astype(BF16)
        keeper, own, far = place(c)
        pl.when(keeper == my_seq)(own.start)
        pl.when(keeper != my_seq)(far.start)

    def spread(k, side, p):
        at = (rows_of(my_dp), slice(side * channels + k * LANES, side * channels + (k + 1) * LANES))
        return remote(
            d_in.at[at], d_in.at[at], copy_sent.at[k, side, p], copy_got.at[k, side, my_dp], dp=dp_peers[p]
        )

    def pass_on(c):
        k, is_gate = c % chunks, c < chunks

        @pl.when((my_seq >= half) == is_gate)
        def _():
            for side in range(2):
                source = 2 * lax.rem(my_seq, half) + side
                at = (rows_of(my_dp), slice(side * channels + k * LANES, side * channels + (k + 1) * LANES))

                @pl.when(source == my_seq)
                def _():
                    place(c)[1].wait()

                @pl.when(source != my_seq)
                def _():
                    remote(placed.at[c], d_in.at[at], put_sent.at[c], put_got.at[k, side], seq=source).wait_recv()

                for p in range(1, n_dp):
                    spread(k, side, p).start()

    load_columns.wait()
    for copy in load_normed:
        copy.wait()
    for c in range(chunks):
        product(c, lambda s, c=c: gate_columns[s, :, c * LANES : (c + 1) * LANES])
        scatter(c)
    if chunks > 1:
        start_swap(1)

    load_conv.wait()
    load_gate.wait()
    steps = 2 * inner // depth
    for k in range(steps):
        if k + 1 < steps:
            load_proj(k + 1).start()
        load_proj(k).wait()
        source, at = (conv, k * depth) if k * depth < inner else (gate, k * depth - inner)

        def some_columns(n, nothing, k=k, source=source, at=at):
            cols = pl.ds(pl.multiple_of(n * 256, 256), 256)
            term = lax.dot_general(
                source[:, at : at + depth], proj[k % 2, cols, :], (((1,), (1,)), ((), ())), preferred_element_type=F32
            )
            d_normed[:, cols] = term if k == 0 else d_normed[:, cols] + term
            return nothing

        lax.fori_loop(0, width // 256, some_columns, 0)
        if k == steps // 2:
            for c in range(chunks):
                gather_add(c)
            for c in range(2, chunks):
                start_swap(c)

    load_tokens.wait()
    load_cot.wait()
    gain = gain_ref[...]

    def some_tokens(r, total):
        at = pl.ds(pl.multiple_of(r * 32, 32), 32)
        token = tokens[at, :].astype(F32)
        inverse = lax.rsqrt(jnp.mean(token * token, axis=-1, keepdims=True) + EPS)
        scaled = d_normed[at, :] * gain
        mean = jnp.mean(scaled * token, axis=-1, keepdims=True)
        d_tokens[at, :] = cot[at, :].astype(F32) + inverse * scaled - token * (inverse * inverse * inverse * mean)
        return total + jnp.sum(d_normed[at, :] * token * inverse, axis=0, keepdims=True)

    d_gain = lax.fori_loop(0, count // 32, some_tokens, jnp.zeros((1, width), F32))
    load_small.wait()
    gains = jnp.concatenate([d_gain[:, r * channels : (r + 1) * channels] for r in range(width // channels)], axis=0)
    gains = jnp.pad(gains, ((0, gain_rows - width // channels), (0, 0)))
    for s in range(n_seq):
        small_mid[rows_small:, s * channels : (s + 1) * channels] = gains.astype(BF16)
    for c in range(chunks):
        pass_on(c)

    total = small[...].astype(F32)
    for p in range(1, n_dp):
        remote(
            small, small_dp.at[dp_peers[p]], mid_sent.at[p], mid_got.at[dp_peers[p]],
            dp=dp_peers[p],
        ).wait_recv()
        total += small_dp[dp_peers[p]].astype(F32)
    small_mid[0:rows_small, :] = total.astype(BF16)

    def small_swap(p):
        at = pl.ds(pl.multiple_of(seq_peers[p] * channels, LANES), channels)
        return remote(
            small_mid.at[:, at], small_seq.at[my_seq], far_sent.at[p], far_got.at[my_seq], seq=seq_peers[p]
        )

    for p in range(1, n_seq):
        small_swap(p).start()

    def convolved(c):
        own_swaps[c].wait()
        for p in range(1, n_seq):
            remote(
                conv_hbm.at[:, column_of(my_seq, c)], conv_columns.at[c, seq_peers[p]], swap_sent.at[c, p],
                swap_got.at[c, seq_peers[p]], seq=seq_peers[p],
            ).wait_recv()
        product(chunks + c, lambda s: conv_columns[c, s])
        scatter(chunks + c)

    convolved(0)
    gather_add(chunks)
    for c in range(1, chunks):
        convolved(c)
        pass_on(chunks + c - 1)
        gather_add(chunks + c)
    total = small_mid[:, pl.ds(pl.multiple_of(my_seq * channels, LANES), channels)].astype(F32)
    for p in range(1, n_seq):
        remote(
            small_mid.at[:, 0:channels], small_seq.at[seq_peers[p]], far_sent.at[p], far_got.at[seq_peers[p]],
            seq=seq_peers[p],
        ).wait_recv()
        total += small_seq[seq_peers[p]].astype(F32)
    small_out[my_dp] = total.astype(BF16)

    def small_spread(p):
        return remote(small_out.at[my_dp], small_out.at[my_dp], last_sent.at[p], last_got.at[my_dp], dp=dp_peers[p])

    for p in range(1, n_dp):
        small_spread(p).start()
    pass_on(2 * chunks - 1)

    for c in range(chunks):
        for p in range(1, n_seq):
            swap(c, p).wait_send()
    for c in range(2 * chunks):
        for p in range(1, n_dp):
            add(c, p).wait_send()
        keeper, own, far = place(c)

        @pl.when(keeper != my_seq)
        def _(far=far):
            far.wait_send()

    for k in range(chunks):
        for side in range(2):
            at = slice(side * channels + k * LANES, side * channels + (k + 1) * LANES)
            for p in range(1, n_dp):
                spread(k, side, p).wait_send()
                peer = dp_peers[p]
                remote(
                    d_in.at[rows_of(peer), at], d_in.at[rows_of(peer), at], copy_sent.at[k, side, p],
                    copy_got.at[k, side, peer], dp=peer,
                ).wait_recv()
    for p in range(1, n_dp):
        small_add(p).wait_send()
        small_spread(p).wait_send()
        peer = dp_peers[p]
        remote(
            small_out.at[peer], small_out.at[peer], last_sent.at[p], last_got.at[peer], dp=peer
        ).wait_recv()
    for p in range(1, n_seq):
        small_swap(p).wait_send()

    @pl.when(my_seq == 0)
    def _():
        halo_own.wait()
        for p in range(1, n_seq):
            halo(p).wait_send()

    @pl.when(my_seq != 0)
    def _():
        halo(1).wait_recv()


def finish(d_conv_in, d_gate, gate_columns, normed_all, in_proj, tokens, cot, small, halo_grad, norm_gain):
    n_dp, n_seq = lax.axis_size("dp"), lax.axis_size("seq")
    count, inner = d_conv_in.shape
    width = tokens.shape[1]
    channels = inner // n_seq
    chunks = channels // LANES
    rows = small.shape[0] // n_dp
    gain_rows = -(-width // channels // 16) * 16
    depth = 1024 if inner % 1024 == 0 else LANES
    dma = pltpu.SemaphoreType.DMA
    vmem = pltpu.VMEM
    anywhere = pl.BlockSpec(memory_space=pl.ANY)
    inside = pl.BlockSpec(memory_space=pltpu.VMEM)
    return pl.pallas_call(
        finish_kernel,
        in_specs=[anywhere] * 9 + [inside],
        out_specs=[inside, anywhere, inside, anywhere],
        out_shape=[
            jax.ShapeDtypeStruct((count, width), F32),
            jax.ShapeDtypeStruct((width, 2 * channels), BF16),
            jax.ShapeDtypeStruct((n_dp, rows + gain_rows, channels), BF16),
            jax.ShapeDtypeStruct(halo_grad.shape, F32),
        ],
        scratch_shapes=[
            vmem((count, inner), BF16), vmem((count, inner), BF16),
            vmem((n_seq, count, channels), BF16), vmem((chunks, n_seq, count, LANES), BF16),
            vmem((n_seq, width, count), BF16), vmem((2, width, depth), BF16),
            vmem((count, width), BF16), vmem((count, width), BF16), vmem((rows, inner), BF16),
            vmem((count, width), F32),
            vmem((2 * chunks, width, LANES), BF16), vmem((2 * chunks, n_dp, width // n_dp, LANES), BF16),
            vmem((2 * chunks, width // n_dp, LANES), BF16),
            vmem((n_dp, rows, inner), BF16), vmem((rows + gain_rows, inner), BF16),
            vmem((n_seq, rows + gain_rows, channels), BF16),
            dma((6,)), dma((n_seq,)), dma((2,)),
            dma((chunks, n_seq)), dma((chunks, n_seq)), dma((chunks,)),
            dma((2 * chunks, n_dp)), dma((2 * chunks, n_dp)),
            dma((2 * chunks,)), dma((chunks, 2)), dma((2 * chunks,)),
            dma((chunks, 2, n_dp)), dma((chunks, 2, n_dp)),
            dma((n_dp,)), dma((n_dp,)), dma((n_seq,)), dma((n_seq,)), dma((n_dp,)), dma((n_dp,)),
            dma((n_seq,)), dma((1,)),
        ],
        compiler_params=pltpu.CompilerParams(
            collective_id=3, has_side_effects=True, vmem_limit_bytes=60 * 2**20
        ),
        cost_estimate=pl.CostEstimate(
            flops=12 * count * width * inner, bytes_accessed=40 * count * width, transcendentals=0
        ),
        name="finish",
    )(
        d_conv_in, d_gate, gate_columns, normed_all, in_proj, tokens, cot, small, halo_grad, norm_gain[None],
    )


def diagonal_blocks(value):
    segs, length, states = value.shape
    spread = jnp.tile(jnp.eye(states, dtype=BF16), (1, CHUNK))
    tiled = matmul(value.reshape(segs * length, states).astype(BF16), spread)
    mask = jnp.repeat(jnp.eye(CHUNK, dtype=F32), states, axis=1)
    return (tiled.reshape(segs, length // CHUNK, CHUNK, CHUNK * states) * mask).astype(BF16)


def conv_back_kernel(
    d_act_ref, coeff_ref, proj_ref, conv_ref, before_ref, weight_ref, bias_ref,
    d_in_ref, last_ref, halo_ref, sums_ref, padded, d_out,
):
    taps = weight_ref.shape[0]
    halo = taps - 1
    length, width = conv_ref.shape[1:]
    padded[8 - halo : 8, :] = before_ref[0].astype(F32)
    padded[8 : 8 + length, :] = conv_ref[0].astype(F32)
    d_out[length : length + 8, :] = jnp.zeros((8, width), F32)
    coeff = coeff_ref[0]
    for j in range(width // LANES):
        at = column(j)
        weight = [weight_ref[tap : tap + 1, at] for tap in range(taps)]
        inputs = [padded[8 - halo + tap : 8 - halo + tap + length, at] for tap in range(taps)]
        conv_out = bias_ref[:, at] + sum(weight[tap] * inputs[tap] for tap in range(taps))
        d_act = d_act_ref[0, :, at] + matmul_nt(coeff, proj_ref[at, :])
        d_conv = d_act * silu_parts(conv_out)[1]
        d_out[0:length, at] = d_conv
        for tap in range(taps):
            sums_ref[0, tap : tap + 1, at] = jnp.sum(d_conv * inputs[tap], axis=0, keepdims=True)
        sums_ref[0, taps : taps + 1, at] = jnp.sum(d_conv, axis=0, keepdims=True)
        d_in = sum(weight[tap] * d_out[halo - tap : halo - tap + length, at] for tap in range(taps))
        d_in_ref[0, :, at] = d_in.astype(BF16)
        last_ref[0, :, at] = d_in[length - 8 :]
        for row in range(halo):
            halo_ref[0, row : row + 1, at] = sum(
                weight[tap] * d_conv[row - tap : row - tap + 1] for tap in range(row + 1)
            )
    sums_ref[0, taps + 1 :, :] = jnp.zeros((8 - taps - 1, width), F32)


def conv_back(d_act, d_coeffs, x_proj, conv_in, before, conv_weight, conv_bias):
    segs, length, inner = conv_in.shape
    width = widest(inner, 1536)
    taps, halo = conv_weight.shape[0], before.shape[1]
    tokens = pl.BlockSpec((1, length, width), lambda s, e: (s, 0, e))

    def rows(count):
        return pl.BlockSpec((1, count, width), lambda s, e: (s, 0, e))

    return pl.pallas_call(
        conv_back_kernel,
        grid=(segs, inner // width),
        in_specs=[
            tokens,
            pl.BlockSpec((1, length, d_coeffs.shape[2]), lambda s, e: (s, 0, 0)),
            pl.BlockSpec((width, x_proj.shape[1]), lambda s, e: (e, 0)),
            tokens,
            rows(halo),
            pl.BlockSpec((taps, width), lambda s, e: (0, e)),
            pl.BlockSpec((1, width), lambda s, e: (0, e)),
        ],
        out_specs=[tokens, rows(8), rows(halo), rows(8)],
        out_shape=[
            jax.ShapeDtypeStruct((segs, length, inner), BF16),
            jax.ShapeDtypeStruct((segs, 8, inner), F32),
            jax.ShapeDtypeStruct((segs, halo, inner), F32),
            jax.ShapeDtypeStruct((segs, 8, inner), F32),
        ],
        scratch_shapes=[pltpu.VMEM((length + 8, width), F32), pltpu.VMEM((length + 8, width), F32)],
        compiler_params=pltpu.CompilerParams(vmem_limit_bytes=VMEM_BYTES),
        cost_estimate=pl.CostEstimate(
            flops=50 * conv_in.size, bytes_accessed=8 * conv_in.size, transcendentals=conv_in.size
        ),
        name="conv_back",
    )(d_act, d_coeffs, x_proj, conv_in, before, conv_weight, conv_bias[None])


def norm_kernel(token_ref, gain_ref, normed_ref, turned_ref):
    token = token_ref[...].astype(F32)
    inverse = lax.rsqrt(jnp.mean(token * token, axis=-1, keepdims=True) + EPS)
    normed = token * inverse * gain_ref[...]
    normed_ref[...] = normed.astype(BF16)
    turned_ref[...] = normed.T.astype(BF16)


def norm(tokens, norm_gain):
    count, width = tokens.shape
    rows = 128
    return pl.pallas_call(
        norm_kernel,
        grid=(count // rows,),
        in_specs=[pl.BlockSpec((rows, width), lambda r: (r, 0)), pl.BlockSpec((1, width), lambda r: (0, 0))],
        out_specs=[pl.BlockSpec((rows, width), lambda r: (r, 0)), pl.BlockSpec((width, rows), lambda r: (0, r))],
        out_shape=[jax.ShapeDtypeStruct((count, width), BF16), jax.ShapeDtypeStruct((width, count), BF16)],
        compiler_params=pltpu.CompilerParams(vmem_limit_bytes=32 * 2**20),
        name="norm",
    )(tokens, norm_gain[None])


def body(
    tokens, conv_state, entry_state, norm_gain, in_proj, conv_weight, conv_bias, x_proj,
    dt_proj, dt_bias, a_log, d_skip, out_proj, cotangent,
):
    segs, length, width = tokens.shape
    inner = in_proj.shape[1] // 2
    rank, states, taps = dt_proj.shape[0], a_log.shape[0], conv_weight.shape[0]
    halo = taps - 1
    count = segs * length
    n_seq = lax.axis_size("seq")
    mine = lax.axis_index("seq")
    is_first = mine == 0

    def flat(value):
        return value.reshape((count,) + value.shape[2:])

    def split(value):
        return value.reshape((segs, length) + value.shape[1:])

    token_float = flat(tokens).astype(F32)
    inverse = lax.rsqrt(jnp.mean(token_float * token_float, axis=-1, keepdims=True) + EPS)
    normed, normed_turned = norm(flat(tokens), norm_gain)
    cot = flat(cotangent)
    fast = aligned(inner)
    if fast:
        normed_all = lax.all_gather(normed_turned, "seq", axis=0, tiled=False)
    else:
        normed_all = lax.all_gather(normed, "seq", axis=0, tiled=True)
    cot_rows = swap_rows(cot.T, "dp")
    conv_in = matmul(normed, in_proj[:, :inner]).astype(BF16)
    gate_in = matmul(normed, in_proj[:, inner:])
    d_gated = matmul_nt(cot, out_proj)
    conv_in = split(conv_in)
    before = jnp.where(is_first, conv_state, shifted(conv_in[:, length - halo :], "seq", 1))
    padded = jnp.concatenate([before, conv_in], axis=1).astype(F32)
    conv_out = conv_bias + sum(conv_weight[tap] * padded[:, tap : tap + length] for tap in range(taps))
    activated = (conv_out * jax.nn.sigmoid(conv_out)).astype(BF16)
    coeffs = matmul(flat(activated), x_proj)
    dt_low = coeffs[:, :rank].astype(BF16)
    b_in = split(coeffs[:, rank : rank + states])
    c_in = split(coeffs[:, rank + states :])
    pre_delta = matmul(dt_low, dt_proj) + dt_bias
    delta = split(jax.nn.softplus(pre_delta))
    a_mat = -jnp.exp(a_log)
    gate_in, d_gated = split(gate_in), split(d_gated)

    b_wide = jnp.broadcast_to(b_in[..., None], b_in.shape + (LANES,))
    c_wide = jnp.broadcast_to(c_in[..., None], c_in.shape + (LANES,))
    ends, entry_mu = block_ends(delta, activated, gate_in, d_gated, b_wide, c_wide, a_mat)
    total = jnp.sum(delta, axis=1, keepdims=True)
    start, end, first = carry(ends, entry_mu, total, entry_state, a_mat)
    ones_diag = diagonal_blocks(jnp.ones((1, CHUNK, states), F32))[0, 0]
    gated, d_gate, d_pre_low, d_act, d_b, d_c, d_amat, sums, gated_all, gate_columns, d_entry = scan_both(
        delta, activated, gate_in, d_gated, b_wide, c_wide,
        diagonal_blocks(c_in), diagonal_blocks(b_in), ones_diag, a_mat, d_skip, start, end, first,
    )
    gated, d_gate, d_pre_low, d_act = flat(gated), flat(d_gate), flat(d_pre_low), flat(d_act)
    gated_all, normed_all = lax.optimization_barrier((gated_all, normed_all))
    gated_all = gated_all.reshape(-1, inner)
    gate_columns = gate_columns.reshape(n_seq * count, -1)
    if (inner // n_seq) % LANES:
        gate_columns = swap_columns(d_gate, "seq")
    output = token_float + matmul(gated, out_proj)
    out_part = matmul(cot_rows, gated_all).astype(BF16)
    out_part = lax.psum_scatter(out_part, "seq", scatter_dimension=1, tiled=True)
    d_out_proj = lax.all_gather(out_part, "dp", axis=0, tiled=True).T.astype(F32)

    sums = jnp.sum(sums, axis=0)
    d_dt_bias, d_d_skip = sums[0], sums[1]
    d_dt_proj = matmul_tn(dt_low, d_pre_low)
    d_dt_low = matmul_nt(d_pre_low, dt_proj)
    d_coeffs = jnp.concatenate([d_dt_low, flat(d_b), flat(d_c)], axis=-1).astype(BF16)
    d_x_proj = matmul_tn(d_coeffs, flat(activated))
    d_a_log = jnp.sum(d_amat, axis=0) * a_mat
    d_conv_in, last, halo_grad, conv_sums = conv_back(
        split(d_act), split(d_coeffs), x_proj, conv_in, before, conv_weight, conv_bias
    )
    conv_sums = jnp.sum(conv_sums, axis=0)
    d_conv_weight, d_conv_bias = conv_sums[:taps], conv_sums[taps]
    returned = shifted(halo_grad, "seq", -1)
    last = last + jnp.pad(returned, ((0, 0), (last.shape[1] - halo, 0), (0, 0)))
    d_conv_in = lax.dynamic_update_slice_in_dim(d_conv_in, last.astype(BF16), length - last.shape[1], 1)
    d_conv_in = flat(d_conv_in)
    if fast:
        small = jnp.concatenate(
            [
                part.astype(BF16)
                for part in (
                    d_x_proj, d_dt_proj, d_a_log, d_dt_bias[None], d_d_skip[None], d_conv_weight, d_conv_bias[None]
                )
            ],
            axis=0,
        )
        edge_at = 2 * rank + 3 * states + 2
        channels = inner // n_seq
        small = jnp.pad(small, ((0, -small.shape[0] % (16 * lax.axis_size("dp"))), (0, 0)))
        rows = small.shape[0] // lax.axis_size("dp")
        d_tokens, d_in_proj, small, d_conv_state = finish(
            d_conv_in, d_gate, gate_columns.reshape(n_seq, count, channels), normed_all, in_proj, flat(tokens), cot,
            small, halo_grad, norm_gain,
        )
        d_in_proj, small = d_in_proj.astype(F32), small.astype(F32)
        gain = jnp.sum(small[:, rows : rows + width // channels], axis=0)
        small = small[:, :rows].reshape(-1, channels)
        edges = small[edge_at:]
        d_norm_gain = lax.dynamic_index_in_dim(gain.reshape(n_seq, -1), mine, 0, keepdims=False)
    else:
        d_conv_state = from_first(halo_grad, "seq")

        n_dp = lax.axis_size("dp")
        small = jnp.concatenate([d_x_proj, d_dt_proj, d_a_log, d_dt_bias[None], d_d_skip[None]], axis=0)
        small = jnp.pad(small, ((0, -small.shape[0] % 16), (0, 0))).astype(BF16)
        small_columns = swap_columns(small, "seq")
        edges = jnp.concatenate([d_conv_weight, d_conv_bias[None]], axis=0)
        edges = jnp.pad(edges, ((0, -edges.shape[0] % 16), (0, 0))).astype(BF16)
        conv_columns = swap_columns(jnp.concatenate([d_conv_in, edges], axis=0), "seq").reshape(n_seq, -1, inner // n_seq)
        edge_columns = conv_columns[:, count:]
        conv_columns = conv_columns[:, :count].reshape(n_seq * count, -1)

        def blocks(value, axis):
            return value.reshape((lax.axis_size(axis), -1) + value.shape[1:])

        gate_part = sum_scatter(blocks(matmul_tn(normed_all, gate_columns), "dp"), "dp").astype(BF16)
        conv_part = sum_scatter(blocks(matmul_tn(normed_all, conv_columns), "dp"), "dp").astype(BF16)
        half = n_seq // 2
        even = mine % 2 == 0
        straight = [(i, i // 2 + (0 if i % 2 == 0 else half)) for i in range(n_seq)]
        crossed = [(i, i // 2 + (half if i % 2 == 0 else 0)) for i in range(n_seq)]
        first = lax.ppermute(jnp.where(even, conv_part, gate_part), "seq", straight)
        second = lax.ppermute(jnp.where(even, gate_part, conv_part), "seq", crossed)
        low_half = mine < half
        d_in_part = jnp.concatenate(
            [jnp.where(low_half, first, second), jnp.where(low_half, second, first)], axis=1
        )
        d_in_proj = gather_rows(d_in_part, "dp").astype(F32)

        d_normed = matmul_nt(d_conv_in, in_proj[:, :inner]) + matmul_nt(d_gate, in_proj[:, inner:])
        d_norm_gain = jnp.sum(d_normed * token_float * inverse, axis=0)
        scaled = d_normed * norm_gain
        cubed = inverse * inverse * inverse
        d_tokens = (
            cot.astype(F32)
            + inverse * scaled
            - token_float * cubed * jnp.mean(scaled * token_float, axis=-1, keepdims=True)
        )
        gain = sum_scatter(blocks(d_norm_gain, "seq"), "seq")
        channels = inner // n_seq
        per_device = jnp.concatenate(
            [
                jnp.sum(small_columns.reshape(n_seq, -1, channels).astype(F32), axis=0),
                jnp.sum(edge_columns.astype(F32), axis=0),
                jnp.pad(gain, (0, -gain.shape[0] % channels)).reshape(-1, channels),
            ],
            axis=0,
        )
        per_device = per_device.astype(BF16)
        summed = jnp.sum(gather_rows(per_device[None], "dp").astype(F32), axis=0)
        edges = summed[small.shape[0] : small.shape[0] + edges.shape[0]]
        d_norm_gain = summed[small.shape[0] + edges.shape[0] :].reshape(-1)[: gain.shape[0]]
        small = summed

    return (
        split(output),
        split(d_tokens),
        d_conv_state,
        d_entry,
        d_norm_gain,
        d_in_proj,
        edges[:taps],
        edges[taps],
        small[: rank + 2 * states].T,
        small[rank + 2 * states : 2 * rank + 2 * states],
        small[2 * rank + 3 * states],
        small[2 * rank + 2 * states : 2 * rank + 3 * states],
        small[2 * rank + 3 * states + 1],
        d_out_proj,
    )


def solution(mesh):
    by_token, by_segment, whole = P("dp", "seq", None), P("dp", None, None), P()
    return jax.shard_map(
        body,
        mesh=mesh,
        in_specs=(by_token, by_segment, by_segment) + (whole,) * 10 + (by_token,),
        out_specs=(
            by_token, by_token, by_segment, by_segment, P("seq"), P(None, "seq"), P(None, "seq"), P("seq"),
            P("seq", None), P(None, "seq"), P("seq"), P(None, "seq"), P("seq"), P("seq", None),
        ),
        check_vma=False,
    )
```

```python
import functools
import math

import jax
import jax.numpy as jnp
from jax import lax
from jax.experimental import pallas as pl
from jax.experimental.pallas import tpu as pltpu
from jax.sharding import PartitionSpec as P

EPS = 1e-05
LANES = 128
CHUNK = 16
LOG2E = math.log2(math.e)
LN2 = math.log(2.0)
BF16 = jnp.bfloat16
F32 = jnp.float32
VMEM_BYTES = 56 * 2**20


def silu_parts(value):
    sigmoid = jax.nn.sigmoid(value)
    return value * sigmoid, sigmoid * (1.0 + value * (1.0 - sigmoid))


def matmul(left, right):
    return lax.dot_general(left, right, (((1,), (0,)), ((), ())), preferred_element_type=F32)


def matmul_nt(left, right):
    return lax.dot_general(left, right, (((1,), (1,)), ((), ())), preferred_element_type=F32)


def matmul_tn(left, right):
    return lax.dot_general(left, right, (((0,), (0,)), ((), ())), preferred_element_type=F32)


def partner_route(axis, step):
    count = lax.axis_size(axis)
    if count & (count - 1) == 0:
        return [(i, i ^ step) for i in range(count)]
    return [(i, (i + step) % count) for i in range(count)]


def partners(axis, step):
    count, mine = lax.axis_size(axis), lax.axis_index(axis)
    if count & (count - 1) == 0:
        return mine ^ step, mine ^ step
    return (mine + step) % count, (mine + count - step) % count


def swap_columns(block, axis):
    count = lax.axis_size(axis)
    rows, width = block.shape[0], block.shape[1] // count
    gathered = jnp.zeros((count * rows, width), block.dtype)
    for step in range(count):
        target, source = partners(axis, step)
        piece = lax.dynamic_slice_in_dim(block, target * width, width, 1)
        if step:
            piece = lax.ppermute(piece, axis, partner_route(axis, step))
        gathered = lax.dynamic_update_slice_in_dim(gathered, piece, source * rows, 0)
    return gathered


def swap_rows(block, axis):
    count = lax.axis_size(axis)
    rows, width = block.shape[0] // count, block.shape[1]
    gathered = jnp.zeros((rows, count * width), block.dtype)
    for step in range(count):
        target, source = partners(axis, step)
        piece = lax.dynamic_slice_in_dim(block, target * rows, rows, 0)
        if step:
            piece = lax.ppermute(piece, axis, partner_route(axis, step))
        gathered = lax.dynamic_update_slice_in_dim(gathered, piece, source * width, 1)
    return gathered


def sum_scatter(blocks, axis):
    count, mine = lax.axis_size(axis), lax.axis_index(axis)
    if count & (count - 1):
        return lax.psum_scatter(blocks, axis, scatter_dimension=0)
    levels = count.bit_length() - 1
    held = blocks.reshape((2,) * levels + blocks.shape[1:])
    for level in range(levels):
        bit = (mine >> level) & 1
        at = levels - 1 - level
        sent = lax.dynamic_index_in_dim(held, 1 - bit, at, keepdims=False).astype(BF16)
        arrived = lax.ppermute(sent, axis, [(i, i ^ (1 << level)) for i in range(count)])
        held = lax.dynamic_index_in_dim(held, bit, at, keepdims=False).astype(F32) + arrived.astype(F32)
    return held


def gather_rows(block, axis):
    count = lax.axis_size(axis)
    rows = block.shape[0]
    gathered = jnp.zeros((count * rows,) + block.shape[1:], block.dtype)
    for step in range(count):
        _, source = partners(axis, step)
        piece = lax.ppermute(block, axis, partner_route(axis, step)) if step else block
        gathered = lax.dynamic_update_slice_in_dim(gathered, piece, source * rows, 0)
    return gathered


def shifted(block, axis, distance):
    devices = range(lax.axis_size(axis))
    route = [(i - distance, i) for i in devices if i - distance in devices]
    return lax.ppermute(block, axis, route)


def from_first(block, axis):
    count, mine = lax.axis_size(axis), lax.axis_index(axis)
    reach = 1
    while reach < count:
        route = [(i, i + reach) for i in range(min(reach, count - reach))]
        arrived = lax.ppermute(block, axis, route)
        block = jnp.where(mine < reach, block, arrived)
        reach *= 2
    return block


MESH = pl.DeviceIdType.MESH


def carry_kernel(
    pieces, end_ref, mu_ref, total_ref, entry_ref, a_ref, start_ref, lam_ref, first_ref,
    ahead, back, from_left, from_right, sent_right, sent_left, got_left, got_right,
):
    count, mine = lax.axis_size("seq"), lax.axis_index("seq")
    width = end_ref.shape[2] // pieces
    has_left, has_right = mine > 0, mine < count - 1
    left, right = jnp.maximum(mine - 1, 0), jnp.minimum(mine + 1, count - 1)

    barrier = pltpu.get_barrier_semaphore()

    @pl.when(has_left)
    def _():
        pl.semaphore_signal(barrier, inc=1, device_id={"seq": left}, device_id_type=MESH)

    @pl.when(has_right)
    def _():
        pl.semaphore_signal(barrier, inc=1, device_id={"seq": right}, device_id_type=MESH)

    pl.semaphore_wait(barrier, has_left.astype(jnp.int32) + has_right.astype(jnp.int32))

    def at(piece):
        return pl.ds(pl.multiple_of(piece * width, LANES), width)

    def to_right(piece):
        return pltpu.make_async_remote_copy(
            src_ref=ahead.at[:, :, at(piece)], dst_ref=from_left.at[:, :, at(piece)],
            send_sem=sent_right.at[piece], recv_sem=got_left.at[piece],
            device_id={"seq": right}, device_id_type=MESH,
        )

    def to_left(piece):
        return pltpu.make_async_remote_copy(
            src_ref=back.at[:, :, at(piece)], dst_ref=from_right.at[:, :, at(piece)],
            send_sem=sent_left.at[piece], recv_sem=got_right.at[piece],
            device_id={"seq": left}, device_id_type=MESH,
        )

    def decay(piece):
        return jnp.exp(total_ref[:, :, at(piece)] * a_ref[:, at(piece)][None])

    def step(tick, nothing):
        piece = tick - mine

        @pl.when(jnp.logical_and(piece >= 0, piece < pieces))
        def _():
            @pl.when(has_left)
            def _():
                to_right(piece).wait_recv()
                start_ref[:, :, at(piece)] = from_left[:, :, at(piece)].astype(F32)

            @pl.when(jnp.logical_not(has_left))
            def _():
                start_ref[:, :, at(piece)] = entry_ref[:, :, at(piece)]

            @pl.when(has_right)
            def _():
                end = end_ref[:, :, at(piece)] + decay(piece) * start_ref[:, :, at(piece)]
                ahead[:, :, at(piece)] = end.astype(BF16)
                to_right(piece).start()

        other = tick - (count - 1 - mine)

        @pl.when(jnp.logical_and(other >= 0, other < pieces))
        def _():
            @pl.when(has_right)
            def _():
                to_left(other).wait_recv()
                lam_ref[:, :, at(other)] = from_right[:, :, at(other)].astype(F32)

            @pl.when(jnp.logical_not(has_right))
            def _():
                lam_ref[:, :, at(other)] = jnp.zeros(lam_ref.shape[:2] + (width,), F32)

            first = mu_ref[:, :, at(other)] + decay(other) * lam_ref[:, :, at(other)]
            first_ref[:, :, at(other)] = first
            back[:, :, at(other)] = first.astype(BF16)

            @pl.when(has_left)
            def _():
                to_left(other).start()

        return nothing

    lax.fori_loop(0, pieces + count - 1, step, 0)

    def finish(piece, nothing):
        @pl.when(has_right)
        def _():
            to_right(piece).wait_send()

        @pl.when(has_left)
        def _():
            to_left(piece).wait_send()

        return nothing

    lax.fori_loop(0, pieces, finish, 0)


def carry(ends, entry_mu, total, entry_state, a_mat):
    pieces = 4
    while ends.shape[2] % (pieces * LANES):
        pieces -= 1
    shape = jax.ShapeDtypeStruct(ends.shape, F32)
    held = pltpu.VMEM(ends.shape, BF16)
    vmem = pl.BlockSpec(memory_space=pltpu.VMEM)
    return pl.pallas_call(
        functools.partial(carry_kernel, pieces),
        in_specs=[vmem] * 5,
        out_specs=[vmem] * 3,
        out_shape=[shape, shape, shape],
        scratch_shapes=[held] * 4 + [pltpu.SemaphoreType.DMA((pieces,))] * 4,
        compiler_params=pltpu.CompilerParams(
            collective_id=1, has_side_effects=True, vmem_limit_bytes=32 * 2**20
        ),
        name="carry",
    )(ends, entry_mu, total, entry_state, a_mat)


def aligned(inner, axis="seq"):
    channels = inner // lax.axis_size(axis)
    return channels % LANES == 0 and widest(inner, 1536) % channels == 0


def spread_row(ref, rows, at, tile, states):
    row = ref.at[0, rows][at : at + 1, tile * LANES : (tile + 1) * LANES]
    return jnp.broadcast_to(row, (states, LANES))


def column(tile):
    return slice(tile * LANES, (tile + 1) * LANES)


def ends_kernel(d_ref, act_ref, gate_ref, dg_ref, b_ref, c_ref, a_ref, end_ref, mu_ref, drive, up):
    states = a_ref.shape[0]
    length, width = d_ref.shape[1:]
    tiles = width // LANES
    rate = [a_ref[:, column(j)] * LOG2E for j in range(tiles)]
    drive[0] = d_ref[0] * act_ref[0].astype(F32)
    gate = gate_ref[0]
    up[0] = dg_ref[0] * (gate * jax.nn.sigmoid(gate))

    def chunk(i, carry):
        h, p, mu = (list(part) for part in carry)
        rows = pl.ds(pl.multiple_of(i * CHUNK, CHUNK), CHUNK)
        for r in range(CHUNK):
            b, c = b_ref[0, i * CHUNK + r], c_ref[0, i * CHUNK + r]
            for j in range(tiles):
                decay = jnp.exp2(spread_row(d_ref, rows, r, j, states) * rate[j])
                h[j] = h[j] * decay + spread_row(drive, rows, r, j, states) * b
                p[j] = p[j] * decay
                mu[j] = mu[j] + p[j] * (spread_row(up, rows, r, j, states) * c)
        return tuple(h), tuple(p), tuple(mu)

    zeros = tuple(jnp.zeros((states, LANES), F32) for _ in range(tiles))
    ones = tuple(jnp.ones((states, LANES), F32) for _ in range(tiles))
    h, _, mu = lax.fori_loop(0, length // CHUNK, chunk, (zeros, ones, zeros))
    for j in range(tiles):
        end_ref[0, :, column(j)] = h[j]
        mu_ref[0, :, column(j)] = mu[j]


def widest(inner, most):
    width = most
    while inner % width:
        width -= LANES
    return width


def block_ends(delta, act, gate_in, d_gated, b_wide, c_wide, a_mat):
    segs, length, inner = delta.shape
    states = a_mat.shape[0]
    width = widest(inner, 768)
    tokens = pl.BlockSpec((1, length, width), lambda s, e: (s, 0, e))
    wide = pl.BlockSpec((1, length, states, LANES), lambda s, e: (s, 0, 0, 0))
    state = pl.BlockSpec((1, states, width), lambda s, e: (s, 0, e))
    shape = jax.ShapeDtypeStruct((segs, states, inner), F32)
    return pl.pallas_call(
        ends_kernel,
        grid=(segs, inner // width),
        in_specs=[tokens] * 4 + [wide, wide, pl.BlockSpec((states, width), lambda s, e: (0, e))],
        out_specs=[state, state],
        out_shape=[shape, shape],
        scratch_shapes=[pltpu.VMEM((1, length, width), F32)] * 2,
        compiler_params=pltpu.CompilerParams(vmem_limit_bytes=VMEM_BYTES),
        cost_estimate=pl.CostEstimate(
            flops=9 * delta.size * states, bytes_accessed=12 * delta.size, transcendentals=delta.size * states
        ),
        name="block_ends",
    )(delta, act, gate_in, d_gated, b_wide, c_wide, a_mat)


def scan_kernel(
    hosted, n_blocks_static, n_ticks, d_ref, act_ref, gate_ref, dg_ref, b_ref, c_ref, c_diag, b_diag, ones_ref, a_ref, skip_ref, start_ref, end_ref, first_ref,
    gated_ref, dgate_ref, dpre_ref, dact_ref, db_ref, dc_ref, da_ref, sums_ref, gated_all, gate_all, first_all,
    history, drive, up, low_a, low_b, through_a, through_b, db_acc, dc_acc, sum_acc,
    gated_out, gate_out, gated_sent, gated_got, gate_sent, gate_got, own_sem, first_sent, first_got,
    near_got, relay_sent, relay_got,
):
    states = a_ref.shape[0]
    length, width = d_ref.shape[1:]
    tiles, chunks = width // LANES, length // CHUNK
    span = math.gcd(width, 256)
    parts = width // span
    rate = [a_ref[:, column(j)] * LOG2E for j in range(tiles)]
    seg, block, n_blocks = pl.program_id(0), pl.program_id(1), pl.num_programs(1)
    n_dp, n_seq = lax.axis_size("dp"), lax.axis_size("seq")
    my_dp, my_seq = lax.axis_index("dp"), lax.axis_index("seq")
    tick = seg * n_blocks + block
    slot = lax.rem(tick, 2)
    channels = n_blocks_static * width // n_seq
    owners = width // channels if hosted else 0
    relayed = n_dp == 4

    first_own = pltpu.make_async_copy(first_ref, first_all, first_got.at[0])
    first_far = pltpu.make_async_remote_copy(
        src_ref=first_all, dst_ref=first_all, send_sem=first_sent.at[0], recv_sem=first_got.at[0],
        device_id={"seq": jnp.minimum(my_seq + 1, n_seq - 1)}, device_id_type=MESH,
    )

    @pl.when(tick == 0)
    def _():
        barrier = pltpu.get_barrier_semaphore()
        for p in range(1, n_dp):
            pl.semaphore_signal(barrier, inc=1, device_id={"dp": lax.rem(my_dp + p, n_dp)}, device_id_type=MESH)
        for p in range(1, n_seq):
            pl.semaphore_signal(barrier, inc=1, device_id={"seq": lax.rem(my_seq + p, n_seq)}, device_id_type=MESH)
        pl.semaphore_wait(barrier, n_dp + n_seq - 2)

        @pl.when(my_seq == 0)
        def _():
            first_own.start()

    @pl.when(tick == jnp.minimum(my_seq * max(1, n_ticks // n_seq), n_ticks - 1))
    def _():
        @pl.when(my_seq == 0)
        def _():
            first_own.wait()

        @pl.when(my_seq != 0)
        def _():
            first_far.wait_recv()

        @pl.when(my_seq != n_seq - 1)
        def _():
            first_far.start()

    def gated_copies(s, e, slot):
        at = (my_dp, s, slice(None), pl.ds(pl.multiple_of(e * width, LANES), width))
        own = pltpu.make_async_copy(gated_out.at[slot], gated_all.at[at], own_sem.at[slot, 0])
        if relayed:
            ids = [(my_dp ^ (1 + way), near_got.at[way, s * n_blocks + e], way) for way in range(2)]
        else:
            ids = [(lax.rem(my_dp + p, n_dp), gated_got.at[my_dp], p) for p in range(1, n_dp)]
        far = [
            pltpu.make_async_remote_copy(
                src_ref=gated_out.at[slot], dst_ref=gated_all.at[at],
                send_sem=gated_sent.at[slot, p], recv_sem=got,
                device_id={"dp": peer}, device_id_type=MESH,
            )
            for peer, got, p in ids
        ]
        return own, far

    def passed(s, e, way):
        rows = slice(way * (length // 2), (way + 1) * (length // 2))
        at = (my_dp ^ (1 + way), s, rows, pl.ds(pl.multiple_of(e * width, LANES), width))
        return pltpu.make_async_remote_copy(
            src_ref=gated_all.at[at], dst_ref=gated_all.at[at],
            send_sem=relay_sent.at[way, s * n_blocks + e], recv_sem=relay_got.at[way],
            device_id={"dp": my_dp ^ (2 - way)}, device_id_type=MESH,
        )

    def relay(t):
        s, e = t // n_blocks, lax.rem(t, n_blocks)
        for way in range(2):
            peer = my_dp ^ (1 + way)
            at = (peer, s, slice(None), pl.ds(pl.multiple_of(e * width, LANES), width))
            pltpu.make_async_remote_copy(
                src_ref=gated_out.at[0], dst_ref=gated_all.at[at],
                send_sem=gated_sent.at[0, way], recv_sem=near_got.at[way, t],
                device_id={"dp": peer}, device_id_type=MESH,
            ).wait_recv()
            passed(s, e, way).start()

    def gate_copies(s, e, slot):
        for q in range(owners):
            owner = e * owners + q
            source = gate_out.at[slot, :, q * channels : (q + 1) * channels]
            own = pltpu.make_async_copy(source, gate_all.at[my_seq, s], own_sem.at[slot, 1 + q])
            far = pltpu.make_async_remote_copy(
                src_ref=source, dst_ref=gate_all.at[my_seq, s],
                send_sem=gate_sent.at[slot, q], recv_sem=gate_got.at[my_seq],
                device_id={"seq": owner}, device_id_type=MESH,
            )
            yield owner, own, far

    def send(s, e, slot):
        own, far = gated_copies(s, e, slot)
        own.start()
        for copy in far:
            copy.start()
        for owner, own, far in gate_copies(s, e, slot):
            pl.when(owner == my_seq)(own.start)
            pl.when(owner != my_seq)(far.start)

    def drain(s, e, slot):
        own, far = gated_copies(s, e, slot)
        own.wait()
        for copy in far:
            copy.wait_send()
        for owner, own, far in gate_copies(s, e, slot):
            pl.when(owner == my_seq)(own.wait)
            pl.when(owner != my_seq)(far.wait_send)

    @pl.when(tick >= 2)
    def _():
        drain((tick - 2) // n_blocks, lax.rem(tick - 2, n_blocks), slot)

    history[0:states, :] = start_ref[0]
    drive[0] = d_ref[0] * act_ref[0].astype(F32)
    gate_block = gate_ref[0]
    up[0] = dg_ref[0] * (gate_block * jax.nn.sigmoid(gate_block))
    sum_acc[...] = jnp.zeros_like(sum_acc)

    def rows_of(i):
        return pl.ds(pl.multiple_of(i * CHUNK, CHUNK), CHUNK)

    def kept(i, r):
        return pl.ds(pl.multiple_of((i * CHUNK + r) * states, states), states)

    def sum_y(i, low, part):
        at, rows = slice(part * span, (part + 1) * span), rows_of(i)
        produced = jnp.dot(c_diag[0, i], low[:, at], preferred_element_type=F32)
        scanned = produced + skip_ref[:, at] * act_ref[0, rows, at].astype(F32)
        gate = gate_ref[0, rows, at]
        sigmoid = jax.nn.sigmoid(gate)
        gated = (scanned * (gate * sigmoid)).astype(BF16)
        slope = sigmoid * (1.0 + gate * (1.0 - sigmoid))
        d_gate = (dg_ref[0, rows, at] * scanned * slope).astype(BF16)
        gated_ref[0, rows, at] = gated
        dgate_ref[0, rows, at] = d_gate
        gated_out[slot, rows, at] = gated
        if hosted:
            gate_out[slot, rows, at] = d_gate

    def forward(i, h, low, before, low_before):
        rows = rows_of(i)
        waiting = list(range(parts))
        for r in range(CHUNK):
            b = b_ref[0, i * CHUNK + r]
            for j in range(tiles):
                decay = jnp.exp2(spread_row(d_ref, rows, r, j, states) * rate[j])
                h[j] = h[j] * decay + spread_row(drive, rows, r, j, states) * b
                history[kept(i, r + 1), column(j)] = h[j]
                low[r * states : (r + 1) * states, column(j)] = h[j].astype(BF16)
            if waiting and r % max(1, CHUNK // parts) == 1:
                sum_y(before, low_before, waiting.pop(0))
        for part in waiting:
            sum_y(before, low_before, part)
        return h

    def forward_pair(pair, carry):
        h = forward(2 * pair, list(carry), low_a, jnp.maximum(2 * pair - 1, 0), low_b)
        return tuple(forward(2 * pair + 1, h, low_b, 2 * pair, low_a))

    lax.fori_loop(0, chunks // 2, forward_pair, tuple(start_ref[0, :, column(j)] for j in range(tiles)))
    for part in range(parts):
        sum_y(chunks - 1, low_b, part)
    send(seg, block, slot)
    if relayed:

        @pl.when(tick >= 1)
        def _():
            relay(tick - 1)

    @pl.when(pl.program_id(1) == 0)
    def _():
        db_acc[...] = jnp.zeros_like(db_acc)
        dc_acc[...] = jnp.zeros_like(dc_acc)

    def sum_back(i, low, through, part, count=None):
        at, rows = slice(part * span, (part + 1) * span), rows_of(i)
        d_drive = jnp.dot(b_diag[0, i], low[:, at], preferred_element_type=F32)
        d_rate = jnp.dot(ones_ref[...], through[:, at], preferred_element_type=F32)
        delta, act, d_scanned = d_ref[0, rows, at], act_ref[0, rows, at].astype(F32), up[0, rows, at]
        near = delta * (1.0 - delta * (0.5 - delta * (1.0 / 6.0 - delta * (1.0 / 24.0))))
        slope = jnp.where(delta < 0.03, near, 1.0 - jnp.exp(-delta))
        d_pre = (LN2 * d_rate + d_drive * act) * slope
        dpre_ref[0, rows, at] = d_pre.astype(BF16)
        dact_ref[0, rows, at] = skip_ref[:, at] * d_scanned + d_drive * delta
        if count is None:
            sum_acc[0, :, at] += d_pre
            sum_acc[1, :, at] += d_scanned * act
        else:
            sum_acc[0, :, at] += jnp.where(count, d_pre, 0.0)
            sum_acc[1, :, at] += jnp.where(count, d_scanned * act, 0.0)

    def backward(i, lam, da, low, through, before, low_before, through_before, count=None):
        rows = rows_of(i)
        waiting = list(range(parts))
        for r in reversed(range(CHUNK)):
            c = c_ref[0, i * CHUNK + r]
            db = dc = None
            for j in range(tiles):
                step = spread_row(d_ref, rows, r, j, states)
                upstream = spread_row(up, rows, r, j, states)
                adjoint = lam[j] + upstream * c
                db_j = adjoint * spread_row(drive, rows, r, j, states)
                dc_j = upstream * history[kept(i, r + 1), column(j)]
                db, dc = (db_j, dc_j) if db is None else (db + db_j, dc + dc_j)
                low[r * states : (r + 1) * states, column(j)] = adjoint.astype(BF16)
                lam[j] = adjoint * jnp.exp2(step * rate[j])
                flow = lam[j] * history[kept(i, r), column(j)]
                through[r * states : (r + 1) * states, column(j)] = (flow * rate[j]).astype(BF16)
                da[j] = da[j] + flow * step
            db_acc[i * CHUNK + r] += db
            dc_acc[i * CHUNK + r] += dc
            if waiting and (CHUNK - 1 - r) % max(1, CHUNK // parts) == 1:
                sum_back(before, low_before, through_before, waiting.pop(0), count)
        for part in waiting:
            sum_back(before, low_before, through_before, part, count)
        return lam, da

    def backward_pair(pair, carry):
        lam, da = (list(part) for part in carry)
        i = chunks - 1 - 2 * pair
        lam, da = backward(i, lam, da, low_a, through_a, jnp.minimum(i + 1, chunks - 1), low_b, through_b, pair > 0)
        lam, da = backward(i - 1, lam, da, low_b, through_b, i, low_a, through_a)
        return tuple(lam), tuple(da)

    zeros = tuple(jnp.zeros((states, LANES), F32) for _ in range(tiles))
    _, da = lax.fori_loop(
        0, chunks // 2, backward_pair, (tuple(end_ref[0, :, column(j)] for j in range(tiles)), zeros)
    )
    for part in range(parts):
        sum_back(0, low_b, through_b, part)
    for j in range(tiles):
        da_ref[0, :, column(j)] = da[j]
    sums_ref[0, 0:1, :] = jnp.sum(sum_acc[0], axis=0, keepdims=True)
    sums_ref[0, 1:2, :] = jnp.sum(sum_acc[1], axis=0, keepdims=True)
    sums_ref[0, 2:8, :] = jnp.zeros((6, width), F32)

    @pl.when(pl.program_id(1) == pl.num_programs(1) - 1)
    def _():
        db_ref[0] = jnp.sum(db_acc[...], axis=-1)
        dc_ref[0] = jnp.sum(dc_acc[...], axis=-1)

    @pl.when(tick == pl.num_programs(0) * n_blocks - 1)
    def _():
        drain((tick - 1) // n_blocks, lax.rem(tick - 1, n_blocks), 1 - slot)
        if relayed:
            relay(tick)
        drain(seg, block, slot)
        if relayed:

            def finish_relay(t, nothing):
                for way in range(2):
                    passed(t // n_blocks_static, lax.rem(t, n_blocks_static), way).wait_send()
                return nothing

            lax.fori_loop(0, n_ticks, finish_relay, 0)
            across = my_dp ^ 3
            for way in range(2):
                at = (across, slice(None), slice(way * (length // 2), (way + 1) * (length // 2)))
                pltpu.make_async_remote_copy(
                    src_ref=gated_all.at[at], dst_ref=gated_all.at[at],
                    send_sem=gated_sent.at[0, 0], recv_sem=relay_got.at[way],
                    device_id={"dp": across}, device_id_type=MESH,
                ).wait_recv()
        for p in range(1, 1 if relayed else n_dp):
            source = lax.rem(my_dp + p, n_dp)
            pltpu.make_async_remote_copy(
                src_ref=gated_all.at[source], dst_ref=gated_all.at[source],
                send_sem=gated_sent.at[0, 0], recv_sem=gated_got.at[source],
                device_id={"dp": source}, device_id_type=MESH,
            ).wait_recv()

        @pl.when(my_seq != n_seq - 1)
        def _():
            first_far.wait_send()

        for p in range(1, n_seq if hosted else 1):
            source = lax.rem(my_seq + p, n_seq)
            pltpu.make_async_remote_copy(
                src_ref=gate_all.at[source], dst_ref=gate_all.at[source],
                send_sem=gate_sent.at[0, 0], recv_sem=gate_got.at[source],
                device_id={"seq": source}, device_id_type=MESH,
            ).wait_recv()


def scan_both(delta, act, gate_in, d_gated, b_wide, c_wide, c_diag, b_diag, ones_diag, a_mat, d_skip, start, end, first):
    segs, length, inner = delta.shape
    states = a_mat.shape[0]
    width = widest(inner, 1536)
    tokens = pl.BlockSpec((1, length, width), lambda s, e: (s, 0, e))
    wide = pl.BlockSpec((1, length, states, LANES), lambda s, e: (s, 0, 0, 0))
    diag = pl.BlockSpec((1,) + c_diag.shape[1:], lambda s, e: (s, 0, 0, 0))
    state = pl.BlockSpec((1, states, width), lambda s, e: (s, 0, e))
    narrow = pl.BlockSpec((1, length, states), lambda s, e: (s, 0, 0))
    by_token = jax.ShapeDtypeStruct((segs, length, inner), F32)
    by_token_low = jax.ShapeDtypeStruct((segs, length, inner), BF16)
    by_state = jax.ShapeDtypeStruct((segs, length, states), F32)
    low = pltpu.VMEM((CHUNK * states, width), BF16)
    lanes = pltpu.VMEM((length, states, LANES), F32)
    n_dp, n_seq = lax.axis_size("dp"), lax.axis_size("seq")
    channels = inner // n_seq
    hosted = aligned(inner)
    dma = pltpu.SemaphoreType.DMA
    out = pltpu.VMEM((2, length, width), BF16)
    return pl.pallas_call(
        functools.partial(scan_kernel, hosted, inner // width, segs * (inner // width)),
        grid=(segs, inner // width),
        in_specs=[
            tokens, tokens, tokens, tokens, wide, wide, diag, diag,
            pl.BlockSpec(ones_diag.shape, lambda s, e: (0, 0)),
            pl.BlockSpec((states, width), lambda s, e: (0, e)),
            pl.BlockSpec((1, width), lambda s, e: (0, e)),
            state, state,
            pl.BlockSpec(memory_space=pl.ANY),
        ],
        out_specs=[
            tokens, tokens, tokens, tokens, narrow, narrow, state,
            pl.BlockSpec((1, 8, width), lambda s, e: (s, 0, e)),
            pl.BlockSpec(memory_space=pl.ANY),
            pl.BlockSpec(memory_space=pl.ANY),
            pl.BlockSpec(memory_space=pl.ANY),
        ],
        out_shape=[
            by_token_low, by_token_low, by_token_low, by_token, by_state, by_state,
            jax.ShapeDtypeStruct((segs, states, inner), F32),
            jax.ShapeDtypeStruct((segs, 8, inner), F32),
            jax.ShapeDtypeStruct((n_dp, segs, length, inner), BF16),
            jax.ShapeDtypeStruct((n_seq, segs, length, channels), BF16),
            jax.ShapeDtypeStruct(first.shape, F32),
        ],
        scratch_shapes=[
            pltpu.VMEM(((length + 1) * states, width), F32),
            pltpu.VMEM((1, length, width), F32),
            pltpu.VMEM((1, length, width), F32),
            low, low, low, low, lanes, lanes,
            pltpu.VMEM((2, CHUNK, width), F32),
            out, out,
            dma((2, n_dp)), dma((n_dp,)), dma((2, n_seq)), dma((n_seq,)), dma((2, 1 + n_seq)),
            dma((1,)), dma((1,)),
            dma((2, segs * (inner // width))), dma((2, segs * (inner // width))), dma((2,)),
        ],
        compiler_params=pltpu.CompilerParams(
            collective_id=2, has_side_effects=True, vmem_limit_bytes=VMEM_BYTES
        ),
        cost_estimate=pl.CostEstimate(
            flops=20 * delta.size * states, bytes_accessed=24 * delta.size, transcendentals=2 * delta.size * states
        ),
        name="scan_both",
    )(delta, act, gate_in, d_gated, b_wide, c_wide, c_diag, b_diag, ones_diag, a_mat, d_skip[None], start, end, first)


def finish_kernel(
    conv_hbm, gate_hbm, columns_hbm, normed_hbm, proj_hbm, tokens_hbm, cot_hbm, small_hbm, halo_hbm, gain_ref,
    d_tokens, d_in, small_out, halo_out,
    conv, gate, gate_columns, conv_columns, normed, proj, tokens, cot, small, d_normed,
    partial, arrived, placed, small_dp, small_mid, small_seq,
    load, normed_load, proj_load, swap_sent, swap_got, swap_own, add_sent, add_got, put_sent, put_got, put_own,
    copy_sent, copy_got, mid_sent, mid_got, far_sent, far_got, last_sent, last_got, halo_sent, halo_got,
):
    n_dp, n_seq = lax.axis_size("dp"), lax.axis_size("seq")
    my_dp, my_seq = lax.axis_index("dp"), lax.axis_index("seq")
    half = n_seq // 2
    count, inner = conv_hbm.shape
    width = tokens.shape[1]
    channels = inner // n_seq
    chunks = channels // LANES
    rows_dp = width // n_dp
    rows_small = small_hbm.shape[0] // n_dp
    gain_rows = small_mid.shape[0] - rows_small
    dp_peers = [lax.rem(my_dp + p, n_dp) for p in range(n_dp)]
    seq_peers = [lax.rem(my_seq + p, n_seq) for p in range(n_seq)]

    def remote(src, dst, sent, got, **to):
        return pltpu.make_async_remote_copy(
            src_ref=src, dst_ref=dst, send_sem=sent, recv_sem=got, device_id=to, device_id_type=MESH
        )

    loads = [
        pltpu.make_async_copy(src, dst, load.at[k])
        for k, (src, dst) in enumerate(
            [(columns_hbm, gate_columns), (conv_hbm, conv), (gate_hbm, gate), (tokens_hbm, tokens), (cot_hbm, cot),
             (small_hbm.at[pl.ds(pl.multiple_of(my_dp * rows_small, 16), rows_small)], small)]
        )
    ]
    load_columns, load_conv, load_gate, load_tokens, load_cot, load_small = loads
    load_normed = [pltpu.make_async_copy(normed_hbm.at[s], normed.at[s], normed_load.at[s]) for s in range(n_seq)]
    depth = proj.shape[2]

    def load_proj(k):
        return pltpu.make_async_copy(proj_hbm.at[:, k * depth : (k + 1) * depth], proj.at[k % 2], proj_load.at[k % 2])

    load_columns.start()
    for copy in load_normed:
        copy.start()
    load_conv.start()
    load_proj(0).start()
    for copy in (load_gate, load_tokens, load_cot, load_small):
        copy.start()

    barrier = pltpu.get_barrier_semaphore()
    for p in range(1, n_dp):
        pl.semaphore_signal(barrier, inc=1, device_id={"dp": dp_peers[p]}, device_id_type=MESH)
    for p in range(1, n_seq):
        pl.semaphore_signal(barrier, inc=1, device_id={"seq": seq_peers[p]}, device_id_type=MESH)
    pl.semaphore_wait(barrier, n_dp + n_seq - 2)

    def column_of(device, c):
        return pl.ds(pl.multiple_of(device * channels + c * LANES, LANES), LANES)

    def swap(c, p):
        return remote(
            conv_hbm.at[:, column_of(seq_peers[p], c)], conv_columns.at[c, my_seq],
            swap_sent.at[c, p], swap_got.at[c, my_seq], seq=seq_peers[p],
        )

    own_swaps = [
        pltpu.make_async_copy(conv_hbm.at[:, column_of(my_seq, c)], conv_columns.at[c, my_seq], swap_own.at[c])
        for c in range(chunks)
    ]

    def start_swap(c):
        own_swaps[c].start()
        for p in range(1, n_seq):
            swap(c, p).start()

    start_swap(0)

    def halo(p):
        return remote(halo_hbm, halo_out, halo_sent.at[p], halo_got.at[0], seq=p)

    halo_own = pltpu.make_async_copy(halo_hbm, halo_out, halo_got.at[0])

    @pl.when(my_seq == 0)
    def _():
        halo_own.start()
        for p in range(1, n_seq):
            halo(p).start()

    def small_rows(device):
        return pl.ds(pl.multiple_of(device * rows_small, 16), rows_small)

    def small_add(p):
        return remote(
            small_hbm.at[small_rows(dp_peers[p])], small_dp.at[my_dp], mid_sent.at[p], mid_got.at[my_dp], dp=dp_peers[p]
        )

    for p in range(1, n_dp):
        small_add(p).start()
    def product(c, columns):
        tile = 768 if width % 768 == 0 else 256

        def some_rows(r, nothing):
            at = pl.ds(pl.multiple_of(r * tile, tile), tile)
            total = jnp.dot(normed[0, at, :], columns(0), preferred_element_type=F32)
            for s in range(1, n_seq):
                total += jnp.dot(normed[s, at, :], columns(s), preferred_element_type=F32)
            partial[c, at, :] = total.astype(BF16)
            return nothing

        lax.fori_loop(0, width // tile, some_rows, 0)

    def rows_of(device):
        return pl.ds(pl.multiple_of(device * rows_dp, 16), rows_dp)

    def add(c, p):
        return remote(
            partial.at[c, rows_of(dp_peers[p])], arrived.at[c, my_dp], add_sent.at[c, p], add_got.at[c, my_dp],
            dp=dp_peers[p],
        )

    def scatter(c):
        for p in range(1, n_dp):
            add(c, p).start()

    def place(c):
        k, is_gate = c % chunks, c < chunks
        keeper = my_seq // 2 + (half if is_gate else 0)
        side = lax.rem(my_seq, 2)
        at = (rows_of(my_dp), pl.ds(pl.multiple_of(side * channels + k * LANES, LANES), LANES))
        own = pltpu.make_async_copy(placed.at[c], d_in.at[at], put_own.at[c])
        far = remote(placed.at[c], d_in.at[at], put_sent.at[c], put_got.at[k, side], seq=keeper)
        return keeper, own, far

    def gather_add(c):
        total = partial[c, rows_of(my_dp), :].astype(F32)
        for p in range(1, n_dp):
            remote(
                partial.at[c, rows_of(my_dp)], arrived.at[c, dp_peers[p]], add_sent.at[c, p],
                add_got.at[c, dp_peers[p]], dp=dp_peers[p],
            ).wait_recv()
            total += arrived[c, dp_peers[p]].astype(F32)
        placed[c] = total.astype(BF16)
        keeper, own, far = place(c)
        pl.when(keeper == my_seq)(own.start)
        pl.when(keeper != my_seq)(far.start)

    def spread(k, side, p):
        at = (rows_of(my_dp), slice(side * channels + k * LANES, side * channels + (k + 1) * LANES))
        return remote(
            d_in.at[at], d_in.at[at], copy_sent.at[k, side, p], copy_got.at[k, side, my_dp], dp=dp_peers[p]
        )

    def pass_on(c):
        k, is_gate = c % chunks, c < chunks

        @pl.when((my_seq >= half) == is_gate)
        def _():
            for side in range(2):
                source = 2 * lax.rem(my_seq, half) + side
                at = (rows_of(my_dp), slice(side * channels + k * LANES, side * channels + (k + 1) * LANES))

                @pl.when(source == my_seq)
                def _():
                    place(c)[1].wait()

                @pl.when(source != my_seq)
                def _():
                    remote(placed.at[c], d_in.at[at], put_sent.at[c], put_got.at[k, side], seq=source).wait_recv()

                for p in range(1, n_dp):
                    spread(k, side, p).start()

    load_columns.wait()
    for copy in load_normed:
        copy.wait()
    for c in range(chunks):
        product(c, lambda s, c=c: gate_columns[s, :, c * LANES : (c + 1) * LANES])
        scatter(c)
    if chunks > 1:
        start_swap(1)

    load_conv.wait()
    load_gate.wait()
    steps = 2 * inner // depth
    for k in range(steps):
        if k + 1 < steps:
            load_proj(k + 1).start()
        load_proj(k).wait()
        source, at = (conv, k * depth) if k * depth < inner else (gate, k * depth - inner)

        def some_columns(n, nothing, k=k, source=source, at=at):
            cols = pl.ds(pl.multiple_of(n * 256, 256), 256)
            term = lax.dot_general(
                source[:, at : at + depth], proj[k % 2, cols, :], (((1,), (1,)), ((), ())), preferred_element_type=F32
            )
            d_normed[:, cols] = term if k == 0 else d_normed[:, cols] + term
            return nothing

        lax.fori_loop(0, width // 256, some_columns, 0)
        if k == steps // 2:
            for c in range(chunks):
                gather_add(c)
            for c in range(2, chunks):
                start_swap(c)

    load_tokens.wait()
    load_cot.wait()
    gain = gain_ref[...]

    def some_tokens(r, total):
        at = pl.ds(pl.multiple_of(r * 32, 32), 32)
        token = tokens[at, :].astype(F32)
        inverse = lax.rsqrt(jnp.mean(token * token, axis=-1, keepdims=True) + EPS)
        scaled = d_normed[at, :] * gain
        mean = jnp.mean(scaled * token, axis=-1, keepdims=True)
        d_tokens[at, :] = cot[at, :].astype(F32) + inverse * scaled - token * (inverse * inverse * inverse * mean)
        return total + jnp.sum(d_normed[at, :] * token * inverse, axis=0, keepdims=True)

    d_gain = lax.fori_loop(0, count // 32, some_tokens, jnp.zeros((1, width), F32))
    load_small.wait()
    gains = jnp.concatenate([d_gain[:, r * channels : (r + 1) * channels] for r in range(width // channels)], axis=0)
    gains = jnp.pad(gains, ((0, gain_rows - width // channels), (0, 0)))
    for s in range(n_seq):
        small_mid[rows_small:, s * channels : (s + 1) * channels] = gains.astype(BF16)
    for c in range(chunks):
        pass_on(c)

    total = small[...].astype(F32)
    for p in range(1, n_dp):
        remote(
            small, small_dp.at[dp_peers[p]], mid_sent.at[p], mid_got.at[dp_peers[p]],
            dp=dp_peers[p],
        ).wait_recv()
        total += small_dp[dp_peers[p]].astype(F32)
    small_mid[0:rows_small, :] = total.astype(BF16)

    def small_swap(p):
        at = pl.ds(pl.multiple_of(seq_peers[p] * channels, LANES), channels)
        return remote(
            small_mid.at[:, at], small_seq.at[my_seq], far_sent.at[p], far_got.at[my_seq], seq=seq_peers[p]
        )

    for p in range(1, n_seq):
        small_swap(p).start()

    def convolved(c):
        own_swaps[c].wait()
        for p in range(1, n_seq):
            remote(
                conv_hbm.at[:, column_of(my_seq, c)], conv_columns.at[c, seq_peers[p]], swap_sent.at[c, p],
                swap_got.at[c, seq_peers[p]], seq=seq_peers[p],
            ).wait_recv()
        product(chunks + c, lambda s: conv_columns[c, s])
        scatter(chunks + c)

    convolved(0)
    gather_add(chunks)
    for c in range(1, chunks):
        convolved(c)
        pass_on(chunks + c - 1)
        gather_add(chunks + c)
    total = small_mid[:, pl.ds(pl.multiple_of(my_seq * channels, LANES), channels)].astype(F32)
    for p in range(1, n_seq):
        remote(
            small_mid.at[:, 0:channels], small_seq.at[seq_peers[p]], far_sent.at[p], far_got.at[seq_peers[p]],
            seq=seq_peers[p],
        ).wait_recv()
        total += small_seq[seq_peers[p]].astype(F32)
    small_out[my_dp] = total.astype(BF16)

    def small_spread(p):
        return remote(small_out.at[my_dp], small_out.at[my_dp], last_sent.at[p], last_got.at[my_dp], dp=dp_peers[p])

    for p in range(1, n_dp):
        small_spread(p).start()
    pass_on(2 * chunks - 1)

    for c in range(chunks):
        for p in range(1, n_seq):
            swap(c, p).wait_send()
    for c in range(2 * chunks):
        for p in range(1, n_dp):
            add(c, p).wait_send()
        keeper, own, far = place(c)

        @pl.when(keeper != my_seq)
        def _(far=far):
            far.wait_send()

    for k in range(chunks):
        for side in range(2):
            at = slice(side * channels + k * LANES, side * channels + (k + 1) * LANES)
            for p in range(1, n_dp):
                spread(k, side, p).wait_send()
                peer = dp_peers[p]
                remote(
                    d_in.at[rows_of(peer), at], d_in.at[rows_of(peer), at], copy_sent.at[k, side, p],
                    copy_got.at[k, side, peer], dp=peer,
                ).wait_recv()
    for p in range(1, n_dp):
        small_add(p).wait_send()
        small_spread(p).wait_send()
        peer = dp_peers[p]
        remote(
            small_out.at[peer], small_out.at[peer], last_sent.at[p], last_got.at[peer], dp=peer
        ).wait_recv()
    for p in range(1, n_seq):
        small_swap(p).wait_send()

    @pl.when(my_seq == 0)
    def _():
        halo_own.wait()
        for p in range(1, n_seq):
            halo(p).wait_send()

    @pl.when(my_seq != 0)
    def _():
        halo(1).wait_recv()


def finish(d_conv_in, d_gate, gate_columns, normed_all, in_proj, tokens, cot, small, halo_grad, norm_gain):
    n_dp, n_seq = lax.axis_size("dp"), lax.axis_size("seq")
    count, inner = d_conv_in.shape
    width = tokens.shape[1]
    channels = inner // n_seq
    chunks = channels // LANES
    rows = small.shape[0] // n_dp
    gain_rows = -(-width // channels // 16) * 16
    depth = 1024 if inner % 1024 == 0 else LANES
    dma = pltpu.SemaphoreType.DMA
    vmem = pltpu.VMEM
    anywhere = pl.BlockSpec(memory_space=pl.ANY)
    inside = pl.BlockSpec(memory_space=pltpu.VMEM)
    return pl.pallas_call(
        finish_kernel,
        in_specs=[anywhere] * 9 + [inside],
        out_specs=[inside, anywhere, inside, anywhere],
        out_shape=[
            jax.ShapeDtypeStruct((count, width), F32),
            jax.ShapeDtypeStruct((width, 2 * channels), BF16),
            jax.ShapeDtypeStruct((n_dp, rows + gain_rows, channels), BF16),
            jax.ShapeDtypeStruct(halo_grad.shape, F32),
        ],
        scratch_shapes=[
            vmem((count, inner), BF16), vmem((count, inner), BF16),
            vmem((n_seq, count, channels), BF16), vmem((chunks, n_seq, count, LANES), BF16),
            vmem((n_seq, width, count), BF16), vmem((2, width, depth), BF16),
            vmem((count, width), BF16), vmem((count, width), BF16), vmem((rows, inner), BF16),
            vmem((count, width), F32),
            vmem((2 * chunks, width, LANES), BF16), vmem((2 * chunks, n_dp, width // n_dp, LANES), BF16),
            vmem((2 * chunks, width // n_dp, LANES), BF16),
            vmem((n_dp, rows, inner), BF16), vmem((rows + gain_rows, inner), BF16),
            vmem((n_seq, rows + gain_rows, channels), BF16),
            dma((6,)), dma((n_seq,)), dma((2,)),
            dma((chunks, n_seq)), dma((chunks, n_seq)), dma((chunks,)),
            dma((2 * chunks, n_dp)), dma((2 * chunks, n_dp)),
            dma((2 * chunks,)), dma((chunks, 2)), dma((2 * chunks,)),
            dma((chunks, 2, n_dp)), dma((chunks, 2, n_dp)),
            dma((n_dp,)), dma((n_dp,)), dma((n_seq,)), dma((n_seq,)), dma((n_dp,)), dma((n_dp,)),
            dma((n_seq,)), dma((1,)),
        ],
        compiler_params=pltpu.CompilerParams(
            collective_id=3, has_side_effects=True, vmem_limit_bytes=60 * 2**20
        ),
        cost_estimate=pl.CostEstimate(
            flops=12 * count * width * inner, bytes_accessed=40 * count * width, transcendentals=0
        ),
        name="finish",
    )(
        d_conv_in, d_gate, gate_columns, normed_all, in_proj, tokens, cot, small, halo_grad, norm_gain[None],
    )


def diagonal_blocks(value):
    segs, length, states = value.shape
    spread = jnp.tile(jnp.eye(states, dtype=BF16), (1, CHUNK))
    tiled = matmul(value.reshape(segs * length, states).astype(BF16), spread)
    mask = jnp.repeat(jnp.eye(CHUNK, dtype=F32), states, axis=1)
    return (tiled.reshape(segs, length // CHUNK, CHUNK, CHUNK * states) * mask).astype(BF16)


def conv_back_kernel(
    d_act_ref, coeff_ref, proj_ref, conv_ref, before_ref, weight_ref, bias_ref,
    d_in_ref, last_ref, halo_ref, sums_ref, padded, d_out,
):
    taps = weight_ref.shape[0]
    halo = taps - 1
    length, width = conv_ref.shape[1:]
    padded[8 - halo : 8, :] = before_ref[0].astype(F32)
    padded[8 : 8 + length, :] = conv_ref[0].astype(F32)
    d_out[length : length + 8, :] = jnp.zeros((8, width), F32)
    coeff = coeff_ref[0]
    for j in range(width // LANES):
        at = column(j)
        weight = [weight_ref[tap : tap + 1, at] for tap in range(taps)]
        inputs = [padded[8 - halo + tap : 8 - halo + tap + length, at] for tap in range(taps)]
        conv_out = bias_ref[:, at] + sum(weight[tap] * inputs[tap] for tap in range(taps))
        d_act = d_act_ref[0, :, at] + matmul_nt(coeff, proj_ref[at, :])
        d_conv = d_act * silu_parts(conv_out)[1]
        d_out[0:length, at] = d_conv
        for tap in range(taps):
            sums_ref[0, tap : tap + 1, at] = jnp.sum(d_conv * inputs[tap], axis=0, keepdims=True)
        sums_ref[0, taps : taps + 1, at] = jnp.sum(d_conv, axis=0, keepdims=True)
        d_in = sum(weight[tap] * d_out[halo - tap : halo - tap + length, at] for tap in range(taps))
        d_in_ref[0, :, at] = d_in.astype(BF16)
        last_ref[0, :, at] = d_in[length - 8 :]
        for row in range(halo):
            halo_ref[0, row : row + 1, at] = sum(
                weight[tap] * d_conv[row - tap : row - tap + 1] for tap in range(row + 1)
            )
    sums_ref[0, taps + 1 :, :] = jnp.zeros((8 - taps - 1, width), F32)


def conv_back(d_act, d_coeffs, x_proj, conv_in, before, conv_weight, conv_bias):
    segs, length, inner = conv_in.shape
    width = widest(inner, 1536)
    taps, halo = conv_weight.shape[0], before.shape[1]
    tokens = pl.BlockSpec((1, length, width), lambda s, e: (s, 0, e))

    def rows(count):
        return pl.BlockSpec((1, count, width), lambda s, e: (s, 0, e))

    return pl.pallas_call(
        conv_back_kernel,
        grid=(segs, inner // width),
        in_specs=[
            tokens,
            pl.BlockSpec((1, length, d_coeffs.shape[2]), lambda s, e: (s, 0, 0)),
            pl.BlockSpec((width, x_proj.shape[1]), lambda s, e: (e, 0)),
            tokens,
            rows(halo),
            pl.BlockSpec((taps, width), lambda s, e: (0, e)),
            pl.BlockSpec((1, width), lambda s, e: (0, e)),
        ],
        out_specs=[tokens, rows(8), rows(halo), rows(8)],
        out_shape=[
            jax.ShapeDtypeStruct((segs, length, inner), BF16),
            jax.ShapeDtypeStruct((segs, 8, inner), F32),
            jax.ShapeDtypeStruct((segs, halo, inner), F32),
            jax.ShapeDtypeStruct((segs, 8, inner), F32),
        ],
        scratch_shapes=[pltpu.VMEM((length + 8, width), F32), pltpu.VMEM((length + 8, width), F32)],
        compiler_params=pltpu.CompilerParams(vmem_limit_bytes=VMEM_BYTES),
        cost_estimate=pl.CostEstimate(
            flops=50 * conv_in.size, bytes_accessed=8 * conv_in.size, transcendentals=conv_in.size
        ),
        name="conv_back",
    )(d_act, d_coeffs, x_proj, conv_in, before, conv_weight, conv_bias[None])


def norm_kernel(token_ref, gain_ref, normed_ref, turned_ref):
    token = token_ref[...].astype(F32)
    inverse = lax.rsqrt(jnp.mean(token * token, axis=-1, keepdims=True) + EPS)
    normed = token * inverse * gain_ref[...]
    normed_ref[...] = normed.astype(BF16)
    turned_ref[...] = normed.T.astype(BF16)


def norm(tokens, norm_gain):
    count, width = tokens.shape
    rows = 128
    return pl.pallas_call(
        norm_kernel,
        grid=(count // rows,),
        in_specs=[pl.BlockSpec((rows, width), lambda r: (r, 0)), pl.BlockSpec((1, width), lambda r: (0, 0))],
        out_specs=[pl.BlockSpec((rows, width), lambda r: (r, 0)), pl.BlockSpec((width, rows), lambda r: (0, r))],
        out_shape=[jax.ShapeDtypeStruct((count, width), BF16), jax.ShapeDtypeStruct((width, count), BF16)],
        compiler_params=pltpu.CompilerParams(vmem_limit_bytes=32 * 2**20),
        name="norm",
    )(tokens, norm_gain[None])


def body(
    tokens, conv_state, entry_state, norm_gain, in_proj, conv_weight, conv_bias, x_proj,
    dt_proj, dt_bias, a_log, d_skip, out_proj, cotangent,
):
    segs, length, width = tokens.shape
    inner = in_proj.shape[1] // 2
    rank, states, taps = dt_proj.shape[0], a_log.shape[0], conv_weight.shape[0]
    halo = taps - 1
    count = segs * length
    n_seq = lax.axis_size("seq")
    mine = lax.axis_index("seq")
    is_first = mine == 0

    def flat(value):
        return value.reshape((count,) + value.shape[2:])

    def split(value):
        return value.reshape((segs, length) + value.shape[1:])

    token_float = flat(tokens).astype(F32)
    inverse = lax.rsqrt(jnp.mean(token_float * token_float, axis=-1, keepdims=True) + EPS)
    normed, normed_turned = norm(flat(tokens), norm_gain)
    cot = flat(cotangent)
    fast = aligned(inner)
    if fast:
        normed_all = lax.all_gather(normed_turned, "seq", axis=0, tiled=False)
    else:
        normed_all = lax.all_gather(normed, "seq", axis=0, tiled=True)
    cot_rows = swap_rows(cot.T, "dp")
    conv_in = matmul(normed, in_proj[:, :inner]).astype(BF16)
    gate_in = matmul(normed, in_proj[:, inner:])
    d_gated = matmul_nt(cot, out_proj)
    conv_in = split(conv_in)
    before = jnp.where(is_first, conv_state, shifted(conv_in[:, length - halo :], "seq", 1))
    padded = jnp.concatenate([before, conv_in], axis=1).astype(F32)
    conv_out = conv_bias + sum(conv_weight[tap] * padded[:, tap : tap + length] for tap in range(taps))
    activated = (conv_out * jax.nn.sigmoid(conv_out)).astype(BF16)
    coeffs = matmul(flat(activated), x_proj)
    dt_low = coeffs[:, :rank].astype(BF16)
    b_in = split(coeffs[:, rank : rank + states])
    c_in = split(coeffs[:, rank + states :])
    pre_delta = matmul(dt_low, dt_proj) + dt_bias
    delta = split(jax.nn.softplus(pre_delta))
    a_mat = -jnp.exp(a_log)
    gate_in, d_gated = split(gate_in), split(d_gated)

    b_wide = jnp.broadcast_to(b_in[..., None], b_in.shape + (LANES,))
    c_wide = jnp.broadcast_to(c_in[..., None], c_in.shape + (LANES,))
    ends, entry_mu = block_ends(delta, activated, gate_in, d_gated, b_wide, c_wide, a_mat)
    total = jnp.sum(delta, axis=1, keepdims=True)
    start, end, first = carry(ends, entry_mu, total, entry_state, a_mat)
    ones_diag = diagonal_blocks(jnp.ones((1, CHUNK, states), F32))[0, 0]
    gated, d_gate, d_pre_low, d_act, d_b, d_c, d_amat, sums, gated_all, gate_columns, d_entry = scan_both(
        delta, activated, gate_in, d_gated, b_wide, c_wide,
        diagonal_blocks(c_in), diagonal_blocks(b_in), ones_diag, a_mat, d_skip, start, end, first,
    )
    gated, d_gate, d_pre_low, d_act = flat(gated), flat(d_gate), flat(d_pre_low), flat(d_act)
    gated_all, normed_all = lax.optimization_barrier((gated_all, normed_all))
    gated_all = gated_all.reshape(-1, inner)
    gate_columns = gate_columns.reshape(n_seq * count, -1)
    if (inner // n_seq) % LANES:
        gate_columns = swap_columns(d_gate, "seq")
    output = token_float + matmul(gated, out_proj)
    out_part = matmul(cot_rows, gated_all).astype(BF16)
    out_part = lax.psum_scatter(out_part, "seq", scatter_dimension=1, tiled=True)
    d_out_proj = lax.all_gather(out_part, "dp", axis=0, tiled=True).T.astype(F32)

    sums = jnp.sum(sums, axis=0)
    d_dt_bias, d_d_skip = sums[0], sums[1]
    d_dt_proj = matmul_tn(dt_low, d_pre_low)
    d_dt_low = matmul_nt(d_pre_low, dt_proj)
    d_coeffs = jnp.concatenate([d_dt_low, flat(d_b), flat(d_c)], axis=-1).astype(BF16)
    d_x_proj = matmul_tn(d_coeffs, flat(activated))
    d_a_log = jnp.sum(d_amat, axis=0) * a_mat
    d_conv_in, last, halo_grad, conv_sums = conv_back(
        split(d_act), split(d_coeffs), x_proj, conv_in, before, conv_weight, conv_bias
    )
    conv_sums = jnp.sum(conv_sums, axis=0)
    d_conv_weight, d_conv_bias = conv_sums[:taps], conv_sums[taps]
    returned = shifted(halo_grad, "seq", -1)
    last = last + jnp.pad(returned, ((0, 0), (last.shape[1] - halo, 0), (0, 0)))
    d_conv_in = lax.dynamic_update_slice_in_dim(d_conv_in, last.astype(BF16), length - last.shape[1], 1)
    d_conv_in = flat(d_conv_in)
    if fast:
        small = jnp.concatenate(
            [
                part.astype(BF16)
                for part in (
                    d_x_proj, d_dt_proj, d_a_log, d_dt_bias[None], d_d_skip[None], d_conv_weight, d_conv_bias[None]
                )
            ],
            axis=0,
        )
        edge_at = 2 * rank + 3 * states + 2
        channels = inner // n_seq
        small = jnp.pad(small, ((0, -small.shape[0] % (16 * lax.axis_size("dp"))), (0, 0)))
        rows = small.shape[0] // lax.axis_size("dp")
        d_tokens, d_in_proj, small, d_conv_state = finish(
            d_conv_in, d_gate, gate_columns.reshape(n_seq, count, channels), normed_all, in_proj, flat(tokens), cot,
            small, halo_grad, norm_gain,
        )
        d_in_proj, small = d_in_proj.astype(F32), small.astype(F32)
        gain = jnp.sum(small[:, rows : rows + width // channels], axis=0)
        small = small[:, :rows].reshape(-1, channels)
        edges = small[edge_at:]
        d_norm_gain = lax.dynamic_index_in_dim(gain.reshape(n_seq, -1), mine, 0, keepdims=False)
    else:
        d_conv_state = from_first(halo_grad, "seq")

        n_dp = lax.axis_size("dp")
        small = jnp.concatenate([d_x_proj, d_dt_proj, d_a_log, d_dt_bias[None], d_d_skip[None]], axis=0)
        small = jnp.pad(small, ((0, -small.shape[0] % 16), (0, 0))).astype(BF16)
        small_columns = swap_columns(small, "seq")
        edges = jnp.concatenate([d_conv_weight, d_conv_bias[None]], axis=0)
        edges = jnp.pad(edges, ((0, -edges.shape[0] % 16), (0, 0))).astype(BF16)
        conv_columns = swap_columns(jnp.concatenate([d_conv_in, edges], axis=0), "seq").reshape(n_seq, -1, inner // n_seq)
        edge_columns = conv_columns[:, count:]
        conv_columns = conv_columns[:, :count].reshape(n_seq * count, -1)

        def blocks(value, axis):
            return value.reshape((lax.axis_size(axis), -1) + value.shape[1:])

        gate_part = sum_scatter(blocks(matmul_tn(normed_all, gate_columns), "dp"), "dp").astype(BF16)
        conv_part = sum_scatter(blocks(matmul_tn(normed_all, conv_columns), "dp"), "dp").astype(BF16)
        half = n_seq // 2
        even = mine % 2 == 0
        straight = [(i, i // 2 + (0 if i % 2 == 0 else half)) for i in range(n_seq)]
        crossed = [(i, i // 2 + (half if i % 2 == 0 else 0)) for i in range(n_seq)]
        first = lax.ppermute(jnp.where(even, conv_part, gate_part), "seq", straight)
        second = lax.ppermute(jnp.where(even, gate_part, conv_part), "seq", crossed)
        low_half = mine < half
        d_in_part = jnp.concatenate(
            [jnp.where(low_half, first, second), jnp.where(low_half, second, first)], axis=1
        )
        d_in_proj = gather_rows(d_in_part, "dp").astype(F32)

        d_normed = matmul_nt(d_conv_in, in_proj[:, :inner]) + matmul_nt(d_gate, in_proj[:, inner:])
        d_norm_gain = jnp.sum(d_normed * token_float * inverse, axis=0)
        scaled = d_normed * norm_gain
        cubed = inverse * inverse * inverse
        d_tokens = (
            cot.astype(F32)
            + inverse * scaled
            - token_float * cubed * jnp.mean(scaled * token_float, axis=-1, keepdims=True)
        )
        gain = sum_scatter(blocks(d_norm_gain, "seq"), "seq")
        channels = inner // n_seq
        per_device = jnp.concatenate(
            [
                jnp.sum(small_columns.reshape(n_seq, -1, channels).astype(F32), axis=0),
                jnp.sum(edge_columns.astype(F32), axis=0),
                jnp.pad(gain, (0, -gain.shape[0] % channels)).reshape(-1, channels),
            ],
            axis=0,
        )
        per_device = per_device.astype(BF16)
        summed = jnp.sum(gather_rows(per_device[None], "dp").astype(F32), axis=0)
        edges = summed[small.shape[0] : small.shape[0] + edges.shape[0]]
        d_norm_gain = summed[small.shape[0] + edges.shape[0] :].reshape(-1)[: gain.shape[0]]
        small = summed

    return (
        split(output),
        split(d_tokens),
        d_conv_state,
        d_entry,
        d_norm_gain,
        d_in_proj,
        edges[:taps],
        edges[taps],
        small[: rank + 2 * states].T,
        small[rank + 2 * states : 2 * rank + 2 * states],
        small[2 * rank + 3 * states],
        small[2 * rank + 2 * states : 2 * rank + 3 * states],
        small[2 * rank + 3 * states + 1],
        d_out_proj,
    )


def solution(mesh):
    by_token, by_segment, whole = P("dp", "seq", None), P("dp", None, None), P()
    return jax.shard_map(
        body,
        mesh=mesh,
        in_specs=(by_token, by_segment, by_segment) + (whole,) * 10 + (by_token,),
        out_specs=(
            by_token, by_token, by_segment, by_segment, P("seq"), P(None, "seq"), P(None, "seq"), P("seq"),
            P("seq", None), P(None, "seq"), P("seq"), P(None, "seq"), P("seq"), P("seq", None),
        ),
        check_vma=False,
    )
```
